32 devices in a mesh: dp: 8 (over y, x, core), fsdp: 4 (over z).
Axes of the slice: x: 2, y: 2, z: 4, core: 2. Of those that a mesh axis runs over, the one named last changes fastest.
Arguments:
- inputs: bfloat16 [32, 448, 1024], P(('dp', 'fsdp')), may hold values from -10 to 10
- encoder: bfloat16 [32, 1500, 1024], P(('dp', 'fsdp')), may hold values from -7 to 7
- cotangent: bfloat16 [32, 448, 1024], P(('dp', 'fsdp')), may hold values from -6 to 6
- attention_master: float32 [8, 1024, 1024], P(None, ('dp', 'fsdp')), may hold values from -2 to 2
- expand_master: float32 [1024, 4096], P(('dp', 'fsdp')), may hold values from -0.1875 to 0.1875
- contract_master: float32 [4096, 1024], P(('dp', 'fsdp')), may hold values from -0.09375 to 0.09375
- vectors_master: float32 [17, 1024], P(None, ('dp', 'fsdp')), may hold values from -1.5 to 1.5
- attention_first: bfloat16 [8, 1024, 1024], P(None, ('dp', 'fsdp')), may hold values from -20 to 20
- expand_first: bfloat16 [1024, 4096], P(('dp', 'fsdp')), may hold values from -20 to 20
- contract_first: bfloat16 [4096, 1024], P(('dp', 'fsdp')), may hold values from -20 to 20
- vectors_first: bfloat16 [17, 1024], P(None, ('dp', 'fsdp')), may hold values from -20 to 20
- attention_second: float32 [8, 1024, 1024], P(None, ('dp', 'fsdp')), may hold values from 1.4336 to 143.36
- expand_second: float32 [1024, 4096], P(('dp', 'fsdp')), may hold values from 1.4336 to 143.36
- contract_second: float32 [4096, 1024], P(('dp', 'fsdp')), may hold values from 1.4336 to 143.36
- vectors_second: float32 [17, 1024], P(None, ('dp', 'fsdp')), may hold values from 1.4336 to 143.36
Outputs:
- output: bfloat16 [32, 448, 1024], P(('dp', 'fsdp'))
- grad_input: float32 [32, 448, 1024], P(('dp', 'fsdp'))
- grad_encoder: float32 [32, 1500, 1024], P(('dp', 'fsdp'))
- grad_attention: float32 [8, 1024, 1024], P(None, ('dp', 'fsdp'))
- grad_expand: float32 [1024, 4096], P(('dp', 'fsdp'))
- grad_contract: float32 [4096, 1024], P(('dp', 'fsdp'))
- grad_vectors: float32 [17, 1024], P(None, ('dp', 'fsdp'))
- first_attention: float32 [8, 1024, 1024], P(None, ('dp', 'fsdp'))
- first_expand: float32 [1024, 4096], P(('dp', 'fsdp'))
- first_contract: float32 [4096, 1024], P(('dp', 'fsdp'))
- first_vectors: float32 [17, 1024], P(None, ('dp', 'fsdp'))
- second_attention: float32 [8, 1024, 1024], P(None, ('dp', 'fsdp'))
- second_expand: float32 [1024, 4096], P(('dp', 'fsdp'))
- second_contract: float32 [4096, 1024], P(('dp', 'fsdp'))
- second_vectors: float32 [17, 1024], P(None, ('dp', 'fsdp'))
- master_attention: float32 [8, 1024, 1024], P(None, ('dp', 'fsdp'))
- master_expand: float32 [1024, 4096], P(('dp', 'fsdp'))
- master_contract: float32 [4096, 1024], P(('dp', 'fsdp'))
- master_vectors: float32 [17, 1024], P(None, ('dp', 'fsdp'))
The draws below stay inside these ranges and needn't reach their ends.
All inputs are finite; a program needn't handle non-finite values.
Results may differ from the reference program's by a relative error of at most 0.02.
The reference program's roundings to bfloat16 on the way count: a program that leaves them out, or rounds other values in their place, can miss the bound.
Values may be sent and summed in bfloat16 or wider, within the bound.
No kernel may reach another device: no remote copies, remote signals or barrier semaphores. Data moves between devices by JAX's collectives and lax.ppermute only.
A program may use at most 320 MiB of HBM per device.

```python
import math
import jax
import jax.numpy as jnp
from jax import lax

D = 1024
H = 16
HD = 64
FF = 4096
L = 448
FRAMES = 1500
ADAM_STEP = 4
NV = 17
SEQS = 32
TOKENS = 14336


def draw_inputs(key, part):
    key_base = jax.random.fold_in(key, 11)
    key_common = jax.random.fold_in(key, 12)
    base = jnp.clip(jax.random.normal(key_base, (SEQS, L, D), jnp.float32), -5.0, 5.0)
    common = jnp.clip(jax.random.normal(key_common, (SEQS, 1, D), jnp.float32), -4.0, 4.0)
    ramp = 0.2 + 0.8 * jnp.arange(SEQS, dtype=jnp.float32) / max(SEQS - 1, 1)
    return (base + ramp[:, None, None] * common).astype(jnp.bfloat16)


def draw_encoder(key, part):
    key_base = jax.random.fold_in(key, 21)
    base = jnp.clip(jax.random.normal(key_base, (SEQS, FRAMES, D), jnp.float32), -5.0, 5.0)
    top, bottom = (1.35, 0.45)
    falling = 1.0 - jnp.arange(SEQS, dtype=jnp.float32) / max(SEQS - 1, 1)
    ramp = bottom + (top - bottom) * falling
    return (base * ramp[:, None, None]).astype(jnp.bfloat16)


def draw_attention_master(key, part):
    key_base = jax.random.fold_in(key, 31)
    key_heads = jax.random.fold_in(key, 32)
    base = jnp.clip(jax.random.normal(key_base, (8, D, D), jnp.float32), -5.0, 5.0)
    head_scale = jnp.exp(jax.random.uniform(key_heads, (8, H), jnp.float32, 0.0, math.log(1.4)))
    matrix_index = jnp.arange(8)[:, None]
    factor = jnp.where(matrix_index % 4 < 2, head_scale, jnp.where(matrix_index == 3, 4.0, jnp.where(matrix_index == 7, 6.0, 1.0)))
    columns = jnp.repeat(factor, HD, axis=1)[:, None, :]
    return base * columns * (1.0 / math.sqrt(D))


def draw_vectors_master(key, part):
    key_base = jax.random.fold_in(key, 41)
    base = jnp.clip(jax.random.normal(key_base, (NV, D), jnp.float32), -4.0, 4.0)
    row_index = jnp.arange(NV)[:, None]
    is_gain = (row_index == 0) | (row_index == 2) | (row_index == 4)
    return jnp.where(is_gain, 1.0 + 0.1 * base, 0.3 * base)


def block_scale(own_key, shape, pieces, smallest, high):
    level = 1.0
    for position, blocks in pieces:
        draws = jax.random.uniform(jax.random.fold_in(jax.random.fold_in(own_key, 6), position), (blocks,), jnp.float32, smallest / len(pieces), high / len(pieces))
        level = level * jnp.repeat(jnp.exp(draws), shape[position] // blocks).reshape((-1,) + (1,) * (len(shape) - 1 - position))
    return level


def bell_draw(stream_key, extent, width, most, shards=(), kind=jnp.bfloat16):
    loudness = block_scale(stream_key, extent, shards, -0.22, 0.18) if shards else 1.0
    drawn = jax.random.normal(stream_key, extent, jnp.float32) * width * loudness
    return jnp.minimum(jnp.maximum(drawn, -most), most).astype(kind)


def setup_inputs(seed: int = 0) -> dict:
    splits = jax.random.split(jax.random.key(seed), 16)
    inputs = draw_inputs(jax.random.fold_in(splits[15], 71), 0)
    encoder = draw_encoder(jax.random.fold_in(splits[15], 71), 0)
    cotangent = bell_draw(splits[2], (SEQS, L, D), 1.0, 6.0, ((0, 32),))
    attention_master = draw_attention_master(jax.random.fold_in(splits[15], 71), 0)
    expand_master = bell_draw(splits[4], (D, FF), D ** -0.5, 0.1875, ((0, 32),), jnp.float32)
    contract_master = bell_draw(splits[5], (FF, D), FF ** -0.5, 0.09375, ((0, 32),), jnp.float32)
    vectors_master = draw_vectors_master(jax.random.fold_in(splits[15], 71), 0)
    attention_first = bell_draw(splits[7], (8, D, D), (0.03 * TOKENS ** 0.5), 20.0, ((1, 32),))
    expand_first = bell_draw(splits[8], (D, FF), (0.03 * TOKENS ** 0.5), 20.0, ((0, 32),))
    contract_first = bell_draw(splits[9], (FF, D), (0.03 * TOKENS ** 0.5), 20.0, ((0, 32),))
    vectors_first = bell_draw(splits[10], (NV, D), (0.03 * TOKENS ** 0.5), 20.0, ((1, 32),))
    attention_second = jnp.clip(jnp.exp(math.log(143.36) - 4.6051702 * jax.random.uniform(splits[11], (8, D, D), jnp.float32) ** block_scale(splits[11], (8, D, D), ((1, 32),), -0.2, 0.2)), 1.4336, 143.36)
    expand_second = jnp.clip(jnp.exp(math.log(143.36) - 4.6051702 * jax.random.uniform(splits[12], (D, FF), jnp.float32) ** block_scale(splits[12], (D, FF), ((0, 32),), -0.2, 0.2)), 1.4336, 143.36)
    contract_second = jnp.clip(jnp.exp(math.log(143.36) - 4.6051702 * jax.random.uniform(splits[13], (FF, D), jnp.float32) ** block_scale(splits[13], (FF, D), ((0, 32),), -0.2, 0.2)), 1.4336, 143.36)
    vectors_second = jnp.clip(jnp.exp(math.log(143.36) - 4.6051702 * jax.random.uniform(splits[14], (NV, D), jnp.float32) ** block_scale(splits[14], (NV, D), ((1, 32),), -0.2, 0.2)), 1.4336, 143.36)
    return {"inputs": inputs, "encoder": encoder, "cotangent": cotangent, "attention_master": attention_master, "expand_master": expand_master, "contract_master": contract_master, "vectors_master": vectors_master, "attention_first": attention_first, "expand_first": expand_first, "contract_first": contract_first, "vectors_first": vectors_first, "attention_second": attention_second, "expand_second": expand_second, "contract_second": contract_second, "vectors_second": vectors_second}


highest = lax.Precision.HIGHEST
eps_norm = 1e-05
clip_limit = 1.0
learn_rate = 0.05
beta_first = 0.9
beta_second = 0.999
eps_adam = 1e-08
weight_decay = 0.1

@jax.custom_vjp
def low(v):
    return lax.optimization_barrier(v.astype(jnp.bfloat16)).astype(jnp.float32)

@jax.custom_vjp
def low_back(v):
    return v

def low_keep(v):
    return (low(v), None)

def low_pass(kept, grad):
    return (grad,)

def back_keep(v):
    return (v, None)

def back_low(kept, grad):
    return (low(grad),)
low.defvjp(low_keep, low_pass)
low_back.defvjp(back_keep, back_low)

def matmul(left, right):
    return jnp.dot(left, right, precision=highest)

def layer_norm(values, gain, shift):
    centered = values - lax.optimization_barrier(jnp.mean(values, axis=-1, keepdims=True))
    spread = lax.optimization_barrier(jnp.mean(centered * centered, axis=-1, keepdims=True))
    return centered * lax.rsqrt(spread + eps_norm) * gain + shift

def attend(query_in, key_in, value_in, causal):
    query_h = query_in.reshape(query_in.shape[0], H, HD)
    key_h = key_in.reshape(key_in.shape[0], H, HD)
    value_h = value_in.reshape(value_in.shape[0], H, HD)
    scores = low_back(jnp.einsum('qhd,khd->hqk', query_h, key_h, precision=highest) * HD ** (-0.5))
    if causal:
        allowed = jnp.arange(key_in.shape[0])[None, :] <= jnp.arange(query_in.shape[0])[:, None]
        scores = jnp.where(allowed[None], scores, -1e+30)
    row_max = lax.optimization_barrier(jnp.max(scores, axis=-1, keepdims=True))
    exp_scores = jnp.exp(scores - row_max)
    attn_probs = exp_scores / lax.optimization_barrier(jnp.sum(exp_scores, axis=-1, keepdims=True))
    mixed_out = jnp.einsum('hqk,khd->qhd', low(attn_probs), value_h, precision=highest)
    mixed_out = mixed_out.reshape(query_in.shape[0], H * HD)
    return (low(low_back(mixed_out)), lax.optimization_barrier(jnp.max(row_max[:, :, 0], axis=1)))

def forward(params, hidden_in, enc_rows):
    w_attention, w_expand, w_contract, vectors = params
    norm_one = low(layer_norm(hidden_in, vectors[0], vectors[1]))
    q_self = low(low_back(matmul(norm_one, w_attention[0]) + vectors[6]))
    k_self = low(low_back(matmul(norm_one, w_attention[1])))
    v_self = low(low_back(matmul(norm_one, w_attention[2]) + vectors[7]))
    mixed_self, max_self = attend(q_self, k_self, v_self, True)
    resid_one = hidden_in + low_back(matmul(mixed_self, w_attention[3]) + vectors[8])
    norm_two = low(layer_norm(resid_one, vectors[2], vectors[3]))
    q_cross = low(low_back(matmul(norm_two, w_attention[4]) + vectors[9]))
    k_cross = low(low_back(matmul(enc_rows, w_attention[5])))
    v_cross = low(low_back(matmul(enc_rows, w_attention[6]) + vectors[10]))
    mixed_cross, max_cross = attend(q_cross, k_cross, v_cross, False)
    resid_two = resid_one + low_back(matmul(mixed_cross, w_attention[7]) + vectors[11])
    norm_three = low(layer_norm(resid_two, vectors[4], vectors[5]))
    pre_gelu = low_back(matmul(norm_three, w_expand) + vectors[13:].reshape(-1))
    hidden_act = low(jax.nn.gelu(pre_gelu, approximate=False))
    result = resid_two + low_back(matmul(hidden_act, w_contract) + vectors[12])
    return (result, jnp.stack([max_self, max_cross]))

def adam_update(master, gradient, first, second, step_value, clip_scale):
    first_new = beta_first * first.astype(jnp.float32) + (1.0 - beta_first) * gradient
    second_new = beta_second * second + (1.0 - beta_second) * gradient * gradient
    direction = first_new / (1.0 - beta_first ** step_value) / (jnp.sqrt(second_new / (1.0 - beta_second ** step_value)) + eps_adam)
    master_new = (master - learn_rate * (direction + weight_decay * master)) * clip_scale
    return (first_new, second_new, master_new)

def reference(inputs, encoder, cotangent, attention_master, expand_master, contract_master, vectors_master, attention_first, expand_first, contract_first, vectors_first, attention_second, expand_second, contract_second, vectors_second):
    params = (low(attention_master), low(expand_master), low(contract_master), low(vectors_master))
    inputs_wide = inputs.astype(jnp.float32)
    encoder_wide = encoder.astype(jnp.float32)

    def whole(params_in, inputs_in, encoder_in):

        def one_seq(running_max, seq_pair):
            out_seq, max_seq = jax.checkpoint(forward)(params_in, seq_pair[0], seq_pair[1])
            return (jnp.maximum(running_max, max_seq), out_seq)
        start_max = jnp.full((2, H), -1e+30, jnp.float32)
        maxima_all, outputs_all = lax.scan(one_seq, start_max, (inputs_in, encoder_in))
        return (outputs_all, maxima_all)
    outputs_all, pullback, maxima = jax.vjp(whole, params, inputs_wide, encoder_wide, has_aux=True)
    grad_params, grad_input, grad_encoder = pullback(cotangent.astype(jnp.float32))
    clip_cols = jnp.repeat(jnp.sqrt(clip_limit / jnp.maximum(maxima, clip_limit)), HD, axis=1)
    unit_row = jnp.ones_like(clip_cols[0])
    clip_attention = jnp.stack([clip_cols[0], clip_cols[0], unit_row, unit_row, clip_cols[1], clip_cols[1], unit_row, unit_row])[:, None, :]
    clip_vectors = jnp.ones_like(vectors_master).at[6].set(clip_cols[0]).at[9].set(clip_cols[1])
    step_value = float(ADAM_STEP)
    masters = (attention_master, expand_master, contract_master, vectors_master)
    firsts = (attention_first, expand_first, contract_first, vectors_first)
    seconds = (attention_second, expand_second, contract_second, vectors_second)
    clips = (clip_attention, jnp.ones_like(expand_master[:1]), jnp.ones_like(contract_master[:1]), clip_vectors)
    updates = [adam_update(masters[index], grad_params[index], firsts[index], seconds[index], step_value, clips[index]) for index in range(4)]
    return (outputs_all.astype(jnp.bfloat16), grad_input, grad_encoder, grad_params[0], grad_params[1], grad_params[2], grad_params[3], updates[0][0], updates[1][0], updates[2][0], updates[3][0], updates[0][1], updates[1][1], updates[2][1], updates[3][1], updates[0][2], updates[1][2], updates[2][2], updates[3][2])
```

```python
import functools
import math

import jax
import jax.numpy as jnp
from jax import lax
from jax.experimental import pallas as pl
from jax.experimental.pallas import tpu as pltpu
from jax.sharding import Mesh
from jax.sharding import PartitionSpec as P

HD = 64
ADAM_STEP = 4

eps_norm = 1e-05
clip_limit = 1.0
learn_rate = 0.05
beta_first = 0.9
beta_second = 0.999
eps_adam = 1e-08
weight_decay = 0.1

BF = jnp.bfloat16
F32 = jnp.float32
ALL = ("y", "x", "c", "z")
TILE = 256
KEY_CHUNK = 256
VEC_ROWS = 17
MIB = 1024 * 1024


def dot(left, right):
    return jnp.dot(left, right, preferred_element_type=F32)


def dot_tn(left, right):
    return lax.dot_general(left, right, (((0,), (0,)), ((), ())), preferred_element_type=F32)


def dot_nt(left, right):
    return lax.dot_general(left, right, (((1,), (1,)), ((), ())), preferred_element_type=F32)


def params(limit=48):
    return pltpu.CompilerParams(vmem_limit_bytes=limit * MIB)


def vmem():
    return pl.BlockSpec(memory_space=pltpu.VMEM)


def hbm():
    return pl.BlockSpec(memory_space=pl.ANY)


def smem():
    return pl.BlockSpec(memory_space=pltpu.SMEM)


def shape(dims, dtype):
    return jax.ShapeDtypeStruct(tuple(dims), dtype)


def cost(flops, nbytes):
    return pl.CostEstimate(flops=int(flops), bytes_accessed=int(nbytes), transcendentals=0)


def weight_copy(pack, row, buf, sem):
    return pltpu.make_async_copy(pack.at[:, pl.ds(row, buf.shape[1]), :], buf, sem)


def times(act_ref, buf, put):
    depth = buf.shape[0] * buf.shape[1]

    @pl.loop(0, buf.shape[2] // TILE)
    def _(n):
        start = pl.multiple_of(n * TILE, TILE)
        put(start, dot(act_ref[...], buf[:, :, pl.ds(start, TILE)].reshape(depth, TILE)))


def times_t(act_ref, buf, put):
    per = TILE // buf.shape[1]

    @pl.loop(0, buf.shape[0] // per)
    def _(n):
        start = pl.multiple_of(n * TILE, TILE)
        rows = buf[pl.ds(n * per, per)].reshape(TILE, buf.shape[2])
        put(start, dot_nt(act_ref[...], rows))


def grad_weight(act_ref, grad_ref, out):
    @pl.loop(0, 4)
    def _(n):
        start = pl.multiple_of(n * TILE, TILE)
        tile = dot_tn(act_ref[:, pl.ds(start, TILE)], grad_ref[...])
        out[pl.ds(2 * n, 2)] = tile.astype(BF).reshape((2,) + out.shape[1:])


def block_copies(sel, grad, keep, send, row, sems):
    out = []
    for j in range(8):
        across, plane = j // 4, j % 4
        block = jnp.bitwise_xor(sel, plane * 2 + across)
        target = (send if across else keep).at[plane, :, pl.ds(row, grad.shape[2]), :]
        out.append(pltpu.make_async_copy(grad.at[block], target, sems.at[j]))
    return out


def start_all(copies):
    for one in copies:
        one.start()


def wait_all(copies):
    for one in copies:
        one.wait()


def row_chunks(count, size=64):
    return [slice(a, min(a + size, count)) for a in range(0, count, size)]


def normalise(values):
    centered = values - jnp.mean(values, axis=-1, keepdims=True)
    inv = lax.rsqrt(jnp.mean(centered * centered, axis=-1, keepdims=True) + eps_norm)
    return centered * inv, inv


def norm_into(src, gain, shift, out_ref):
    for rows in row_chunks(src.shape[0]):
        normed, _ = normalise(src[rows, :].astype(F32))
        out_ref[rows, :] = (normed * gain + shift).astype(BF)


def norm_grad(src, grad_ref, gain, put):
    gain_sum = jnp.zeros((1, src.shape[1]), F32)
    shift_sum = jnp.zeros((1, src.shape[1]), F32)
    for rows in row_chunks(src.shape[0]):
        normed, inv = normalise(src[rows, :].astype(F32))
        grad = grad_ref[rows, :]
        gain_sum += jnp.sum(grad * normed, axis=0, keepdims=True)
        shift_sum += jnp.sum(grad, axis=0, keepdims=True)
        scaled = grad * gain
        mean_one = jnp.mean(scaled, axis=-1, keepdims=True)
        mean_two = jnp.mean(scaled * normed, axis=-1, keepdims=True)
        put(rows, inv * (scaled - mean_one - normed * mean_two))
    return gain_sum, shift_sum


def column_sum(ref):
    total = jnp.zeros((1, ref.shape[1]), F32)
    for rows in row_chunks(ref.shape[0], 128):
        total += jnp.sum(ref[rows, :].astype(F32), axis=0, keepdims=True)
    return total


def self_in_kernel(x_ref, vec_ref, pack, a_ref, q_ref, k_ref, v_ref, bufs, sems):
    copies = [weight_copy(pack, 32 * n, bufs.at[n], sems.at[n]) for n in range(3)]
    start_all(copies)
    norm_into(x_ref, vec_ref[0:1, :], vec_ref[1:2, :], a_ref)
    for n, (out, bias) in enumerate(((q_ref, 6), (k_ref, None), (v_ref, 7))):
        copies[n].wait()

        def put(start, value, out=out, bias=bias):
            if bias is not None:
                value = value + vec_ref[bias : bias + 1, pl.ds(start, TILE)]
            out[:, pl.ds(start, TILE)] = value.astype(BF)

        times(a_ref, bufs.at[n], put)


def self_in(x, vec, pack):
    rows, width = x.shape
    full = shape((rows, width), BF)
    return pl.pallas_call(
        self_in_kernel,
        out_shape=[full] * 4,
        in_specs=[vmem(), vmem(), hbm()],
        out_specs=[vmem()] * 4,
        scratch_shapes=[pltpu.VMEM((3, 32, 32, width), BF), pltpu.SemaphoreType.DMA((3,))],
        compiler_params=params(),
        cost_estimate=cost(6 * rows * width * width, 10 * MIB),
        name="self_in",
    )(x, vec, pack)


def masked_pair(value):
    lane = lax.broadcasted_iota(jnp.int32, value.shape, 1)
    zero = jnp.zeros_like(value)
    return jnp.concatenate([jnp.where(lane < HD, value, zero), jnp.where(lane < HD, zero, value)], axis=0)


def pair_back(both, rows):
    line = lax.broadcasted_iota(jnp.int32, (2 * HD, rows), 0)
    return jnp.where(line < HD, both[:, :rows], both[:, rows:]).T


def key_chunks(count):
    return [(a, min(a + KEY_CHUNK, count)) for a in range(0, count, KEY_CHUNK)]


def exclude(scores, start, rows, causal, valid):
    key = lax.broadcasted_iota(jnp.int32, scores.shape, 0) + start
    if causal:
        query = lax.broadcasted_iota(jnp.int32, scores.shape, 1)
        query = jnp.where(query >= rows, query - rows, query)
        return jnp.where(key <= query, scores, -1e30)
    if start + scores.shape[0] > valid:
        return jnp.where(key < valid, scores, -1e30)
    return scores


def attend_kernel(causal, valid, q_ref, k_ref, v_ref, o_ref, lse_ref, top_ref, held):
    rows = q_ref.shape[0]
    query = masked_pair(q_ref[...] * jnp.asarray(HD**-0.5, BF))
    top = jnp.full((1, 2 * rows), -1e30, F32)
    for a, b in key_chunks(k_ref.shape[0]):
        scores = exclude(dot_nt(k_ref[a:b, :], query), a, rows, causal, valid)
        held[a:b, :] = scores
        top = jnp.maximum(top, jnp.max(scores, axis=0, keepdims=True))
    total = jnp.zeros((1, 2 * rows), F32)
    mixed = jnp.zeros((2 * HD, 2 * rows), F32)
    for a, b in key_chunks(k_ref.shape[0]):
        probs = jnp.exp(held[a:b, :] - top)
        total += jnp.sum(probs, axis=0, keepdims=True)
        mixed += dot_tn(v_ref[a:b, :], probs.astype(BF))
    o_ref[...] = pair_back(mixed * (1.0 / total), rows).astype(BF)
    top_ref[0] = top
    lse_ref[0] = top + jnp.log(total)


def attend(query, key, value, causal, valid):
    rows, width = query.shape
    keys = key.shape[0]
    pairs = width // (2 * HD)

    def column(count):
        return pl.BlockSpec((count, 2 * HD), lambda h: (0, h))

    line = pl.BlockSpec((1, 1, 2 * rows), lambda h: (h, 0, 0))
    return pl.pallas_call(
        functools.partial(attend_kernel, causal, valid),
        grid=(pairs,),
        out_shape=[shape((rows, width), BF)] + [shape((pairs, 1, 2 * rows), F32)] * 2,
        in_specs=[column(rows), column(keys), column(keys)],
        out_specs=[column(rows), line, line],
        scratch_shapes=[pltpu.VMEM((keys, 2 * rows), F32)],
        compiler_params=params(),
        cost_estimate=cost(16 * rows * keys * width, 4 * keys * width),
        name="attend_causal" if causal else "attend",
    )(query, key, value)


def self_out_kernel(o_ref, x_ref, vec_ref, pack, x1_ref, a_ref, q_ref, bufs, sems):
    copies = [weight_copy(pack, 32 * (3 + n), bufs.at[n], sems.at[n]) for n in range(2)]
    start_all(copies)
    copies[0].wait()

    def put_residual(start, value):
        cols = pl.ds(start, TILE)
        x1_ref[:, cols] = x_ref[:, cols].astype(F32) + (value + vec_ref[8:9, cols])

    times(o_ref, bufs.at[0], put_residual)
    norm_into(x1_ref, vec_ref[2:3, :], vec_ref[3:4, :], a_ref)
    copies[1].wait()

    def put_query(start, value):
        cols = pl.ds(start, TILE)
        q_ref[:, cols] = (value + vec_ref[9:10, cols]).astype(BF)

    times(a_ref, bufs.at[1], put_query)


def self_out(mixed, x, vec, pack):
    rows, width = x.shape
    return pl.pallas_call(
        self_out_kernel,
        out_shape=[shape((rows, width), F32), shape((rows, width), BF), shape((rows, width), BF)],
        in_specs=[vmem()] * 3 + [hbm()],
        out_specs=[vmem()] * 3,
        scratch_shapes=[pltpu.VMEM((2, 32, 32, width), BF), pltpu.SemaphoreType.DMA((2,))],
        compiler_params=params(),
        cost_estimate=cost(4 * rows * width * width, 10 * MIB),
        name="self_out",
    )(mixed, x, vec, pack)


def cross_in_kernel(e_ref, vec_ref, pack, k_ref, v_ref, bufs, sems):
    copies = [weight_copy(pack, 32 * (5 + n), bufs.at[n], sems.at[n]) for n in range(2)]
    start_all(copies)
    for n, (out, bias) in enumerate(((k_ref, None), (v_ref, 10))):
        copies[n].wait()

        def put(start, value, out=out, bias=bias):
            if bias is not None:
                value = value + vec_ref[bias : bias + 1, pl.ds(start, TILE)]
            out[:, pl.ds(start, TILE)] = value.astype(BF)

        times(e_ref, bufs.at[n], put)


def cross_in(enc, vec, pack):
    frames, width = enc.shape
    return pl.pallas_call(
        cross_in_kernel,
        out_shape=[shape((frames, width), BF)] * 2,
        in_specs=[vmem()] * 2 + [hbm()],
        out_specs=[vmem()] * 2,
        scratch_shapes=[pltpu.VMEM((2, 32, 32, width), BF), pltpu.SemaphoreType.DMA((2,))],
        compiler_params=params(),
        cost_estimate=cost(4 * frames * width * width, 14 * MIB),
        name="cross_in",
    )(enc, vec, pack)


def cross_out_kernel(o_ref, x1_ref, vec_ref, pack, x2_ref, a_ref, buf, sem):
    copy = weight_copy(pack, 32 * 7, buf, sem)
    copy.start()
    copy.wait()

    def put(start, value):
        cols = pl.ds(start, TILE)
        x2_ref[:, cols] = x1_ref[:, cols] + (value + vec_ref[11:12, cols])

    times(o_ref, buf, put)
    norm_into(x2_ref, vec_ref[4:5, :], vec_ref[5:6, :], a_ref)


def cross_out(mixed, x1, vec, pack):
    rows, width = x1.shape
    return pl.pallas_call(
        cross_out_kernel,
        out_shape=[shape((rows, width), F32), shape((rows, width), BF)],
        in_specs=[vmem()] * 3 + [hbm()],
        out_specs=[vmem()] * 2,
        scratch_shapes=[pltpu.VMEM((32, 32, width), BF), pltpu.SemaphoreType.DMA],
        compiler_params=params(),
        cost_estimate=cost(2 * rows * width * width, 8 * MIB),
        name="cross_out",
    )(mixed, x1, vec, pack)


def feed_kernel(
    sel_ref, a_ref, x2_ref, e_ref, vec_ref, bias_ref, w1_ref, w2_ref,
    out_ref, da_ref, gb1_ref, gb2_ref, keep1, send1, keep2, send2,
    total, g1, g2, sems1, sems2,
):
    step = pl.program_id(0)
    steps = pl.num_programs(0)
    sel = sel_ref[0]
    slot = lax.rem(step, 2)
    wide = w1_ref.shape[2]
    depth = a_ref.shape[1]

    def copies_one(at_step, at_slot):
        cols = pl.ds(pl.multiple_of(at_step * wide, wide), wide)
        return block_copies(sel, g1.at[at_slot], keep1.at[:, :, :, cols], send1.at[:, :, :, cols], 0, sems1.at[at_slot])

    def copy_two(at_step, at_slot, ref):
        place = jnp.bitwise_xor(sel, at_step)
        return pltpu.make_async_copy(g2.at[at_slot], ref.at[lax.div(place, 2)], sems2.at[at_slot])

    @pl.when(step >= 2)
    def _():
        wait_all(copies_one(step - 2, slot))
        copy_two(step - 2, slot, keep2).wait()

    w1 = w1_ref[...].reshape(depth, wide)
    w2 = w2_ref[...].reshape(wide, depth)
    pre = dot(a_ref[...], w1) + bias_ref[0]
    cdf = 0.5 * (1.0 + lax.erf(pre * math.sqrt(0.5)))
    act = (pre * cdf).astype(BF)
    slope = cdf + pre * (jnp.exp(-0.5 * (pre * pre)) * (1.0 / math.sqrt(2.0 * math.pi)))
    grad_pre = (dot_nt(e_ref[...], w2) * slope).astype(BF)
    gb1_ref[0] = jnp.sum(grad_pre.astype(F32), axis=0, keepdims=True)
    g2[slot] = dot_tn(act, e_ref[...]).astype(BF).reshape(g2.shape[1:])

    place = jnp.bitwise_xor(sel, step)

    @pl.when(lax.rem(place, 2) == 0)
    def _():
        copy_two(step, slot, keep2).start()

    @pl.when(lax.rem(place, 2) == 1)
    def _():
        copy_two(step, slot, send2).start()

    g1[slot] = dot_tn(a_ref[...], grad_pre).astype(BF).reshape(g1.shape[1:])
    start_all(copies_one(step, slot))

    @pl.when(step == 0)
    def _():
        total[...] = x2_ref[...] + vec_ref[12:13, :]
        da_ref[...] = jnp.zeros_like(da_ref)
        gb2_ref[...] = column_sum(e_ref)

    total[...] += dot(act, w2)
    da_ref[...] += dot_nt(grad_pre, w1)

    @pl.when(step == steps - 1)
    def _():
        out_ref[...] = total[...].astype(BF)
        wait_all(copies_one(step - 1, 1 - slot))
        copy_two(step - 1, 1 - slot, keep2).wait()
        wait_all(copies_one(step, slot))
        copy_two(step, slot, keep2).wait()


def feed(sel, a3, x2, cot, vec, pack):
    rows, width = a3.shape
    hidden = 4 * width
    wide = hidden // 8
    bias = vec[13:].reshape(8, 1, wide)

    def whole(dims):
        return pl.BlockSpec(dims, lambda n: (0,) * len(dims))

    return pl.pallas_call(
        feed_kernel,
        grid=(8,),
        out_shape=[
            shape((rows, width), BF),
            shape((rows, width), F32),
            shape((8, 1, wide), F32),
            shape((1, width), F32),
            shape((4, 4, 32, hidden), BF),
            shape((4, 4, 32, hidden), BF),
            shape((4, 4, 128, width), BF),
            shape((4, 4, 128, width), BF),
        ],
        in_specs=[
            smem(),
            whole((rows, width)),
            whole((rows, width)),
            whole((rows, width)),
            whole(vec.shape),
            pl.BlockSpec((1, 1, wide), lambda n: (n, 0, 0)),
            pl.BlockSpec((32, 32, wide), lambda n: (0, n // 2, n % 2)),
            pl.BlockSpec((4, 128, width), lambda n: (n, 1, 0)),
        ],
        out_specs=[
            whole((rows, width)),
            whole((rows, width)),
            pl.BlockSpec((1, 1, wide), lambda n: (n, 0, 0)),
            whole((1, width)),
            hbm(), hbm(), hbm(), hbm(),
        ],
        scratch_shapes=[
            pltpu.VMEM((rows, width), F32),
            pltpu.VMEM((2, 8, 4, 32, wide), BF),
            pltpu.VMEM((2, 4, 128, width), BF),
            pltpu.SemaphoreType.DMA((2, 8)),
            pltpu.SemaphoreType.DMA((2,)),
        ],
        compiler_params=params(),
        cost_estimate=cost(12 * rows * width * hidden, 40 * MIB),
        name="feed",
    )(sel, a3, x2, cot, vec, bias, pack, pack)


def cross_out_grad_kernel(
    sel_ref, da_ref, x2_ref, cot_ref, o_ref, vec_ref, pack,
    dx_ref, do_ref, sums_ref, keep, send, buf, e_ref, grad, sem, sems,
):
    copy = weight_copy(pack, 32 * 7, buf, sem)
    copy.start()

    def put(rows, value):
        total = cot_ref[rows, :].astype(F32) + value
        dx_ref[rows, :] = total
        e_ref[rows, :] = total.astype(BF)

    gain, shift = norm_grad(x2_ref, da_ref, vec_ref[4:5, :], put)
    sums_ref[0:1, :] = gain
    sums_ref[1:2, :] = shift
    sums_ref[2:3, :] = column_sum(e_ref)
    grad_weight(o_ref, e_ref, grad)
    out = block_copies(sel_ref[0], grad, keep, send, 0, sems)
    start_all(out)
    copy.wait()

    def put_mixed(start, value):
        do_ref[:, pl.ds(start, TILE)] = value.astype(BF)

    times_t(e_ref, buf, put_mixed)
    wait_all(out)


def cross_out_grad(sel, da3, x2, cot, mixed, vec, pack):
    rows, width = x2.shape
    return pl.pallas_call(
        cross_out_grad_kernel,
        out_shape=[
            shape((rows, width), F32), shape((rows, width), BF), shape((3, width), F32),
            shape((4, 4, 32, width), BF), shape((4, 4, 32, width), BF),
        ],
        in_specs=[smem()] + [vmem()] * 5 + [hbm()],
        out_specs=[vmem()] * 3 + [hbm()] * 2,
        scratch_shapes=[
            pltpu.VMEM((32, 32, width), BF), pltpu.VMEM((rows, width), BF), pltpu.VMEM((8, 4, 32, width), BF),
            pltpu.SemaphoreType.DMA, pltpu.SemaphoreType.DMA((8,)),
        ],
        compiler_params=params(),
        cost_estimate=cost(4 * rows * width * width, 14 * MIB),
        name="cross_out_grad",
    )(sel, da3, x2, cot, mixed, vec, pack)


def attend_grad_kernel(causal, valid, q_ref, k_ref, v_ref, o_ref, do_ref, lse_ref, dq_ref, dk_ref, dv_ref):
    rows = q_ref.shape[0]
    scale = jnp.asarray(HD**-0.5, BF)
    query = masked_pair(q_ref[...] * scale)
    grad_out = masked_pair(do_ref[...])
    product = (do_ref[...].astype(F32) * o_ref[...].astype(F32)).T
    delta = jnp.concatenate(
        [jnp.sum(product[:HD], axis=0, keepdims=True), jnp.sum(product[HD:], axis=0, keepdims=True)], axis=1
    )
    lse = lse_ref[0]
    grad_query = jnp.zeros((2 * HD, 2 * rows), F32)
    for a, b in key_chunks(k_ref.shape[0]):
        key = k_ref[a:b, :]
        scores = exclude(dot_nt(key, query), a, rows, causal, valid)
        probs = jnp.exp(scores - lse)
        grad_probs = dot_nt(v_ref[a:b, :], grad_out)
        grad_scores = (probs * (grad_probs - delta)).astype(BF)
        dv_ref[a:b, :] = dot(probs.astype(BF), grad_out).astype(BF)
        dk_ref[a:b, :] = dot(grad_scores, query).astype(BF)
        grad_query += dot_tn(key, grad_scores)
    dq_ref[...] = (pair_back(grad_query, rows) * HD**-0.5).astype(BF)


def attend_grad(query, key, value, mixed, grad_mixed, lse, causal, valid):
    rows, width = query.shape
    keys = key.shape[0]
    pairs = width // (2 * HD)

    def column(count):
        return pl.BlockSpec((count, 2 * HD), lambda h: (0, h))

    line = pl.BlockSpec((1, 1, 2 * rows), lambda h: (h, 0, 0))
    return pl.pallas_call(
        functools.partial(attend_grad_kernel, causal, valid),
        grid=(pairs,),
        out_shape=[shape((rows, width), BF)] + [shape((keys, width), BF)] * 2,
        in_specs=[column(rows), column(keys), column(keys), column(rows), column(rows), line],
        out_specs=[column(rows), column(keys), column(keys)],
        compiler_params=params(),
        cost_estimate=cost(40 * rows * keys * width, 8 * keys * width),
        name="attend_causal_grad" if causal else "attend_grad",
    )(query, key, value, mixed, grad_mixed, lse)


def cross_query_grad_kernel(
    sel_ref, a_ref, dq_ref, x1_ref, dx2_ref, o_ref, vec_ref, pack,
    dx_ref, do_ref, sums_ref, keep, send, bufs, da_ref, e_ref, grads, sem, sems,
):
    copies = [weight_copy(pack, 32 * (4 - n), bufs.at[n], sem.at[n]) for n in range(2)]
    start_all(copies)
    sel = sel_ref[0]
    grad_weight(a_ref, dq_ref, grads.at[0])
    out = block_copies(sel, grads.at[0], keep, send, 32, sems.at[0])
    start_all(out)
    sums_ref[0:1, :] = column_sum(dq_ref)
    copies[0].wait()

    def put_act(start, value):
        da_ref[:, pl.ds(start, TILE)] = value

    times_t(dq_ref, bufs.at[0], put_act)

    def put(rows, value):
        total = dx2_ref[rows, :] + value
        dx_ref[rows, :] = total
        e_ref[rows, :] = total.astype(BF)

    gain, shift = norm_grad(x1_ref, da_ref, vec_ref[2:3, :], put)
    sums_ref[1:2, :] = gain
    sums_ref[2:3, :] = shift
    sums_ref[3:4, :] = column_sum(e_ref)
    grad_weight(o_ref, e_ref, grads.at[1])
    more = block_copies(sel, grads.at[1], keep, send, 0, sems.at[1])
    start_all(more)
    copies[1].wait()

    def put_mixed(start, value):
        do_ref[:, pl.ds(start, TILE)] = value.astype(BF)

    times_t(e_ref, bufs.at[1], put_mixed)
    wait_all(out)
    wait_all(more)


def cross_query_grad(sel, a2, dq2, x1, dx2, mixed, vec, pack):
    rows, width = x1.shape
    return pl.pallas_call(
        cross_query_grad_kernel,
        out_shape=[
            shape((rows, width), F32), shape((rows, width), BF), shape((4, width), F32),
            shape((4, 4, 64, width), BF), shape((4, 4, 64, width), BF),
        ],
        in_specs=[smem()] + [vmem()] * 6 + [hbm()],
        out_specs=[vmem()] * 3 + [hbm()] * 2,
        scratch_shapes=[
            pltpu.VMEM((2, 32, 32, width), BF), pltpu.VMEM((rows, width), F32), pltpu.VMEM((rows, width), BF),
            pltpu.VMEM((2, 8, 4, 32, width), BF), pltpu.SemaphoreType.DMA((2,)), pltpu.SemaphoreType.DMA((2, 8)),
        ],
        compiler_params=params(),
        cost_estimate=cost(8 * rows * width * width, 20 * MIB),
        name="cross_query_grad",
    )(sel, a2, dq2, x1, dx2, mixed, vec, pack)


def cross_key_grad_kernel(sel_ref, e_ref, dk_ref, dv_ref, sums_ref, keep, send, grads, sems):
    sel = sel_ref[0]
    copies = []
    for n, ref in enumerate((dk_ref, dv_ref)):
        grad_weight(e_ref, ref, grads.at[n])
        out = block_copies(sel, grads.at[n], keep, send, 32 * n, sems.at[n])
        start_all(out)
        copies += out
    sums_ref[...] = column_sum(dv_ref)
    wait_all(copies)


def cross_key_grad(sel, enc, dk2, dv2):
    frames, width = enc.shape
    return pl.pallas_call(
        cross_key_grad_kernel,
        out_shape=[shape((1, width), F32), shape((4, 4, 64, width), BF), shape((4, 4, 64, width), BF)],
        in_specs=[smem()] + [vmem()] * 3,
        out_specs=[vmem()] + [hbm()] * 2,
        scratch_shapes=[pltpu.VMEM((2, 8, 4, 32, width), BF), pltpu.SemaphoreType.DMA((2, 8))],
        compiler_params=params(),
        cost_estimate=cost(4 * frames * width * width, 14 * MIB),
        name="cross_key_grad",
    )(sel, enc, dk2, dv2)


def encoder_grad_kernel(dk_ref, dv_ref, pack, out_ref, bufs, sems):
    copies = [weight_copy(pack, 32 * (5 + n), bufs.at[n], sems.at[n]) for n in range(2)]
    start_all(copies)
    wait_all(copies)

    def put(start, value):
        out_ref[:, pl.ds(start, TILE)] = value

    times_t(dk_ref, bufs.at[0], put)

    def add(start, value):
        out_ref[:, pl.ds(start, TILE)] += value

    times_t(dv_ref, bufs.at[1], add)


def encoder_grad(dk2, dv2, pack):
    frames, width = dk2.shape
    return pl.pallas_call(
        encoder_grad_kernel,
        out_shape=shape((frames, width), F32),
        in_specs=[vmem()] * 2 + [hbm()],
        out_specs=vmem(),
        scratch_shapes=[pltpu.VMEM((2, 32, 32, width), BF), pltpu.SemaphoreType.DMA((2,))],
        compiler_params=params(),
        cost_estimate=cost(4 * frames * width * width, 16 * MIB),
        name="encoder_grad",
    )(dk2, dv2, pack)


def self_in_grad_kernel(
    sel_ref, a_ref, dq_ref, dk_ref, dv_ref, x_ref, dx1_ref, vec_ref, pack,
    dx_ref, sums_ref, keep, send, bufs, da_ref, grads, sem, sems,
):
    copies = [weight_copy(pack, 32 * n, bufs.at[n], sem.at[n]) for n in range(3)]
    start_all(copies)
    sel = sel_ref[0]
    out = []
    grad_refs = (dq_ref, dk_ref, dv_ref)
    for n, ref in enumerate(grad_refs):
        grad_weight(a_ref, ref, grads.at[n])
        more = block_copies(sel, grads.at[n], keep, send, 32 * n, sems.at[n])
        start_all(more)
        out += more
    sums_ref[0:1, :] = column_sum(dq_ref)
    sums_ref[1:2, :] = column_sum(dv_ref)
    for n, ref in enumerate(grad_refs):
        copies[n].wait()

        def put_act(start, value, n=n):
            if n:
                da_ref[:, pl.ds(start, TILE)] += value
            else:
                da_ref[:, pl.ds(start, TILE)] = value

        times_t(ref, bufs.at[n], put_act)

    def put(rows, value):
        dx_ref[rows, :] = dx1_ref[rows, :] + value

    gain, shift = norm_grad(x_ref, da_ref, vec_ref[0:1, :], put)
    sums_ref[2:3, :] = gain
    sums_ref[3:4, :] = shift
    wait_all(out)


def self_in_grad(sel, a1, dq1, dk1, dv1, x, dx1, vec, pack):
    rows, width = x.shape
    return pl.pallas_call(
        self_in_grad_kernel,
        out_shape=[
            shape((rows, width), F32), shape((4, width), F32),
            shape((4, 4, 96, width), BF), shape((4, 4, 96, width), BF),
        ],
        in_specs=[smem()] + [vmem()] * 7 + [hbm()],
        out_specs=[vmem()] * 2 + [hbm()] * 2,
        scratch_shapes=[
            pltpu.VMEM((3, 32, 32, width), BF), pltpu.VMEM((rows, width), F32),
            pltpu.VMEM((3, 8, 4, 32, width), BF), pltpu.SemaphoreType.DMA((3,)), pltpu.SemaphoreType.DMA((3, 8)),
        ],
        compiler_params=params(),
        cost_estimate=cost(12 * rows * width * width, 24 * MIB),
        name="self_in_grad",
    )(sel, a1, dq1, dk1, dv1, x, dx1, vec, pack)


SWAP = [(0, 1), (1, 0)]


def add_rounded(left, right):
    return (left.astype(F32) + right.astype(F32)).astype(BF)


def reduce_chain(part, received, first, second):
    def side(value, axis, at):
        return lax.index_in_dim(value, at, axis=0 if axis == "y" else 1, keepdims=True)

    out = add_rounded(side(part, first, 1), side(received, first, 1))
    mine = add_rounded(side(part, first, 0), side(received, first, 0))
    other = lax.ppermute(out, first, SWAP)
    out = add_rounded(side(mine, second, 1), side(other, second, 1))
    mine = add_rounded(side(mine, second, 0), side(other, second, 0))
    other = lax.ppermute(out, second, SWAP)
    return add_rounded(mine, other)[0, 0]


def reduce_fast(keep, send):
    rows, columns = keep.shape[2:]
    received = lax.ppermute(send, "c", SWAP)
    keep = keep.reshape((2, 2, 4, rows, columns))
    received = received.reshape(keep.shape)
    half = rows // 2
    parts = [
        reduce_chain(keep[:, :, :, :half], received[:, :, :, :half], "x", "y"),
        reduce_chain(keep[:, :, :, half:], received[:, :, :, half:], "y", "x"),
    ]
    both = jnp.concatenate(parts, axis=1)
    here = lax.axis_index("z")
    total = lax.dynamic_index_in_dim(both, here, 0, keepdims=False).astype(F32)
    for step in (1, 3, 2):
        piece = lax.dynamic_index_in_dim(both, lax.rem(here + step, 4), 0, keepdims=False)
        total += lax.ppermute(piece, "z", [(n, (n + step) % 4) for n in range(4)]).astype(F32)
    return total


def reduce_plain(keep, send):
    count = lax.axis_size(ALL)
    rows, columns = keep.shape[2:]
    whole = jnp.stack([keep, send], axis=1).reshape(32, rows, columns)
    if rows == 128:
        whole = whole.reshape(32 * rows, columns)
        return lax.psum_scatter(whole.astype(F32), ALL, scatter_dimension=0, tiled=True)
    many = rows // 32
    whole = whole.reshape(32, many, 32, columns).swapaxes(0, 1).reshape(many, 1024, columns)
    mine = lax.psum_scatter(whole.astype(F32), ALL, scatter_dimension=1, tiled=True)
    return mine.reshape(many * (1024 // count), columns)


def exchange(value, combine, axes):
    for axis in axes:
        size = lax.axis_size(axis)
        moved = [lax.ppermute(value, axis, [(n, (n + step) % size) for n in range(size)]) for step in range(1, size)]
        for other in moved:
            value = combine(value, other)
    return value


def gather_fast(attention, expand, contract, vectors):
    width = attention.shape[2]
    line = jnp.pad(vectors.reshape(1, -1), ((0, 7), (0, width - vectors.size)))
    attention = jnp.concatenate([attention.reshape(-1, width), line], axis=0)
    pieces = [expand[:, n * width : (n + 1) * width] for n in range(expand.shape[1] // width)]
    feed_pack = jnp.concatenate(pieces + [contract], axis=0)
    pack_a = lax.all_gather(attention, ALL, axis=0, tiled=False)
    pack_f = lax.all_gather(feed_pack, ALL, axis=0, tiled=False)
    vec = pack_a[:, 256, : vectors.size].reshape((32,) + vectors.shape).swapaxes(0, 1)
    return pack_a, pack_f, vec.reshape(vectors.shape[0], width).astype(F32)


def gather_plain(attention, expand, contract, vectors):
    attention = lax.all_gather(attention, ALL, axis=1, tiled=True)
    expand = lax.all_gather(expand, ALL, axis=0, tiled=True)
    contract = lax.all_gather(contract, ALL, axis=0, tiled=True)
    vectors = lax.all_gather(vectors, ALL, axis=1, tiled=True)
    width = attention.shape[2]
    pack_a = attention.reshape(8, 32, 32, width).swapaxes(0, 1).reshape(32, 256, width)
    first = expand.reshape(32, 32, 4, width).swapaxes(1, 2).reshape(32, 128, width)
    pack_f = jnp.concatenate([first, contract.reshape(32, 128, width)], axis=1)
    return pack_a, pack_f, vectors.astype(F32)


def adam_update(master, gradient, first, second, step_value, clip_scale):
    first_new = beta_first * first.astype(F32) + (1.0 - beta_first) * gradient
    second_new = beta_second * second + (1.0 - beta_second) * gradient * gradient
    direction = (
        first_new
        / (1.0 - beta_first**step_value)
        / (jnp.sqrt(second_new / (1.0 - beta_second**step_value)) + eps_adam)
    )
    master_new = (master - learn_rate * (direction + weight_decay * master)) * clip_scale
    return (first_new, second_new, master_new)


def head_maxima(top, rows):
    return jnp.max(top.reshape(-1, rows), axis=1)


def one_sequence(sel, x, enc, frames, cot, vec, pack_a, pack_f):
    rows = x.shape[0]
    a1, q1, k1, v1 = self_in(x, vec, pack_a)
    o1, lse1, top1 = attend(q1, k1, v1, True, rows)
    x1, a2, q2 = self_out(o1, x, vec, pack_a)
    k2, v2 = cross_in(enc, vec, pack_a)
    o2, lse2, top2 = attend(q2, k2, v2, False, frames)
    maxima = jnp.stack([head_maxima(top1, rows), head_maxima(top2, rows)])
    x2, a3 = cross_out(o2, x1, vec, pack_a)
    result, da3, gb1, gb2, keep1, send1, keep2, send2 = feed(sel, a3, x2, cot, vec, pack_f)
    dx2, do2, sums3, keep_co, send_co = cross_out_grad(sel, da3, x2, cot, o2, vec, pack_a)
    dq2, dk2, dv2 = attend_grad(q2, k2, v2, o2, do2, lse2, False, frames)
    sums_v, keep_kv, send_kv = cross_key_grad(sel, enc, dk2, dv2)
    dx1, do1, sums2, keep_oq, send_oq = cross_query_grad(sel, a2, dq2, x1, dx2, o1, vec, pack_a)
    dq1, dk1, dv1 = attend_grad(q1, k1, v1, o1, do1, lse1, True, rows)
    grad_input, sums1, keep_s, send_s = self_in_grad(sel, a1, dq1, dk1, dv1, x, dx1, vec, pack_a)
    grad_encoder = encoder_grad(dk2, dv2, pack_a)[:frames]
    g_vectors = jnp.concatenate(
        [
            sums1[2:4], sums2[1:3], sums3[0:2],
            sums1[0:2], sums2[3:4], sums2[0:1], sums_v, sums3[2:3], gb2,
            gb1.reshape(-1, x.shape[1]),
        ],
        axis=0,
    )
    packs = [(keep1, send1), (keep2, send2), (keep_co, send_co), (keep_kv, send_kv), (keep_oq, send_oq), (keep_s, send_s)]
    return result, grad_input, grad_encoder, g_vectors, maxima, packs


def local(
    fast,
    inputs,
    encoder,
    cotangent,
    attention_master,
    expand_master,
    contract_master,
    vectors_master,
    attention_first,
    expand_first,
    contract_first,
    vectors_first,
    attention_second,
    expand_second,
    contract_second,
    vectors_second,
):
    sequences, rows, width = inputs.shape
    frames = encoder.shape[1]
    padded = -(-frames // 16) * 16
    owned = [m.astype(BF) for m in (attention_master, expand_master, contract_master, vectors_master)]
    pack_a, pack_f, vec = (gather_fast if fast else gather_plain)(*owned)
    place = lax.axis_index(("y", "x", "c")) if fast else 0
    sel = jnp.full((1,), place, jnp.int32)
    done = []
    for n in range(sequences):
        enc = jnp.pad(encoder[n], ((0, padded - frames), (0, 0)))
        done.append(one_sequence(sel, inputs[n], enc, frames, cotangent[n], vec, pack_a, pack_f))
    result, grad_input, grad_encoder = (jnp.stack([d[k] for d in done]) for k in range(3))
    g_vectors = sum(d[3] for d in done[1:]) + done[0][3] if sequences > 1 else done[0][3]
    maxima = functools.reduce(jnp.maximum, [d[4] for d in done])
    packs = done[0][5]
    for d in done[1:]:
        packs = [tuple(add_rounded(a, b) for a, b in zip(p, q)) for p, q in zip(packs, d[5])]

    if fast:
        maxima = exchange(jnp.pad(maxima, ((0, 6), (0, 112))), jnp.maximum, ("c", "x", "y", "z"))[:2, :16]
        reduce = reduce_fast
    else:
        maxima = lax.pmax(maxima, ALL)
        reduce = reduce_plain
    g_expand, g_contract, g_co, g_kv, g_oq, g_s = [reduce(*p) for p in packs]

    def apart(value):
        return value.reshape(-1, attention_master.shape[1], width)

    g_oq, g_kv = apart(g_oq), apart(g_kv)
    g_attention = jnp.concatenate([apart(g_s), g_oq, g_kv, apart(g_co)], axis=0)
    shard_cols = vectors_master.shape[1]
    first_col = lax.axis_index(ALL) * shard_cols
    if fast:
        g_vectors = exchange(jnp.pad(g_vectors, ((0, 7), (0, 0))), jnp.add, ("c", "x", "y", "z"))[:VEC_ROWS]
        g_vectors = lax.dynamic_slice_in_dim(g_vectors, first_col, shard_cols, 1)
    else:
        g_vectors = lax.psum_scatter(g_vectors, ALL, scatter_dimension=1, tiled=True)

    clip_cols = jnp.repeat(jnp.sqrt(clip_limit / jnp.maximum(maxima, clip_limit)), HD, axis=1)
    unit_row = jnp.ones_like(clip_cols[0])
    clip_attention = jnp.stack(
        [clip_cols[0], clip_cols[0], unit_row, unit_row, clip_cols[1], clip_cols[1], unit_row, unit_row]
    )[:, None, :]
    local_cols = lax.dynamic_slice_in_dim(clip_cols, first_col, shard_cols, 1)
    clip_vectors = jnp.ones_like(vectors_master).at[6].set(local_cols[0]).at[9].set(local_cols[1])
    step_value = float(ADAM_STEP)
    new_attention = adam_update(
        attention_master, g_attention, attention_first, attention_second, step_value, clip_attention
    )
    new_expand = adam_update(expand_master, g_expand, expand_first, expand_second, step_value, 1.0)
    new_contract = adam_update(contract_master, g_contract, contract_first, contract_second, step_value, 1.0)
    new_vectors = adam_update(vectors_master, g_vectors, vectors_first, vectors_second, step_value, clip_vectors)
    return (
        result,
        grad_input,
        grad_encoder,
        g_attention,
        g_expand,
        g_contract,
        g_vectors,
        new_attention[0],
        new_expand[0],
        new_contract[0],
        new_vectors[0],
        new_attention[1],
        new_expand[1],
        new_contract[1],
        new_vectors[1],
        new_attention[2],
        new_expand[2],
        new_contract[2],
        new_vectors[2],
    )


def solution(mesh):
    planes = mesh.shape["dp"] // 2
    side = math.isqrt(planes)
    if side * side * 2 != mesh.shape["dp"]:
        side = 1
    sizes = (mesh.shape["dp"] // (2 * side), side, 2, mesh.shape["fsdp"])
    fast = sizes == (2, 2, 2, 4)
    mesh = Mesh(mesh.devices.reshape(sizes), ALL)
    shards = (
        P(ALL, None, None),
        P(ALL, None, None),
        P(ALL, None, None),
    )
    weights = (P(None, ALL, None), P(ALL, None), P(ALL, None), P(None, ALL))
    return jax.shard_map(
        functools.partial(local, fast),
        mesh=mesh,
        in_specs=shards + weights * 3,
        out_specs=shards + weights * 4,
        check_vma=False,
    )
```

```python
import functools
import math

import jax
import jax.numpy as jnp
from jax import lax
from jax.experimental import pallas as pl
from jax.experimental.pallas import tpu as pltpu
from jax.sharding import Mesh
from jax.sharding import PartitionSpec as P

HD = 64
ADAM_STEP = 4

eps_norm = 1e-05
clip_limit = 1.0
learn_rate = 0.05
beta_first = 0.9
beta_second = 0.999
eps_adam = 1e-08
weight_decay = 0.1

BF = jnp.bfloat16
F32 = jnp.float32
ALL = ("y", "x", "c", "z")
TILE = 256
KEY_CHUNK = 256
VEC_ROWS = 17
MIB = 1024 * 1024


def dot(left, right):
    return jnp.dot(left, right, preferred_element_type=F32)


def dot_tn(left, right):
    return lax.dot_general(left, right, (((0,), (0,)), ((), ())), preferred_element_type=F32)


def dot_nt(left, right):
    return lax.dot_general(left, right, (((1,), (1,)), ((), ())), preferred_element_type=F32)


def params(limit=60):
    return pltpu.CompilerParams(vmem_limit_bytes=limit * MIB)


def vmem():
    return pl.BlockSpec(memory_space=pltpu.VMEM)


def hbm():
    return pl.BlockSpec(memory_space=pltpu.HBM)


def smem():
    return pl.BlockSpec(memory_space=pltpu.SMEM)


def shape(dims, dtype):
    return jax.ShapeDtypeStruct(tuple(dims), dtype)


def cost(flops, nbytes):
    return pl.CostEstimate(flops=int(flops), bytes_accessed=int(nbytes), transcendentals=0)


class Pack:
    def __init__(self, array, base=0):
        self.array, self.base = array, base


def weight_start(place_ref, pack, row, buf, sem):
    lines = pl.ds(pack.base + row, buf.shape[1])
    pltpu.make_async_copy(pack.array.at[:, lines, :], buf, sem).start()


def call(kernel, packs, args, **settings):
    first, last = len(args), len(args) + len(packs)

    def body(*refs):
        held = [Pack(ref, p.base) for ref, p in zip(refs[first:last], packs)]
        kernel(*refs[:first], *held, *refs[last:])

    specs = settings.pop("in_specs") + [hbm()] * len(packs)
    return pl.pallas_call(body, in_specs=specs, **settings)(*args, *[p.array for p in packs])


def weight_wait(buf, sem):
    pltpu.make_async_copy(buf, buf, sem).wait()


def times(act_ref, buf, put):
    depth = buf.shape[0] * buf.shape[1]

    @pl.loop(0, buf.shape[2] // TILE)
    def _(n):
        start = pl.multiple_of(n * TILE, TILE)
        put(start, dot(act_ref[...], buf[:, :, pl.ds(start, TILE)].reshape(depth, TILE)))


def times_t(act_ref, buf, put):
    per = TILE // buf.shape[1]

    @pl.loop(0, buf.shape[0] // per)
    def _(n):
        start = pl.multiple_of(n * TILE, TILE)
        rows = buf[pl.ds(n * per, per)].reshape(TILE, buf.shape[2])
        put(start, dot_nt(act_ref[...], rows))


def grad_weight(act_ref, grad_ref, out):
    @pl.loop(0, 4)
    def _(n):
        start = pl.multiple_of(n * TILE, TILE)
        tile = dot_tn(act_ref[:, pl.ds(start, TILE)], grad_ref[...])
        out[pl.ds(2 * n, 2)] = tile.astype(BF).reshape((2,) + out.shape[1:])


def block_copies(sel, grad, keep, send, row, sems):
    out = []
    for j in range(8):
        across, plane = j // 4, j % 4
        block = jnp.bitwise_xor(sel, plane * 2 + across)
        target = (send if across else keep).at[plane, :, pl.ds(row, grad.shape[2]), :]
        out.append(pltpu.make_async_copy(grad.at[block], target, sems.at[j]))
    return out


def start_all(copies):
    for one in copies:
        one.start()


def wait_all(copies):
    for one in copies:
        one.wait()


def row_chunks(count, size=64):
    return [slice(a, min(a + size, count)) for a in range(0, count, size)]


def normalise(values):
    centered = values - jnp.mean(values, axis=-1, keepdims=True)
    inv = lax.rsqrt(jnp.mean(centered * centered, axis=-1, keepdims=True) + eps_norm)
    return centered * inv, inv


def norm_into(src, gain, shift, out_ref):
    for rows in row_chunks(src.shape[0]):
        normed, _ = normalise(src[rows, :].astype(F32))
        out_ref[rows, :] = (normed * gain + shift).astype(BF)


def norm_grad(src, grad_ref, gain, put):
    gain_sum = jnp.zeros((1, src.shape[1]), F32)
    shift_sum = jnp.zeros((1, src.shape[1]), F32)
    for rows in row_chunks(src.shape[0]):
        normed, inv = normalise(src[rows, :].astype(F32))
        grad = grad_ref[rows, :]
        gain_sum += jnp.sum(grad * normed, axis=0, keepdims=True)
        shift_sum += jnp.sum(grad, axis=0, keepdims=True)
        scaled = grad * gain
        mean_one = jnp.mean(scaled, axis=-1, keepdims=True)
        mean_two = jnp.mean(scaled * normed, axis=-1, keepdims=True)
        put(rows, inv * (scaled - mean_one - normed * mean_two))
    return gain_sum, shift_sum


def column_sum(ref):
    total = jnp.zeros((1, ref.shape[1]), F32)
    for rows in row_chunks(ref.shape[0], 128):
        total += jnp.sum(ref[rows, :].astype(F32), axis=0, keepdims=True)
    return total


def self_in_kernel(place_ref, x_ref, vec_ref, one, two, a_ref, q_ref, k_ref, v_ref, bufs, sems):
    weight_start(place_ref, one, 0, bufs.at[0], sems.at[0])
    weight_start(place_ref, one, 32, bufs.at[1], sems.at[1])
    weight_start(place_ref, two, 0, bufs.at[2], sems.at[2])
    norm_into(x_ref, vec_ref[0:1, :], vec_ref[1:2, :], a_ref)
    for n, (out, bias) in enumerate(((q_ref, 6), (k_ref, None), (v_ref, 7))):
        weight_wait(bufs.at[n], sems.at[n])

        def put(start, value, out=out, bias=bias):
            if bias is not None:
                value = value + vec_ref[bias : bias + 1, pl.ds(start, TILE)]
            out[:, pl.ds(start, TILE)] = value.astype(BF)

        times(a_ref, bufs.at[n], put)


def self_in(place, x, vec, packs):
    rows, width = x.shape
    full = shape((rows, width), BF)
    return call(
        self_in_kernel,
        packs,
        [place, x, vec],
        out_shape=[full] * 4,
        in_specs=[smem(), vmem(), vmem()],
        out_specs=[vmem()] * 4,
        scratch_shapes=[pltpu.VMEM((3, 32, 32, width), BF), pltpu.SemaphoreType.DMA((3,))],
        compiler_params=params(48),
        cost_estimate=cost(6 * rows * width * width, 10 * MIB),
        name="self_in",
    )


def masked_pair(value):
    lane = lax.broadcasted_iota(jnp.int32, value.shape, 1)
    zero = jnp.zeros_like(value)
    return jnp.concatenate([jnp.where(lane < HD, value, zero), jnp.where(lane < HD, zero, value)], axis=0)


def pair_back(both, rows):
    line = lax.broadcasted_iota(jnp.int32, (2 * HD, rows), 0)
    return jnp.where(line < HD, both[:, :rows], both[:, rows:]).T


def key_chunks(count):
    return [(a, min(a + KEY_CHUNK, count)) for a in range(0, count, KEY_CHUNK)]


def exclude(scores, start, rows, causal, valid):
    key = lax.broadcasted_iota(jnp.int32, scores.shape, 0) + start
    if causal:
        query = lax.broadcasted_iota(jnp.int32, scores.shape, 1)
        query = jnp.where(query >= rows, query - rows, query)
        return jnp.where(key <= query, scores, -1e30)
    if start + scores.shape[0] > valid:
        return jnp.where(key < valid, scores, -1e30)
    return scores


def attend_kernel(causal, valid, q_ref, k_ref, v_ref, o_ref, lse_ref, top_ref, held):
    rows = q_ref.shape[0]
    query = masked_pair(q_ref[...] * jnp.asarray(HD**-0.5, BF))
    top = jnp.full((1, 2 * rows), -1e30, F32)
    for a, b in key_chunks(k_ref.shape[0]):
        scores = exclude(dot_nt(k_ref[a:b, :], query), a, rows, causal, valid)
        held[a:b, :] = scores
        top = jnp.maximum(top, jnp.max(scores, axis=0, keepdims=True))
    total = jnp.zeros((1, 2 * rows), F32)
    mixed = jnp.zeros((2 * HD, 2 * rows), F32)
    for a, b in key_chunks(k_ref.shape[0]):
        probs = jnp.exp(held[a:b, :] - top)
        total += jnp.sum(probs, axis=0, keepdims=True)
        mixed += dot_tn(v_ref[a:b, :], probs.astype(BF))
    o_ref[...] = pair_back(mixed * (1.0 / total), rows).astype(BF)
    lane = lax.broadcasted_iota(jnp.int32, (1, 2 * HD), 1)
    first, second = (jnp.max(part, axis=1, keepdims=True) for part in (top[:, :rows], top[:, rows:]))
    top_ref[0] = jnp.where(lane == 0, first, second)
    lse_ref[0] = top + jnp.log(total)


def attend(query, key, value, causal, valid):
    rows, width = query.shape
    keys = key.shape[0]
    pairs = width // (2 * HD)

    def column(count):
        return pl.BlockSpec((count, 2 * HD), lambda h: (0, h))

    line = pl.BlockSpec((1, 1, 2 * rows), lambda h: (h, 0, 0))
    return pl.pallas_call(
        functools.partial(attend_kernel, causal, valid),
        grid=(pairs,),
        out_shape=[shape((rows, width), BF), shape((pairs, 1, 2 * rows), F32), shape((pairs, 1, 2 * HD), F32)],
        in_specs=[column(rows), column(keys), column(keys)],
        out_specs=[column(rows), line, pl.BlockSpec((1, 1, 2 * HD), lambda h: (h, 0, 0))],
        scratch_shapes=[pltpu.VMEM((keys, 2 * rows), F32)],
        compiler_params=params(48),
        cost_estimate=cost(16 * rows * keys * width, 4 * keys * width),
        name="attend_causal" if causal else "attend",
    )(query, key, value)


def self_out_kernel(place_ref, o_ref, x_ref, vec_ref, one, two, x1_ref, a_ref, q_ref, bufs, sems):
    weight_start(place_ref, two, 32, bufs.at[0], sems.at[0])
    weight_start(place_ref, one, 32, bufs.at[1], sems.at[1])
    weight_wait(bufs.at[0], sems.at[0])

    def put_residual(start, value):
        cols = pl.ds(start, TILE)
        x1_ref[:, cols] = x_ref[:, cols].astype(F32) + (value + vec_ref[8:9, cols])

    times(o_ref, bufs.at[0], put_residual)
    norm_into(x1_ref, vec_ref[2:3, :], vec_ref[3:4, :], a_ref)
    weight_wait(bufs.at[1], sems.at[1])

    def put_query(start, value):
        cols = pl.ds(start, TILE)
        q_ref[:, cols] = (value + vec_ref[9:10, cols]).astype(BF)

    times(a_ref, bufs.at[1], put_query)


def self_out(place, mixed, x, vec, packs):
    rows, width = x.shape
    return call(
        self_out_kernel,
        packs,
        [place, mixed, x, vec],
        out_shape=[shape((rows, width), F32), shape((rows, width), BF), shape((rows, width), BF)],
        in_specs=[smem()] + [vmem()] * 3,
        out_specs=[vmem()] * 3,
        scratch_shapes=[pltpu.VMEM((2, 32, 32, width), BF), pltpu.SemaphoreType.DMA((2,))],
        compiler_params=params(48),
        cost_estimate=cost(4 * rows * width * width, 10 * MIB),
        name="self_out",
    )


def cross_in_kernel(place_ref, e_ref, vec_ref, one, two, k_ref, v_ref, bufs, sems):
    for n, part in enumerate((one, two)):
        weight_start(place_ref, part, 0, bufs.at[n], sems.at[n])
    for n, (out, bias) in enumerate(((k_ref, None), (v_ref, 10))):
        weight_wait(bufs.at[n], sems.at[n])

        def put(start, value, out=out, bias=bias):
            if bias is not None:
                value = value + vec_ref[bias : bias + 1, pl.ds(start, TILE)]
            out[:, pl.ds(start, TILE)] = value.astype(BF)

        times(e_ref, bufs.at[n], put)


def cross_in(place, enc, vec, packs):
    frames, width = enc.shape
    return call(
        cross_in_kernel,
        packs,
        [place, enc, vec],
        out_shape=[shape((frames, width), BF)] * 2,
        in_specs=[smem()] + [vmem()] * 2,
        out_specs=[vmem()] * 2,
        scratch_shapes=[pltpu.VMEM((2, 32, 32, width), BF), pltpu.SemaphoreType.DMA((2,))],
        compiler_params=params(48),
        cost_estimate=cost(4 * frames * width * width, 14 * MIB),
        name="cross_in",
    )


def cross_out_kernel(place_ref, o_ref, x1_ref, vec_ref, two, x2_ref, a_ref, buf, sem):
    weight_start(place_ref, two, 32, buf, sem)
    weight_wait(buf, sem)

    def put(start, value):
        cols = pl.ds(start, TILE)
        x2_ref[:, cols] = x1_ref[:, cols] + (value + vec_ref[11:12, cols])

    times(o_ref, buf, put)
    norm_into(x2_ref, vec_ref[4:5, :], vec_ref[5:6, :], a_ref)


def cross_out(place, mixed, x1, vec, packs):
    rows, width = x1.shape
    return call(
        cross_out_kernel,
        packs,
        [place, mixed, x1, vec],
        out_shape=[shape((rows, width), F32), shape((rows, width), BF)],
        in_specs=[smem()] + [vmem()] * 3,
        out_specs=[vmem()] * 2,
        scratch_shapes=[pltpu.VMEM((32, 32, width), BF), pltpu.SemaphoreType.DMA],
        compiler_params=params(48),
        cost_estimate=cost(2 * rows * width * width, 8 * MIB),
        name="cross_out",
    )


def whole(dims):
    return pl.BlockSpec(dims, lambda n: (0,) * len(dims))


def feed_kernel(
    a_ref, x2_ref, e_ref, vec_ref, bias_ref, w1_ref, w2_ref, out_ref, df_ref, gb1_ref, gb2_ref, grad_ref, total
):
    step = pl.program_id(0)
    wide = w1_ref.shape[2]
    depth = a_ref.shape[1]

    @pl.when(step == 0)
    def _():
        total[...] = x2_ref[...] + vec_ref[12:13, :]
        gb2_ref[...] = column_sum(e_ref)

    w2 = w2_ref[...].reshape(wide, depth)
    pre = dot(a_ref[...], w1_ref[...].reshape(depth, wide)) + bias_ref[0]
    cdf = 0.5 * (1.0 + lax.erf(pre * math.sqrt(0.5)))
    act = (pre * cdf).astype(BF)
    slope = cdf + pre * (jnp.exp(-0.5 * (pre * pre)) * (1.0 / math.sqrt(2.0 * math.pi)))
    grad_ref[0] = dot_tn(act, e_ref[...]).astype(BF).reshape(grad_ref.shape[1:])
    grad_pre = (dot_nt(e_ref[...], w2) * slope).astype(BF)
    df_ref[...] = grad_pre
    gb1_ref[0] = jnp.sum(grad_pre.astype(F32), axis=0, keepdims=True)
    total[...] += dot(act, w2)

    @pl.when(step == pl.num_programs(0) - 1)
    def _():
        out_ref[...] = total[...].astype(BF)


def feed(a3, x2, cot, vec, pack):
    rows, width = a3.shape
    hidden = 4 * width
    wide = hidden // 8
    bias = vec[13:].reshape(8, 1, wide)
    return pl.pallas_call(
        feed_kernel,
        grid=(8,),
        out_shape=[
            shape((rows, width), BF), shape((rows, hidden), BF), shape((8, 1, wide), F32), shape((1, width), F32),
            shape((8, 4, 256, width), BF),
        ],
        in_specs=[
            whole((rows, width)),
            whole((rows, width)),
            whole((rows, width)),
            whole(vec.shape),
            pl.BlockSpec((1, 1, wide), lambda n: (n, 0, 0)),
            pl.BlockSpec((32, 32, wide), lambda n: (0, n // 2, n % 2)),
            pl.BlockSpec((4, 128, width), lambda n: (n, 1, 0)),
        ],
        out_specs=[
            whole((rows, width)),
            pl.BlockSpec((rows, wide), lambda n: (0, n)),
            pl.BlockSpec((1, 1, wide), lambda n: (n, 0, 0)),
            whole((1, width)),
            pl.BlockSpec((1, 4, 128, width), lambda n: (n, 0, 1, 0)),
        ],
        scratch_shapes=[pltpu.VMEM((rows, width), F32)],
        compiler_params=params(48),
        cost_estimate=cost(8 * rows * width * hidden, 30 * MIB),
        name="feed",
    )(a3, x2, cot, vec, bias, pack, pack)


def feed_grad_kernel(a_ref, df_ref, w1_ref, grad_in, da_ref, grad_ref):
    wide = w1_ref.shape[2]
    grad_pre = df_ref[...]
    grad_ref[...] = dot_tn(a_ref[...], grad_pre).astype(BF).reshape(grad_ref.shape)

    @pl.when(pl.program_id(0) == 0)
    def _():
        da_ref[...] = jnp.zeros_like(da_ref)

    da_ref[...] += dot_nt(grad_pre, w1_ref[...].reshape(a_ref.shape[1], wide))


def feed_grad(a3, df, grad, pack):
    rows, width = a3.shape
    hidden = df.shape[1]
    wide = hidden // 8
    return pl.pallas_call(
        feed_grad_kernel,
        grid=(8,),
        out_shape=[shape((rows, width), F32), shape(grad.shape, BF)],
        in_specs=[
            whole((rows, width)),
            pl.BlockSpec((rows, wide), lambda n: (0, n)),
            pl.BlockSpec((32, 32, wide), lambda n: (0, n // 2, n % 2)),
            hbm(),
        ],
        out_specs=[
            whole((rows, width)),
            pl.BlockSpec((8, 4, 32, wide), lambda n: (0, 0, n // 2, n % 2)),
        ],
        input_output_aliases={3: 1},
        compiler_params=params(48),
        cost_estimate=cost(4 * rows * width * hidden, 22 * MIB),
        name="feed_grad",
    )(a3, df, pack, grad)


def cross_out_grad_kernel(
    place_ref, da_ref, x2_ref, cot_ref, o_ref, vec_ref, two,
    dx_ref, do_ref, sums_ref, keep, send, buf, e_ref, grad, sem, sems,
):
    weight_start(place_ref, two, 32, buf, sem)

    def put(rows, value):
        total = cot_ref[rows, :].astype(F32) + value
        dx_ref[rows, :] = total
        e_ref[rows, :] = total.astype(BF)

    gain, shift = norm_grad(x2_ref, da_ref, vec_ref[4:5, :], put)
    sums_ref[0:1, :] = gain
    sums_ref[1:2, :] = shift
    sums_ref[2:3, :] = column_sum(e_ref)
    grad_weight(o_ref, e_ref, grad)
    out = block_copies(place_ref[0], grad, keep, send, 64, sems)
    start_all(out)
    weight_wait(buf, sem)

    def put_mixed(start, value):
        do_ref[:, pl.ds(start, TILE)] = value.astype(BF)

    times_t(e_ref, buf, put_mixed)
    wait_all(out)


def cross_out_grad(place, da3, x2, cot, mixed, vec, packs):
    rows, width = x2.shape
    blocks = shape((4, 4, 96, width), BF)
    return call(
        cross_out_grad_kernel,
        packs,
        [place, da3, x2, cot, mixed, vec],
        out_shape=[
            shape((rows, width), F32), shape((rows, width), BF), shape((3, width), F32), blocks, blocks,
        ],
        in_specs=[smem()] + [vmem()] * 5,
        out_specs=[vmem()] * 3 + [hbm()] * 2,
        scratch_shapes=[
            pltpu.VMEM((32, 32, width), BF), pltpu.VMEM((rows, width), BF), pltpu.VMEM((8, 4, 32, width), BF),
            pltpu.SemaphoreType.DMA, pltpu.SemaphoreType.DMA((8,)),
        ],
        compiler_params=params(48),
        cost_estimate=cost(4 * rows * width * width, 14 * MIB),
        name="cross_out_grad",
    )


def attend_grad_kernel(causal, valid, q_ref, k_ref, v_ref, o_ref, do_ref, lse_ref, *refs):
    dq_ref, dk_ref, dv_ref = refs[-3:]
    rows = q_ref.shape[0]
    scale = jnp.asarray(HD**-0.5, BF)
    query = masked_pair(q_ref[...] * scale)
    grad_out = masked_pair(do_ref[...])
    product = (do_ref[...].astype(F32) * o_ref[...].astype(F32)).T
    delta = jnp.concatenate(
        [jnp.sum(product[:HD], axis=0, keepdims=True), jnp.sum(product[HD:], axis=0, keepdims=True)], axis=1
    )
    lse = lse_ref[0]
    grad_query = jnp.zeros((2 * HD, 2 * rows), F32)
    for a, b in key_chunks(k_ref.shape[0]):
        key = k_ref[a:b, :]
        scores = exclude(dot_nt(key, query), a, rows, causal, valid)
        probs = jnp.exp(scores - lse)
        grad_probs = dot_nt(v_ref[a:b, :], grad_out)
        grad_scores = (probs * (grad_probs - delta)).astype(BF)
        dv_ref[a:b, :] = dot(probs.astype(BF), grad_out).astype(BF)
        dk_ref[a:b, :] = dot(grad_scores, query).astype(BF)
        grad_query += dot_tn(key, grad_scores)
    dq_ref[...] = (pair_back(grad_query, rows) * HD**-0.5).astype(BF)


def attend_grad(query, key, value, mixed, grad_mixed, lse, causal, valid, part=(0, 1), before=()):
    rows, width = query.shape
    keys = key.shape[0]
    pairs = width // (2 * HD) // part[1]
    skip = part[0] * pairs

    def column(count):
        return pl.BlockSpec((count, 2 * HD), lambda h: (0, h + skip))

    line = pl.BlockSpec((1, 1, 2 * rows), lambda h: (h + skip, 0, 0))
    return pl.pallas_call(
        functools.partial(attend_grad_kernel, causal, valid),
        grid=(pairs,),
        out_shape=[shape((rows, width), BF)] + [shape((keys, width), BF)] * 2,
        in_specs=[column(rows), column(keys), column(keys), column(rows), column(rows), line] + [hbm()] * len(before),
        out_specs=[column(rows), column(keys), column(keys)],
        input_output_aliases={6 + n: n for n in range(len(before))},
        compiler_params=params(),
        cost_estimate=cost(40 * rows * keys * width // part[1], 8 * keys * width),
        name="attend_causal_grad" if causal else "attend_grad",
    )(query, key, value, mixed, grad_mixed, lse, *before)


def cross_query_grad_kernel(
    place_ref, a_ref, dq_ref, x1_ref, dx2_ref, o_ref, vec_ref, keep_in, send_in, one, two,
    dx_ref, do_ref, sums_ref, keep, send, bufs, da_ref, e_ref, grads, sem, sems,
):
    for n, part in enumerate((one, two)):
        weight_start(place_ref, part, 32, bufs.at[n], sem.at[n])
    place = place_ref[0]
    grad_weight(a_ref, dq_ref, grads.at[0])
    out = block_copies(place, grads.at[0], keep, send, 32, sems.at[0])
    start_all(out)
    sums_ref[0:1, :] = column_sum(dq_ref)
    weight_wait(bufs.at[0], sem.at[0])

    def put_act(start, value):
        da_ref[:, pl.ds(start, TILE)] = value

    times_t(dq_ref, bufs.at[0], put_act)

    def put(rows, value):
        total = dx2_ref[rows, :] + value
        dx_ref[rows, :] = total
        e_ref[rows, :] = total.astype(BF)

    gain, shift = norm_grad(x1_ref, da_ref, vec_ref[2:3, :], put)
    sums_ref[1:2, :] = gain
    sums_ref[2:3, :] = shift
    sums_ref[3:4, :] = column_sum(e_ref)
    grad_weight(o_ref, e_ref, grads.at[1])
    more = block_copies(place, grads.at[1], keep, send, 0, sems.at[1])
    start_all(more)
    weight_wait(bufs.at[1], sem.at[1])

    def put_mixed(start, value):
        do_ref[:, pl.ds(start, TILE)] = value.astype(BF)

    times_t(e_ref, bufs.at[1], put_mixed)
    wait_all(out)
    wait_all(more)


def cross_query_grad(place, a2, dq2, x1, dx2, mixed, vec, keep, send, packs):
    rows, width = x1.shape
    return call(
        cross_query_grad_kernel,
        packs,
        [place, a2, dq2, x1, dx2, mixed, vec, keep, send],
        out_shape=[
            shape((rows, width), F32), shape((rows, width), BF), shape((4, width), F32),
            shape(keep.shape, BF), shape(send.shape, BF),
        ],
        in_specs=[smem()] + [vmem()] * 6 + [hbm()] * 2,
        out_specs=[vmem()] * 3 + [hbm()] * 2,
        scratch_shapes=[
            pltpu.VMEM((2, 32, 32, width), BF), pltpu.VMEM((rows, width), F32), pltpu.VMEM((rows, width), BF),
            pltpu.VMEM((2, 8, 4, 32, width), BF), pltpu.SemaphoreType.DMA((2,)), pltpu.SemaphoreType.DMA((2, 8)),
        ],
        input_output_aliases={7: 3, 8: 4},
        compiler_params=params(),
        cost_estimate=cost(8 * rows * width * width, 20 * MIB),
        name="cross_query_grad",
    )


def cross_key_grad_kernel(place_ref, e_ref, dk_ref, dv_ref, keep_in, send_in, sums_ref, keep, send, grads, sems):
    copies = []
    for n, ref in enumerate((dk_ref, dv_ref)):
        grad_weight(e_ref, ref, grads.at[n])
        out = block_copies(place_ref[0], grads.at[n], keep, send, 96 + 32 * n, sems.at[n])
        start_all(out)
        copies += out
    sums_ref[...] = column_sum(dv_ref)
    wait_all(copies)


def cross_key_grad(place, enc, dk2, dv2, keep, send):
    frames, width = enc.shape
    return pl.pallas_call(
        cross_key_grad_kernel,
        out_shape=[shape((1, width), F32), shape(keep.shape, BF), shape(send.shape, BF)],
        in_specs=[smem()] + [vmem()] * 3 + [hbm()] * 2,
        input_output_aliases={4: 1, 5: 2},
        out_specs=[vmem()] + [hbm()] * 2,
        scratch_shapes=[pltpu.VMEM((2, 8, 4, 32, width), BF), pltpu.SemaphoreType.DMA((2, 8))],
        compiler_params=params(),
        cost_estimate=cost(4 * frames * width * width, 14 * MIB),
        name="cross_key_grad",
    )(place, enc, dk2, dv2, keep, send)


def encoder_grad_kernel(frames, place_ref, dk_ref, dv_ref, one, two, out_ref, bufs, sems):
    for n, part in enumerate((one, two)):
        weight_start(place_ref, part, 0, bufs.at[n], sems.at[n])
    for n in range(2):
        weight_wait(bufs.at[n], sems.at[n])
    width = dk_ref.shape[1]
    per = TILE // 32
    lines = width // 128

    @pl.loop(0, width // TILE)
    def _(n):
        total = dot_nt(dk_ref[...], bufs[0, pl.ds(n * per, per)].reshape(TILE, width))
        total += dot_nt(dv_ref[...], bufs[1, pl.ds(n * per, per)].reshape(TILE, width))
        for side in range(TILE // 128):
            start = n * (TILE // 128) + side
            out_ref[pl.ds(start, frames, stride=lines), :] = total[:frames, side * 128 : (side + 1) * 128]


def encoder_grad(place, dk2, dv2, packs, frames):
    width = dk2.shape[1]
    return call(
        functools.partial(encoder_grad_kernel, frames),
        packs,
        [place, dk2, dv2],
        out_shape=shape((frames * (width // 128), 128), F32),
        in_specs=[smem()] + [vmem()] * 2,
        out_specs=vmem(),
        scratch_shapes=[pltpu.VMEM((2, 32, 32, width), BF), pltpu.SemaphoreType.DMA((2,))],
        compiler_params=params(),
        cost_estimate=cost(4 * frames * width * width, 16 * MIB),
        name="encoder_grad",
    )


def self_weight_grad_kernel(place_ref, a_ref, dq_ref, dk_ref, dv_ref, sums_ref, keep, send, grads, sems):
    out = []
    for n, ref in enumerate((dq_ref, dk_ref, dv_ref)):
        grad_weight(a_ref, ref, grads.at[n])
        more = block_copies(place_ref[0], grads.at[n], keep, send, 32 * n, sems.at[n])
        start_all(more)
        out += more
    sums_ref[0:1, :] = column_sum(dq_ref)
    sums_ref[1:2, :] = column_sum(dv_ref)
    wait_all(out)


def self_weight_grad(place, a1, dq1, dk1, dv1):
    rows, width = a1.shape
    blocks = shape((4, 4, 160, width), BF)
    return pl.pallas_call(
        self_weight_grad_kernel,
        out_shape=[shape((2, width), F32), blocks, blocks],
        in_specs=[smem()] + [vmem()] * 4,
        out_specs=[vmem()] + [hbm()] * 2,
        scratch_shapes=[pltpu.VMEM((3, 8, 4, 32, width), BF), pltpu.SemaphoreType.DMA((3, 8))],
        compiler_params=params(),
        cost_estimate=cost(6 * rows * width * width, 10 * MIB),
        name="self_weight_grad",
    )(place, a1, dq1, dk1, dv1)


def self_in_grad_kernel(
    place_ref, dq_ref, dk_ref, dv_ref, x_ref, dx1_ref, vec_ref, one, two, dx_ref, sums_ref, bufs, da_ref, sems
):
    weight_start(place_ref, one, 0, bufs.at[0], sems.at[0])
    weight_start(place_ref, one, 32, bufs.at[1], sems.at[1])
    weight_start(place_ref, two, 0, bufs.at[2], sems.at[2])
    for n, ref in enumerate((dq_ref, dk_ref, dv_ref)):
        weight_wait(bufs.at[n], sems.at[n])

        def put_act(start, value, n=n):
            if n:
                da_ref[:, pl.ds(start, TILE)] += value
            else:
                da_ref[:, pl.ds(start, TILE)] = value

        times_t(ref, bufs.at[n], put_act)

    def put(rows, value):
        dx_ref[rows, :] = dx1_ref[rows, :] + value

    gain, shift = norm_grad(x_ref, da_ref, vec_ref[0:1, :], put)
    sums_ref[0:1, :] = gain
    sums_ref[1:2, :] = shift


def self_in_grad(place, dq1, dk1, dv1, x, dx1, vec, packs):
    rows, width = x.shape
    return call(
        self_in_grad_kernel,
        packs,
        [place, dq1, dk1, dv1, x, dx1, vec],
        out_shape=[shape((rows, width), F32), shape((2, width), F32)],
        in_specs=[smem()] + [vmem()] * 6,
        out_specs=[vmem()] * 2,
        scratch_shapes=[
            pltpu.VMEM((3, 32, 32, width), BF), pltpu.VMEM((rows, width), F32), pltpu.SemaphoreType.DMA((3,)),
        ],
        compiler_params=params(),
        cost_estimate=cost(6 * rows * width * width, 14 * MIB),
        name="self_in_grad",
    )


SWAP = [(0, 1), (1, 0)]
MATRICES = ((0, 1), (2, 3), (5, 4), (6, 7))


class Unit:
    def __init__(self, chain):
        self.chain, self.result, self.moved = chain, None, None
        self.wanted = next(chain)

    def advance(self, arrived):
        try:
            self.wanted = self.chain.send(arrived)
        except StopIteration as stop:
            self.wanted, self.result = None, stop.value


def step(run=None, inputs=(), start=(), finish=()):
    start, finish = ([u for u in units if u is not None] for units in (start, finish))
    operands = [[value for value, _, _ in u.wanted] for u in start]
    inputs, operands = lax.optimization_barrier((tuple(inputs), operands))
    for u, values in zip(start, operands):
        u.moved = [lax.ppermute(v, axis, pairs) for v, (_, axis, pairs) in zip(values, u.wanted)]
    out = run(*inputs) if run else ()
    if finish:
        out, moved = lax.optimization_barrier((out, [u.moved for u in finish]))
        for u, values in zip(finish, moved):
            u.advance(values)
    return out


def turns():
    return [[(n, (n + k) % 4) for n in range(4)] for k in range(4)]


def add_rounded(left, right):
    return (left.astype(F32) + right.astype(F32)).astype(BF)


def add_kernel(plan, sources, place_ref, *refs):
    left, right = refs[:sources], refs[sources : 2 * sources]
    *outs, one, two, total, sems, out_sems = refs[2 * sources :]
    pieces = plan(place_ref)
    copies = [
        [
            pltpu.make_async_copy(side[source].at[index], held.at[n], sems.at[k, n])
            for k, (side, held) in enumerate(((left, one), (right, two)))
        ]
        for n, (source, index, _, _) in enumerate(pieces)
    ]
    for pair in copies:
        start_all(pair)
    away = []
    for n, (_, _, out, index) in enumerate(pieces):
        wait_all(copies[n])
        total[n] = add_rounded(one[n], two[n])
        away.append(pltpu.make_async_copy(total.at[n], outs[out].at[index], out_sems.at[n]))
        away[-1].start()
    wait_all(away)


def add_pieces(place, left, right, outs, piece, plan, count):
    held = pltpu.VMEM((count,) + piece, BF)
    return pl.pallas_call(
        functools.partial(add_kernel, plan, len(left)),
        out_shape=[shape(o, BF) for o in outs],
        in_specs=[smem()] + [hbm()] * (2 * len(left)),
        out_specs=[hbm()] * len(outs),
        scratch_shapes=[
            held, held, held, pltpu.SemaphoreType.DMA((2, count)), pltpu.SemaphoreType.DMA((count,)),
        ],
        compiler_params=params(),
        cost_estimate=cost(0, 6 * count * math.prod(piece)),
        name="add_pieces",
    )(place, *left, *right)


def turn_z(place_ref, k):
    return jnp.bitwise_and(place_ref[1] + k, 3)


def reduce_chain(place, keep, send):
    rows, columns = keep.shape[2:]
    half = rows // 2
    parts = [pl.ds(0, half), pl.ds(half, half)]
    (moved,) = yield [(send, "c", SWAP)]

    def plan_one(_):
        out = []
        for plane in (3, 1, 2, 0):
            y, x = plane // 2, plane % 2
            out.append((0, (plane, slice(None), parts[0]), 0 if x else 2, y))
            out.append((0, (plane, slice(None), parts[1]), 1 if y else 3, x))
        return out

    outs = [(2, 4, half, columns)] * 4
    one, two, *mine = add_pieces(place, [keep], [moved], outs, (4, half, columns), plan_one, 8)
    moved = yield [(one, "x", SWAP), (two, "y", SWAP)]

    def plan_two(_):
        return [(n, side, n if side else 2 + n, slice(None)) for side in (1, 0) for n in range(2)]

    outs = [(4, half, columns)] * 4
    one, two, *mine = add_pieces(place, mine, list(moved), outs, (4, half, columns), plan_two, 4)
    moved = yield [(one, "y", SWAP), (two, "x", SWAP)]

    def plan_three(place_ref):
        return [(n, turn_z(place_ref, k), k, parts[n]) for k in (2, 1, 3, 0) for n in range(2)]

    pieces = add_pieces(place, mine, list(moved), [(rows, columns)] * 4, (half, columns), plan_three, 8)
    moved = yield [(pieces[k], "z", turns()[k]) for k in (1, 3, 2)]
    return functools.reduce(jnp.add, [value.astype(F32) for value in moved], pieces[0].astype(F32))


def z_chain(both):
    here = lax.axis_index("z")

    def piece(k):
        return lax.dynamic_index_in_dim(both, lax.rem(here + k, 4), 0, keepdims=False)

    moved = yield [(piece(k), "z", turns()[k]) for k in (1, 3, 2)]
    return functools.reduce(jnp.add, [value.astype(F32) for value in moved], piece(0).astype(F32))


def reduce_plain(keep, send):
    count = lax.axis_size(ALL)
    rows, columns = keep.shape[2:]
    total = jnp.stack([keep, send], axis=1).reshape(32, rows, columns)
    many = rows // 32
    total = total.reshape(32, many, 32, columns).swapaxes(0, 1).reshape(many, 1024, columns)
    mine = lax.psum_scatter(total.astype(F32), ALL, scatter_dimension=1, tiled=True)
    return mine.reshape(many * (1024 // count), columns)


def reduce_feed_plain(grad):
    columns = grad.shape[3]
    grad1 = grad[:, :, :128].reshape(32, 4, 32, columns).swapaxes(1, 2).reshape(1024, 4 * columns)
    grad2 = grad[:, :, 128:].reshape(4096, columns)
    return [lax.psum_scatter(g.astype(F32), ALL, scatter_dimension=0, tiled=True) for g in (grad1, grad2)]


def table_chain(table):
    row = lax.broadcasted_iota(jnp.int32, table.shape, 0)

    def combine(left, right):
        return jnp.where(row < VEC_ROWS, left + right, jnp.maximum(left, right))

    for axis in ("c", "x", "y"):
        moved = yield [(table, axis, SWAP)]
        table = combine(table, moved[0])
    for pairs in ([(0, 1), (1, 0), (2, 3), (3, 2)], [(0, 2), (2, 0), (1, 3), (3, 1)]):
        moved = yield [(table, "z", pairs)]
        table = combine(table, moved[0])
    return table


def vector_table(pack, row, rows, shard_cols):
    table = pack[:, row, : rows * shard_cols].reshape(32, rows, shard_cols).swapaxes(0, 1)
    return table.reshape(rows, 32 * shard_cols).astype(F32)


def feed_shard(expand, contract):
    width = contract.shape[1]
    pieces = [expand[:, n * width : (n + 1) * width] for n in range(expand.shape[1] // width)]
    return jnp.concatenate(pieces + [contract], axis=0)


def gather_fast(attention, expand, contract, vectors):
    width = attention.shape[2]
    line = jnp.pad(vectors.reshape(1, -1), ((0, 15), (0, width - vectors.size)))
    shard = jnp.concatenate([attention[m] for group in MATRICES for m in group] + [line], axis=0)
    pack = lax.all_gather(shard, ALL, axis=0, tiled=False)
    pack_f = lax.all_gather(feed_shard(expand, contract), ALL, axis=0, tiled=False)
    return parts_of(pack), pack_f, vector_table(pack, 256, *vectors.shape)


def parts_of(pack):
    return [Pack(pack, 64 * n) for n in range(4)]


def gather_plain(attention, expand, contract, vectors):
    attention = lax.all_gather(attention, ALL, axis=1, tiled=True)
    expand = lax.all_gather(expand, ALL, axis=0, tiled=True)
    contract = lax.all_gather(contract, ALL, axis=0, tiled=True)
    vectors = lax.all_gather(vectors, ALL, axis=1, tiled=True)
    width = attention.shape[2]
    pack = jnp.concatenate([attention[m].reshape(32, 32, width) for group in MATRICES for m in group], axis=1)
    first = expand.reshape(32, 32, 4, width).swapaxes(1, 2).reshape(32, 128, width)
    pack_f = jnp.concatenate([first, contract.reshape(32, 128, width)], axis=1)
    return parts_of(pack), pack_f, vectors.astype(F32)


def adam_update(master, gradient, first, second, step_value, clip_scale):
    first_new = beta_first * first.astype(F32) + (1.0 - beta_first) * gradient
    second_new = beta_second * second + (1.0 - beta_second) * gradient * gradient
    direction = (
        first_new
        / (1.0 - beta_first**step_value)
        / (jnp.sqrt(second_new / (1.0 - beta_second**step_value)) + eps_adam)
    )
    master_new = (master - learn_rate * (direction + weight_decay * master)) * clip_scale
    return (first_new, second_new, master_new)


def table_kernel(sums1, bias1, sums2, sums3, sums_v, gb1, gb2, top1, top2, out):
    out[...] = jnp.zeros_like(out)
    rows = [
        sums1[0:1, :], sums1[1:2, :], sums2[1:2, :], sums2[2:3, :], sums3[0:1, :], sums3[1:2, :],
        bias1[0:1, :], bias1[1:2, :], sums2[3:4, :], sums2[0:1, :], sums_v[...], sums3[2:3, :], gb2[...],
    ]
    for n, row in enumerate(rows):
        out[n : n + 1, :] = row
    half = gb1.shape[2]
    for n in range(gb1.shape[0]):
        out[len(rows) + n // 2 : len(rows) + n // 2 + 1, n % 2 * half : (n % 2 + 1) * half] = gb1[n]
    for n, top in enumerate((top1, top2)):
        for pair in range(top.shape[0]):
            lanes = slice(pair * 2 * HD, (pair + 1) * 2 * HD)
            out[VEC_ROWS + n : VEC_ROWS + n + 1, lanes] = top[pair]


def vector_table_of(*pieces):
    width = pieces[0].shape[1]
    return pl.pallas_call(
        table_kernel,
        out_shape=shape((24, width), F32),
        in_specs=[vmem()] * len(pieces),
        out_specs=vmem(),
        compiler_params=params(),
        cost_estimate=cost(0, 200000),
        name="vector_table",
    )(*pieces)


def maxima_of(table):
    return table[VEC_ROWS : VEC_ROWS + 2].reshape(2, -1, 2 * HD)[:, :, :2].reshape(2, -1)


def sequence_plain(place, x, enc, frames, cot, vec, packs, pack_f):
    rows, width = x.shape
    one_a, one_b, two_a, two_b = packs
    a1, q1, k1, v1 = self_in(place, x, vec, [one_a, one_b])
    o1, lse1, top1 = attend(q1, k1, v1, True, rows)
    x1, a2, q2 = self_out(place, o1, x, vec, [two_a, one_b])
    k2, v2 = cross_in(place, enc, vec, [two_a, two_b])
    o2, lse2, top2 = attend(q2, k2, v2, False, frames)
    x2, a3 = cross_out(place, o2, x1, vec, [two_b])
    result, df, gb1, gb2, grad = feed(a3, x2, cot, vec, pack_f)
    da3, grad = feed_grad(a3, df, grad, pack_f)
    dx2, do2, sums3, keep1, send1 = cross_out_grad(place, da3, x2, cot, o2, vec, [two_b])
    dq2, dk2, dv2 = attend_grad(q2, k2, v2, o2, do2, lse2, False, frames)
    dx1, do1, sums2, keep1, send1 = cross_query_grad(place, a2, dq2, x1, dx2, o1, vec, keep1, send1, [two_a, one_b])
    dq1, dk1, dv1 = attend_grad(q1, k1, v1, o1, do1, lse1, True, rows)
    bias1, keep2, send2 = self_weight_grad(place, a1, dq1, dk1, dv1)
    sums_v, keep2, send2 = cross_key_grad(place, enc, dk2, dv2, keep2, send2)
    grad_input, sums1 = self_in_grad(place, dq1, dk1, dv1, x, dx1, vec, [one_a, one_b])
    grad_encoder = encoder_grad(place, dk2, dv2, [two_a, two_b], frames).reshape(frames, width)
    table = vector_table_of(sums1, bias1, sums2, sums3, sums_v, gb1, gb2, top1, top2)
    g_vectors, maxima = table[:VEC_ROWS], maxima_of(table)
    return result, grad_input, grad_encoder, g_vectors, maxima, [(grad,), (keep1, send1), (keep2, send2)]


def gradients_plain(inputs, encoder, cotangent, owned):
    packs, pack_f, vec = gather_plain(*owned)
    place = jnp.zeros((2,), jnp.int32)
    frames = encoder.shape[1]
    done = []
    for n in range(inputs.shape[0]):
        enc = pad_frames(encoder[n])
        done.append(sequence_plain(place, inputs[n], enc, frames, cotangent[n], vec, packs, pack_f))
    result, grad_input, grad_encoder = (jnp.stack([d[k] for d in done]) for k in range(3))
    g_vectors = functools.reduce(jnp.add, [d[3] for d in done])
    maxima = functools.reduce(jnp.maximum, [d[4] for d in done])
    both = done[0][5]
    for d in done[1:]:
        both = [tuple(add_rounded(a, b) for a, b in zip(p, q)) for p, q in zip(both, d[5])]
    sums = reduce_feed_plain(*both[0]) + [reduce_plain(*p) for p in both[1:]]
    g_vectors = lax.psum_scatter(g_vectors, ALL, scatter_dimension=1, tiled=True)
    return result, grad_input, grad_encoder, sums, g_vectors, lax.pmax(maxima, ALL)


def pad_frames(enc):
    return jnp.pad(enc, ((0, -enc.shape[0] % 16), (0, 0)))


def gradients_fast(inputs, encoder, cotangent, owned):
    attention, expand, contract, vectors = owned
    x, cot = inputs[0], cotangent[0]
    rows, width = x.shape
    frames = encoder.shape[1]
    place = jnp.stack([lax.axis_index(("y", "x", "c")), lax.axis_index("z")]).astype(jnp.int32)
    (one_a, one_b, two_a, two_b), pack_f, vec = gather_fast(*owned)
    enc = pad_frames(encoder[0])
    a1, q1, k1, v1 = self_in(place, x, vec, [one_a, one_b])
    o1, lse1, top1 = attend(q1, k1, v1, True, rows)
    x1, a2, q2 = self_out(place, o1, x, vec, [two_a, one_b])
    k2, v2 = cross_in(place, enc, vec, [two_a, two_b])
    o2, lse2, top2 = attend(q2, k2, v2, False, frames)
    x2, a3 = cross_out(place, o2, x1, vec, [two_b])

    result, df, gb1, gb2, grad = feed(a3, x2, cot, vec, pack_f)
    da3, grad = feed_grad(a3, df, grad, pack_f)
    rf = lax.psum_scatter(grad, ("y", "x", "c"), scatter_dimension=0, tiled=True)[0]
    rf = lax.psum_scatter(rf, "z", scatter_dimension=0, tiled=True)[0].astype(F32)
    dx2, do2, sums3, keep, send = cross_out_grad(place, da3, x2, cot, o2, vec, [two_b])
    dq2, dk2, dv2 = attend_grad(q2, k2, v2, o2, do2, lse2, False, frames)
    dx1, do1, sums2, keep, send = cross_query_grad(place, a2, dq2, x1, dx2, o1, vec, keep, send, [two_a, one_b])
    r1 = Unit(reduce_chain(place, keep, send))
    dq1, dk1, dv1 = step(
        lambda do1: attend_grad(q1, k1, v1, o1, do1, lse1, True, rows), [do1], start=[r1], finish=[r1]
    )
    bias1, keep, send = step(
        lambda dq1, dk1, dv1: self_weight_grad(place, a1, dq1, dk1, dv1), [dq1, dk1, dv1], start=[r1]
    )
    sums_v, keep, send = step(
        lambda dk2: cross_key_grad(place, enc, dk2, dv2, keep, send), [dk2], finish=[r1]
    )
    r2 = Unit(reduce_chain(place, keep, send))
    grad_input, sums1 = step(
        lambda dq1, dk1, dv1: self_in_grad(place, dq1, dk1, dv1, x, dx1, vec, [one_a, one_b]),
        [dq1, dk1, dv1],
        start=[r1, r2],
        finish=[r1, r2],
    )
    table = Unit(table_chain(vector_table_of(sums1, bias1, sums2, sums3, sums_v, gb1, gb2, top1, top2)))
    step(start=[table], finish=[table])
    grad_encoder = step(
        lambda dk2: encoder_grad(place, dk2, dv2, [two_a, two_b], frames),
        [dk2],
        start=[r1, r2],
        finish=[r1, r2],
    )
    step(start=[r2, table], finish=[r2, table])
    step(start=[r2, table], finish=[r2, table])
    step(start=[table], finish=[table])
    step(start=[table], finish=[table])
    total = table.result
    shard_cols = vectors.shape[1]
    g_vectors = lax.dynamic_slice_in_dim(total[:VEC_ROWS], lax.axis_index(ALL) * shard_cols, shard_cols, 1)
    maxima = maxima_of(total)
    grad_encoder = grad_encoder.reshape(1, frames, width)
    g_expand = rf[:128].reshape(4, 32, width).swapaxes(0, 1).reshape(32, 4 * width)
    sums = [g_expand, rf[128:], r1.result, r2.result]
    return result[None], grad_input[None], grad_encoder, sums, g_vectors, maxima


def local(
    fast,
    inputs,
    encoder,
    cotangent,
    attention_master,
    expand_master,
    contract_master,
    vectors_master,
    attention_first,
    expand_first,
    contract_first,
    vectors_first,
    attention_second,
    expand_second,
    contract_second,
    vectors_second,
):
    width = inputs.shape[2]
    owned = [m.astype(BF) for m in (attention_master, expand_master, contract_master, vectors_master)]
    compute = gradients_fast if fast and inputs.shape[0] == 1 else gradients_plain
    result, grad_input, grad_encoder, sums, g_vectors, maxima = compute(inputs, encoder, cotangent, owned)
    g_expand, g_contract = sums[:2]
    out_query, rest = (value.reshape(-1, attention_master.shape[1], width) for value in sums[2:])
    g_attention = jnp.concatenate([rest[:3], out_query[:2], rest[3:], out_query[2:]], axis=0)
    shard_cols = vectors_master.shape[1]
    first_col = lax.axis_index(ALL) * shard_cols

    clip_cols = jnp.repeat(jnp.sqrt(clip_limit / jnp.maximum(maxima, clip_limit)), HD, axis=1)
    unit_row = jnp.ones_like(clip_cols[0])
    clip_attention = jnp.stack(
        [clip_cols[0], clip_cols[0], unit_row, unit_row, clip_cols[1], clip_cols[1], unit_row, unit_row]
    )[:, None, :]
    local_cols = lax.dynamic_slice_in_dim(clip_cols, first_col, shard_cols, 1)
    row = lax.broadcasted_iota(jnp.int32, vectors_master.shape, 0)
    clip_vectors = jnp.where(row == 6, local_cols[0:1], jnp.where(row == 9, local_cols[1:2], 1.0))
    step_value = float(ADAM_STEP)
    new_attention = adam_update(
        attention_master, g_attention, attention_first, attention_second, step_value, clip_attention
    )
    new_expand = adam_update(expand_master, g_expand, expand_first, expand_second, step_value, 1.0)
    new_contract = adam_update(contract_master, g_contract, contract_first, contract_second, step_value, 1.0)
    new_vectors = adam_update(vectors_master, g_vectors, vectors_first, vectors_second, step_value, clip_vectors)
    return (
        result,
        grad_input,
        grad_encoder,
        g_attention,
        g_expand,
        g_contract,
        g_vectors,
        new_attention[0],
        new_expand[0],
        new_contract[0],
        new_vectors[0],
        new_attention[1],
        new_expand[1],
        new_contract[1],
        new_vectors[1],
        new_attention[2],
        new_expand[2],
        new_contract[2],
        new_vectors[2],
    )


def solution(mesh):
    planes = mesh.shape["dp"] // 2
    side = math.isqrt(planes)
    if side * side * 2 != mesh.shape["dp"]:
        side = 1
    sizes = (mesh.shape["dp"] // (2 * side), side, 2, mesh.shape["fsdp"])
    fast = sizes == (2, 2, 2, 4)
    mesh = Mesh(mesh.devices.reshape(sizes), ALL)
    shards = (
        P(ALL, None, None),
        P(ALL, None, None),
        P(ALL, None, None),
    )
    weights = (P(None, ALL, None), P(ALL, None), P(ALL, None), P(None, ALL))
    return jax.shard_map(
        functools.partial(local, fast),
        mesh=mesh,
        in_specs=shards + weights * 3,
        out_specs=shards + weights * 4,
        check_vma=False,
    )
```

```python
import functools
import math

import jax
import jax.numpy as jnp
from jax import lax
from jax.experimental import pallas as pl
from jax.experimental.pallas import tpu as pltpu
from jax.sharding import Mesh
from jax.sharding import PartitionSpec as P

HD = 64
ADAM_STEP = 4

eps_norm = 1e-05
clip_limit = 1.0
learn_rate = 0.05
beta_first = 0.9
beta_second = 0.999
eps_adam = 1e-08
weight_decay = 0.1

BF = jnp.bfloat16
F32 = jnp.float32
ALL = ("y", "x", "c", "z")
TILE = 512
KEY_CHUNK = 256
VEC_ROWS = 17
MIB = 1024 * 1024


def dot(left, right):
    return jnp.dot(left, right, preferred_element_type=F32)


def dot_tn(left, right):
    return lax.dot_general(left, right, (((0,), (0,)), ((), ())), preferred_element_type=F32)


def dot_nt(left, right):
    return lax.dot_general(left, right, (((1,), (1,)), ((), ())), preferred_element_type=F32)


def params(limit=60):
    return pltpu.CompilerParams(vmem_limit_bytes=limit * MIB)


def vmem():
    return pl.BlockSpec(memory_space=pltpu.VMEM)


def hbm():
    return pl.BlockSpec(memory_space=pltpu.HBM)


def smem():
    return pl.BlockSpec(memory_space=pltpu.SMEM)


def shape(dims, dtype):
    return jax.ShapeDtypeStruct(tuple(dims), dtype)


def cost(flops, nbytes):
    return pl.CostEstimate(flops=int(flops), bytes_accessed=int(nbytes), transcendentals=0)


class Pack:
    def __init__(self, array, base=0):
        self.array, self.base = array, base


def weight_start(place_ref, pack, row, buf, sem):
    lines = pl.ds(pack.base + row, buf.shape[1])
    pltpu.make_async_copy(pack.array.at[:, lines, :], buf, sem).start()


def call(kernel, packs, args, **settings):
    first, last = len(args), len(args) + len(packs)

    def body(*refs):
        held = [Pack(ref, p.base) for ref, p in zip(refs[first:last], packs)]
        kernel(*refs[:first], *held, *refs[last:])

    specs = settings.pop("in_specs") + [hbm()] * len(packs)
    return pl.pallas_call(body, in_specs=specs, **settings)(*args, *[p.array for p in packs])


def weight_wait(buf, sem):
    pltpu.make_async_copy(buf, buf, sem).wait()


def times(act_ref, buf, put):
    depth = buf.shape[0] * buf.shape[1]

    @pl.loop(0, buf.shape[2] // TILE)
    def _(n):
        start = pl.multiple_of(n * TILE, TILE)
        put(start, dot(act_ref[...], buf[:, :, pl.ds(start, TILE)].reshape(depth, TILE)))


def times_t(act_ref, buf, put):
    per = TILE // buf.shape[1]

    @pl.loop(0, buf.shape[0] // per)
    def _(n):
        start = pl.multiple_of(n * TILE, TILE)
        rows = buf[pl.ds(n * per, per)].reshape(TILE, buf.shape[2])
        put(start, dot_nt(act_ref[...], rows))


def start_all(copies):
    for one in copies:
        one.start()


def wait_all(copies):
    for one in copies:
        one.wait()


def row_chunks(count, size=64):
    return [slice(a, min(a + size, count)) for a in range(0, count, size)]


def normalise(values):
    centered = values - jnp.mean(values, axis=-1, keepdims=True)
    inv = lax.rsqrt(jnp.mean(centered * centered, axis=-1, keepdims=True) + eps_norm)
    return centered * inv, inv


def norm_into(src, gain, shift, out_ref):
    for rows in row_chunks(src.shape[0]):
        normed, _ = normalise(src[rows, :].astype(F32))
        out_ref[rows, :] = (normed * gain + shift).astype(BF)


def norm_grad(src, grad_ref, gain, put):
    gain_sum = jnp.zeros((1, src.shape[1]), F32)
    shift_sum = jnp.zeros((1, src.shape[1]), F32)
    for rows in row_chunks(src.shape[0]):
        normed, inv = normalise(src[rows, :].astype(F32))
        grad = grad_ref[rows, :]
        gain_sum += jnp.sum(grad * normed, axis=0, keepdims=True)
        shift_sum += jnp.sum(grad, axis=0, keepdims=True)
        scaled = grad * gain
        mean_one = jnp.mean(scaled, axis=-1, keepdims=True)
        mean_two = jnp.mean(scaled * normed, axis=-1, keepdims=True)
        put(rows, inv * (scaled - mean_one - normed * mean_two))
    return gain_sum, shift_sum


def column_sum(ref):
    total = jnp.zeros((1, ref.shape[1]), F32)
    for rows in row_chunks(ref.shape[0], 128):
        total += jnp.sum(ref[rows, :].astype(F32), axis=0, keepdims=True)
    return total


def self_in_kernel(place_ref, x_ref, vec_ref, one, two, a_ref, q_ref, k_ref, v_ref, bufs, sems):
    weight_start(place_ref, one, 0, bufs.at[0], sems.at[0])
    weight_start(place_ref, one, 32, bufs.at[1], sems.at[1])
    weight_start(place_ref, two, 0, bufs.at[2], sems.at[2])
    norm_into(x_ref, vec_ref[0:1, :], vec_ref[1:2, :], a_ref)
    for n, (out, bias) in enumerate(((q_ref, 6), (k_ref, None), (v_ref, 7))):
        weight_wait(bufs.at[n], sems.at[n])

        def put(start, value, out=out, bias=bias):
            if bias is not None:
                value = value + vec_ref[bias : bias + 1, pl.ds(start, TILE)]
            out[:, pl.ds(start, TILE)] = value.astype(BF)

        times(a_ref, bufs.at[n], put)


def self_in(place, x, vec, packs):
    rows, width = x.shape
    full = shape((rows, width), BF)
    return call(
        self_in_kernel,
        packs,
        [place, x, vec],
        out_shape=[full] * 4,
        in_specs=[smem(), vmem(), vmem()],
        out_specs=[vmem()] * 4,
        scratch_shapes=[pltpu.VMEM((3, 32, 32, width), BF), pltpu.SemaphoreType.DMA((3,))],
        compiler_params=params(48),
        cost_estimate=cost(6 * rows * width * width, 10 * MIB),
        name="self_in",
    )


def masked_pair(value):
    lane = lax.broadcasted_iota(jnp.int32, value.shape, 1)
    zero = jnp.zeros_like(value)
    return jnp.concatenate([jnp.where(lane < HD, value, zero), jnp.where(lane < HD, zero, value)], axis=0)


def pair_back(both, rows):
    line = lax.broadcasted_iota(jnp.int32, (2 * HD, rows), 0)
    return jnp.where(line < HD, both[:, :rows], both[:, rows:]).T


def key_chunks(count):
    return [(a, min(a + KEY_CHUNK, count)) for a in range(0, count, KEY_CHUNK)]


def exclude(scores, start, rows, causal, valid):
    key = lax.broadcasted_iota(jnp.int32, scores.shape, 0) + start
    if causal:
        query = lax.broadcasted_iota(jnp.int32, scores.shape, 1)
        query = jnp.where(query >= rows, query - rows, query)
        return jnp.where(key <= query, scores, -1e30)
    if start + scores.shape[0] > valid:
        return jnp.where(key < valid, scores, -1e30)
    return scores


def attend_kernel(causal, valid, q_ref, k_ref, v_ref, o_ref, lse_ref, top_ref, held):
    rows = q_ref.shape[0]
    query = masked_pair(q_ref[...] * jnp.asarray(HD**-0.5, BF))
    top = jnp.full((1, 2 * rows), -1e30, F32)
    for a, b in key_chunks(k_ref.shape[0]):
        scores = exclude(dot_nt(k_ref[a:b, :], query), a, rows, causal, valid)
        held[a:b, :] = scores
        top = jnp.maximum(top, jnp.max(scores, axis=0, keepdims=True))
    total = jnp.zeros((1, 2 * rows), F32)
    mixed = jnp.zeros((2 * HD, 2 * rows), F32)
    for a, b in key_chunks(k_ref.shape[0]):
        probs = jnp.exp(held[a:b, :] - top)
        total += jnp.sum(probs, axis=0, keepdims=True)
        mixed += dot_tn(v_ref[a:b, :], probs.astype(BF))
    o_ref[...] = pair_back(mixed * (1.0 / total), rows).astype(BF)
    lane = lax.broadcasted_iota(jnp.int32, (1, 2 * HD), 1)
    first, second = (jnp.max(part, axis=1, keepdims=True) for part in (top[:, :rows], top[:, rows:]))
    top_ref[0] = jnp.where(lane == 0, first, second)
    lse_ref[0] = top + jnp.log(total)


def attend(query, key, value, causal, valid):
    rows, width = query.shape
    keys = key.shape[0]
    pairs = width // (2 * HD)

    def column(count):
        return pl.BlockSpec((count, 2 * HD), lambda h: (0, h))

    line = pl.BlockSpec((1, 1, 2 * rows), lambda h: (h, 0, 0))
    return pl.pallas_call(
        functools.partial(attend_kernel, causal, valid),
        grid=(pairs,),
        out_shape=[shape((rows, width), BF), shape((pairs, 1, 2 * rows), F32), shape((pairs, 1, 2 * HD), F32)],
        in_specs=[column(rows), column(keys), column(keys)],
        out_specs=[column(rows), line, pl.BlockSpec((1, 1, 2 * HD), lambda h: (h, 0, 0))],
        scratch_shapes=[pltpu.VMEM((keys, 2 * rows), F32)],
        compiler_params=params(48),
        cost_estimate=cost(16 * rows * keys * width, 4 * keys * width),
        name="attend_causal" if causal else "attend",
    )(query, key, value)


def self_out_kernel(place_ref, o_ref, x_ref, vec_ref, one, two, x1_ref, a_ref, q_ref, bufs, sems):
    weight_start(place_ref, two, 32, bufs.at[0], sems.at[0])
    weight_start(place_ref, one, 32, bufs.at[1], sems.at[1])
    weight_wait(bufs.at[0], sems.at[0])

    def put_residual(start, value):
        cols = pl.ds(start, TILE)
        x1_ref[:, cols] = x_ref[:, cols].astype(F32) + (value + vec_ref[8:9, cols])

    times(o_ref, bufs.at[0], put_residual)
    norm_into(x1_ref, vec_ref[2:3, :], vec_ref[3:4, :], a_ref)
    weight_wait(bufs.at[1], sems.at[1])

    def put_query(start, value):
        cols = pl.ds(start, TILE)
        q_ref[:, cols] = (value + vec_ref[9:10, cols]).astype(BF)

    times(a_ref, bufs.at[1], put_query)


def self_out(place, mixed, x, vec, packs):
    rows, width = x.shape
    return call(
        self_out_kernel,
        packs,
        [place, mixed, x, vec],
        out_shape=[shape((rows, width), F32), shape((rows, width), BF), shape((rows, width), BF)],
        in_specs=[smem()] + [vmem()] * 3,
        out_specs=[vmem()] * 3,
        scratch_shapes=[pltpu.VMEM((2, 32, 32, width), BF), pltpu.SemaphoreType.DMA((2,))],
        compiler_params=params(48),
        cost_estimate=cost(4 * rows * width * width, 10 * MIB),
        name="self_out",
    )


def cross_in_kernel(place_ref, e_ref, vec_ref, one, two, k_ref, v_ref, bufs, sems):
    for n, part in enumerate((one, two)):
        weight_start(place_ref, part, 0, bufs.at[n], sems.at[n])
    for n, (out, bias) in enumerate(((k_ref, None), (v_ref, 10))):
        weight_wait(bufs.at[n], sems.at[n])

        def put(start, value, out=out, bias=bias):
            if bias is not None:
                value = value + vec_ref[bias : bias + 1, pl.ds(start, TILE)]
            out[:, pl.ds(start, TILE)] = value.astype(BF)

        times(e_ref, bufs.at[n], put)


def cross_in(place, enc, vec, packs):
    frames, width = enc.shape
    return call(
        cross_in_kernel,
        packs,
        [place, enc, vec],
        out_shape=[shape((frames, width), BF)] * 2,
        in_specs=[smem()] + [vmem()] * 2,
        out_specs=[vmem()] * 2,
        scratch_shapes=[pltpu.VMEM((2, 32, 32, width), BF), pltpu.SemaphoreType.DMA((2,))],
        compiler_params=params(48),
        cost_estimate=cost(4 * frames * width * width, 14 * MIB),
        name="cross_in",
    )


def cross_out_kernel(place_ref, o_ref, x1_ref, vec_ref, two, x2_ref, a_ref, buf, sem):
    weight_start(place_ref, two, 32, buf, sem)
    weight_wait(buf, sem)

    def put(start, value):
        cols = pl.ds(start, TILE)
        x2_ref[:, cols] = x1_ref[:, cols] + (value + vec_ref[11:12, cols])

    times(o_ref, buf, put)
    norm_into(x2_ref, vec_ref[4:5, :], vec_ref[5:6, :], a_ref)


def cross_out(place, mixed, x1, vec, packs):
    rows, width = x1.shape
    return call(
        cross_out_kernel,
        packs,
        [place, mixed, x1, vec],
        out_shape=[shape((rows, width), F32), shape((rows, width), BF)],
        in_specs=[smem()] + [vmem()] * 3,
        out_specs=[vmem()] * 2,
        scratch_shapes=[pltpu.VMEM((32, 32, width), BF), pltpu.SemaphoreType.DMA],
        compiler_params=params(48),
        cost_estimate=cost(2 * rows * width * width, 8 * MIB),
        name="cross_out",
    )


def whole(dims):
    return pl.BlockSpec(dims, lambda n: (0,) * len(dims))


def feed_kernel(
    a_ref, x2_ref, e_ref, vec_ref, bias_ref, w1_ref, w2_ref, out_ref, df_ref, gb1_ref, gb2_ref, grad_ref, total
):
    step = pl.program_id(0)
    wide = w1_ref.shape[2]
    depth = a_ref.shape[1]

    @pl.when(step == 0)
    def _():
        total[...] = x2_ref[...] + vec_ref[12:13, :]
        gb2_ref[...] = column_sum(e_ref)

    w2 = w2_ref[...].reshape(wide, depth)
    pre = dot(a_ref[...], w1_ref[...].reshape(depth, wide)) + bias_ref[0]
    cdf = 0.5 * (1.0 + lax.erf(pre * math.sqrt(0.5)))
    act = (pre * cdf).astype(BF)
    slope = cdf + pre * (jnp.exp(-0.5 * (pre * pre)) * (1.0 / math.sqrt(2.0 * math.pi)))
    grad_ref[0] = dot_tn(act, e_ref[...]).astype(BF).reshape(grad_ref.shape[1:])
    grad_pre = (dot_nt(e_ref[...], w2) * slope).astype(BF)
    df_ref[...] = grad_pre
    gb1_ref[0] = jnp.sum(grad_pre.astype(F32), axis=0, keepdims=True)
    total[...] += dot(act, w2)

    @pl.when(step == pl.num_programs(0) - 1)
    def _():
        out_ref[...] = total[...].astype(BF)


def feed(a3, x2, cot, vec, pack):
    rows, width = a3.shape
    hidden = 4 * width
    wide = hidden // 8
    bias = vec[13:].reshape(8, 1, wide)
    return pl.pallas_call(
        feed_kernel,
        grid=(8,),
        out_shape=[
            shape((rows, width), BF), shape((rows, hidden), BF), shape((8, 1, wide), F32), shape((1, width), F32),
            shape((8, 4, 128, width), BF),
        ],
        in_specs=[
            whole((rows, width)),
            whole((rows, width)),
            whole((rows, width)),
            whole(vec.shape),
            pl.BlockSpec((1, 1, wide), lambda n: (n, 0, 0)),
            pl.BlockSpec((32, 32, wide), lambda n: (0, n // 2, n % 2)),
            pl.BlockSpec((4, 128, width), lambda n: (n, 1, 0)),
        ],
        out_specs=[
            whole((rows, width)),
            pl.BlockSpec((rows, wide), lambda n: (0, n)),
            pl.BlockSpec((1, 1, wide), lambda n: (n, 0, 0)),
            whole((1, width)),
            pl.BlockSpec((1, 4, 128, width), lambda n: (n, 0, 0, 0)),
        ],
        scratch_shapes=[pltpu.VMEM((rows, width), F32)],
        compiler_params=params(),
        cost_estimate=cost(8 * rows * width * hidden, 30 * MIB),
        name="feed",
    )(a3, x2, cot, vec, bias, pack, pack)


def feed_grad_kernel(df_ref, w1_ref, da_ref):
    @pl.when(pl.program_id(0) == 0)
    def _():
        da_ref[...] = jnp.zeros_like(da_ref)

    da_ref[...] += dot_nt(df_ref[...], w1_ref[...].reshape(da_ref.shape[1], w1_ref.shape[2]))


def feed_grad(df, pack):
    rows, hidden = df.shape
    width = pack.shape[2]
    return pl.pallas_call(
        feed_grad_kernel,
        grid=(hidden // width,),
        out_shape=shape((rows, width), F32),
        in_specs=[
            pl.BlockSpec((rows, width), lambda n: (0, n)),
            pl.BlockSpec((32, 32, width), lambda n: (0, n, 0)),
        ],
        out_specs=whole((rows, width)),
        compiler_params=params(),
        cost_estimate=cost(2 * rows * width * hidden, 12 * MIB),
        name="feed_grad",
    )(df, pack)


def cross_out_grad_kernel(place_ref, da_ref, x2_ref, cot_ref, vec_ref, two, dx_ref, do_ref, e_ref, sums_ref, buf, sem):
    weight_start(place_ref, two, 32, buf, sem)

    def put(rows, value):
        total = cot_ref[rows, :].astype(F32) + value
        dx_ref[rows, :] = total
        e_ref[rows, :] = total.astype(BF)

    gain, shift = norm_grad(x2_ref, da_ref, vec_ref[4:5, :], put)
    sums_ref[0:1, :] = gain
    sums_ref[1:2, :] = shift
    sums_ref[2:3, :] = column_sum(e_ref)
    weight_wait(buf, sem)

    def put_mixed(start, value):
        do_ref[:, pl.ds(start, TILE)] = value.astype(BF)

    times_t(e_ref, buf, put_mixed)


def cross_out_grad(place, da3, x2, cot, vec, packs):
    rows, width = x2.shape
    low = shape((rows, width), BF)
    return call(
        cross_out_grad_kernel,
        packs,
        [place, da3, x2, cot, vec],
        out_shape=[shape((rows, width), F32), low, low, shape((3, width), F32)],
        in_specs=[smem()] + [vmem()] * 4,
        out_specs=[vmem()] * 4,
        scratch_shapes=[pltpu.VMEM((32, 32, width), BF), pltpu.SemaphoreType.DMA],
        compiler_params=params(),
        cost_estimate=cost(2 * rows * width * width, 10 * MIB),
        name="cross_out_grad",
    )


def attend_grad_kernel(
    causal, valid, q_ref, k_ref, v_ref, o_ref, do_ref, lse_ref, dq_ref, dk_ref, dv_ref, sums_ref
):
    rows = q_ref.shape[0]
    scale = jnp.asarray(HD**-0.5, BF)
    query = masked_pair(q_ref[...] * scale)
    grad_out = masked_pair(do_ref[...])
    product = (do_ref[...].astype(F32) * o_ref[...].astype(F32)).T
    delta = jnp.concatenate(
        [jnp.sum(product[:HD], axis=0, keepdims=True), jnp.sum(product[HD:], axis=0, keepdims=True)], axis=1
    )
    lse = lse_ref[0]
    grad_query = jnp.zeros((2 * HD, 2 * rows), F32)
    value_sum = jnp.zeros((1, 2 * HD), F32)
    for a, b in key_chunks(k_ref.shape[0]):
        key = k_ref[a:b, :]
        scores = exclude(dot_nt(key, query), a, rows, causal, valid)
        probs = jnp.exp(scores - lse)
        grad_probs = dot_nt(v_ref[a:b, :], grad_out)
        grad_scores = (probs * (grad_probs - delta)).astype(BF)
        grad_value = dot(probs.astype(BF), grad_out).astype(BF)
        dv_ref[a:b, :] = grad_value
        value_sum += jnp.sum(grad_value.astype(F32), axis=0, keepdims=True)
        dk_ref[a:b, :] = dot(grad_scores, query).astype(BF)
        grad_query += dot_tn(key, grad_scores)
    grad_query = (pair_back(grad_query, rows) * HD**-0.5).astype(BF)
    dq_ref[...] = grad_query
    sums_ref[0:1, :] = jnp.sum(grad_query.astype(F32), axis=0, keepdims=True)
    sums_ref[1:2, :] = value_sum


def attend_grad(query, key, value, mixed, grad_mixed, lse, causal, valid):
    rows, width = query.shape
    keys = key.shape[0]
    pairs = width // (2 * HD)

    def column(count):
        return pl.BlockSpec((count, 2 * HD), lambda h: (0, h))

    line = pl.BlockSpec((1, 1, 2 * rows), lambda h: (h, 0, 0))
    return pl.pallas_call(
        functools.partial(attend_grad_kernel, causal, valid),
        grid=(pairs,),
        out_shape=[shape((rows, width), BF)] + [shape((keys, width), BF)] * 2 + [shape((2, width), F32)],
        in_specs=[column(rows), column(keys), column(keys), column(rows), column(rows), line],
        out_specs=[column(rows), column(keys), column(keys), column(2)],
        compiler_params=params(),
        cost_estimate=cost(40 * rows * keys * width, 8 * keys * width),
        name="attend_causal_grad" if causal else "attend_grad",
    )(query, key, value, mixed, grad_mixed, lse)


def cross_query_grad_kernel(
    place_ref, dq_ref, x1_ref, dx2_ref, vec_ref, one, two, dx_ref, do_ref, e_ref, sums_ref, bufs, da_ref, sem
):
    for n, part in enumerate((one, two)):
        weight_start(place_ref, part, 32, bufs.at[n], sem.at[n])
    weight_wait(bufs.at[0], sem.at[0])

    def put_act(start, value):
        da_ref[:, pl.ds(start, TILE)] = value

    times_t(dq_ref, bufs.at[0], put_act)

    def put(rows, value):
        total = dx2_ref[rows, :] + value
        dx_ref[rows, :] = total
        e_ref[rows, :] = total.astype(BF)

    gain, shift = norm_grad(x1_ref, da_ref, vec_ref[2:3, :], put)
    sums_ref[0:1, :] = gain
    sums_ref[1:2, :] = shift
    sums_ref[2:3, :] = column_sum(e_ref)
    weight_wait(bufs.at[1], sem.at[1])

    def put_mixed(start, value):
        do_ref[:, pl.ds(start, TILE)] = value.astype(BF)

    times_t(e_ref, bufs.at[1], put_mixed)


def cross_query_grad(place, dq2, x1, dx2, vec, packs):
    rows, width = x1.shape
    low = shape((rows, width), BF)
    return call(
        cross_query_grad_kernel,
        packs,
        [place, dq2, x1, dx2, vec],
        out_shape=[shape((rows, width), F32), low, low, shape((3, width), F32)],
        in_specs=[smem()] + [vmem()] * 4,
        out_specs=[vmem()] * 4,
        scratch_shapes=[
            pltpu.VMEM((2, 32, 32, width), BF), pltpu.VMEM((rows, width), F32), pltpu.SemaphoreType.DMA((2,)),
        ],
        compiler_params=params(),
        cost_estimate=cost(4 * rows * width * width, 14 * MIB),
        name="cross_query_grad",
    )


def weight_grads_kernel(jobs, lefts, rights, place_ref, *refs):
    count = 2 * (lefts + rights)
    one_away, two_away, one_mine, two_mine = refs[count : count + 4]
    held, (grads, in_sems, sems) = refs[count + 4 : 2 * count + 4], refs[2 * count + 4 :]
    order = []
    for left, right, _ in jobs:
        order += [n for n in (2 * left, 2 * (lefts + right), 2 * left + 1, 2 * (lefts + right) + 1) if n not in order]
    pending = {n: pltpu.make_async_copy(refs[n], held[n], in_sems.at[n]) for n in order}
    start_all(pending.values())

    def ready(n):
        if n in pending:
            pending.pop(n).wait()
        return held[n]

    core = jnp.bitwise_and(place_ref[0], 1)
    plane = lax.shift_right_logical(place_ref[0], 1)
    split = len(jobs) // 2
    width = one_mine.shape[3]
    copies = []
    for pair in ((3, 1), (2, 0)):
        starts = [pl.multiple_of((jnp.bitwise_xor(plane, j) * 2 + core) * 128, 128) for j in pair]
        turned = {}
        for k, (left, right, block) in enumerate(jobs):
            wide = slice(block * width, (block + 1) * width)
            total = None
            for side in range(2):
                act, grad = ready(2 * left + side), ready(2 * (lefts + right) + side)
                if (left, side) not in turned:
                    columns = jnp.concatenate([act[:, pl.ds(start, 128)] for start in starts], axis=1)
                    turned[left, side] = columns.T
                value = dot(turned[left, side], grad[:, wide])
                total = value if total is None else total + value
            rounded = total.astype(BF).reshape((2,) + grads.shape[2:])
            lines = pl.ds(32 * (k % split), 32)
            for n, j in enumerate(pair):
                grads[k, j] = rounded[n]
                y, x = j // 2, j % 2
                if k < split:
                    target = (one_away if x else one_mine).at[y, :, lines, :]
                else:
                    target = (two_away if y else two_mine).at[x, :, lines, :]
                copies.append(pltpu.make_async_copy(grads.at[k, j], target, sems.at[k, j]))
                copies[-1].start()
    wait_all(copies)


def weight_grads(place, lefts, rights, jobs):
    width = lefts[0][0].shape[1]
    count = len(jobs)
    blocks = shape((2, 4, 16 * count, width), BF)
    operands = [value for pair in lefts + rights for value in pair]
    flops = sum(4 * lefts[left][0].shape[0] * width * width // 2 for left, _, _ in jobs)
    return pl.pallas_call(
        functools.partial(weight_grads_kernel, jobs, len(lefts), len(rights)),
        out_shape=[blocks] * 4,
        in_specs=[smem()] + [hbm()] * len(operands),
        out_specs=[hbm()] * 4,
        scratch_shapes=[pltpu.VMEM(value.shape, BF) for value in operands] + [
            pltpu.VMEM((count, 4, 4, 32, width), BF), pltpu.SemaphoreType.DMA((len(operands),)),
            pltpu.SemaphoreType.DMA((count, 4)),
        ],
        compiler_params=params(),
        cost_estimate=cost(flops, 12 * MIB),
        name="weight_grads",
    )(place, *operands)


def encoder_grad_kernel(frames, place_ref, dk_ref, dv_ref, one, two, out_ref, bufs, sems):
    for n, part in enumerate((one, two)):
        weight_start(place_ref, part, 0, bufs.at[n], sems.at[n])
    for n in range(2):
        weight_wait(bufs.at[n], sems.at[n])
    width = dk_ref.shape[1]
    per = TILE // 32
    lines = width // 128

    @pl.loop(0, width // TILE)
    def _(n):
        total = dot_nt(dk_ref[...], bufs[0, pl.ds(n * per, per)].reshape(TILE, width))
        total += dot_nt(dv_ref[...], bufs[1, pl.ds(n * per, per)].reshape(TILE, width))
        for side in range(TILE // 128):
            start = n * (TILE // 128) + side
            out_ref[pl.ds(start, frames, stride=lines), :] = total[:frames, side * 128 : (side + 1) * 128]


def encoder_grad(place, dk2, dv2, packs, frames):
    width = dk2.shape[1]
    return call(
        functools.partial(encoder_grad_kernel, frames),
        packs,
        [place, dk2, dv2],
        out_shape=shape((frames * (width // 128), 128), F32),
        in_specs=[smem()] + [vmem()] * 2,
        out_specs=vmem(),
        scratch_shapes=[pltpu.VMEM((2, 32, 32, width), BF), pltpu.SemaphoreType.DMA((2,))],
        compiler_params=params(),
        cost_estimate=cost(4 * frames * width * width, 16 * MIB),
        name="encoder_grad",
    )


def self_in_grad_kernel(
    place_ref, dq_ref, dk_ref, dv_ref, x_ref, dx1_ref, vec_ref, one, two, dx_ref, sums_ref, bufs, da_ref, sems
):
    weight_start(place_ref, one, 0, bufs.at[0], sems.at[0])
    weight_start(place_ref, one, 32, bufs.at[1], sems.at[1])
    weight_start(place_ref, two, 0, bufs.at[2], sems.at[2])
    for n, ref in enumerate((dq_ref, dk_ref, dv_ref)):
        weight_wait(bufs.at[n], sems.at[n])

        def put_act(start, value, n=n):
            if n:
                da_ref[:, pl.ds(start, TILE)] += value
            else:
                da_ref[:, pl.ds(start, TILE)] = value

        times_t(ref, bufs.at[n], put_act)

    def put(rows, value):
        dx_ref[rows, :] = dx1_ref[rows, :] + value

    gain, shift = norm_grad(x_ref, da_ref, vec_ref[0:1, :], put)
    sums_ref[0:1, :] = gain
    sums_ref[1:2, :] = shift


def self_in_grad(place, dq1, dk1, dv1, x, dx1, vec, packs):
    rows, width = x.shape
    return call(
        self_in_grad_kernel,
        packs,
        [place, dq1, dk1, dv1, x, dx1, vec],
        out_shape=[shape((rows, width), F32), shape((2, width), F32)],
        in_specs=[smem()] + [vmem()] * 6,
        out_specs=[vmem()] * 2,
        scratch_shapes=[
            pltpu.VMEM((3, 32, 32, width), BF), pltpu.VMEM((rows, width), F32), pltpu.SemaphoreType.DMA((3,)),
        ],
        compiler_params=params(),
        cost_estimate=cost(6 * rows * width * width, 14 * MIB),
        name="self_in_grad",
    )


SWAP = [(0, 1), (1, 0)]
MATRICES = ((0, 1), (2, 3), (5, 4), (6, 7))


class Unit:
    def __init__(self, chain):
        self.chain, self.result, self.moved = chain, None, None
        self.wanted = next(chain)

    def advance(self, arrived):
        try:
            self.wanted = self.chain.send(arrived)
        except StopIteration as stop:
            self.wanted, self.result = None, stop.value


def step(run=None, inputs=(), start=(), finish=()):
    start, finish = ([u for u in units if u is not None] for units in (start, finish))
    operands = [[value for value, _, _ in u.wanted] for u in start]
    inputs, operands = lax.optimization_barrier((tuple(inputs), operands))
    for u, values in zip(start, operands):
        u.moved = [lax.ppermute(v, axis, pairs) for v, (_, axis, pairs) in zip(values, u.wanted)]
    out = run(*inputs) if run else ()
    if finish:
        out, moved = lax.optimization_barrier((out, [u.moved for u in finish]))
        for u, values in zip(finish, moved):
            u.advance(values)
    return out


def turns():
    return [[(n, (n + k) % 4) for n in range(4)] for k in range(4)]


def add_rounded(left, right):
    return (left.astype(F32) + right.astype(F32)).astype(BF)


def add_kernel(plan, sources, place_ref, *refs):
    left, right = refs[:sources], refs[sources : 2 * sources]
    *outs, one, two, total, sems, out_sems = refs[2 * sources :]
    pieces = plan(place_ref)
    copies = [
        [
            pltpu.make_async_copy(side[source].at[index], held.at[n], sems.at[k, n])
            for k, (side, held) in enumerate(((left, one), (right, two)))
        ]
        for n, (source, index, _, _) in enumerate(pieces)
    ]
    for pair in copies:
        start_all(pair)
    away = []
    for n, (_, _, out, index) in enumerate(pieces):
        wait_all(copies[n])
        total[n] = add_rounded(one[n], two[n])
        away.append(pltpu.make_async_copy(total.at[n], outs[out].at[index], out_sems.at[n]))
        away[-1].start()
    wait_all(away)


def add_pieces(place, left, right, outs, piece, plan, count):
    held = pltpu.VMEM((count,) + piece, BF)
    return pl.pallas_call(
        functools.partial(add_kernel, plan, len(left)),
        out_shape=[shape(o, BF) for o in outs],
        in_specs=[smem()] + [hbm()] * (2 * len(left)),
        out_specs=[hbm()] * len(outs),
        scratch_shapes=[
            held, held, held, pltpu.SemaphoreType.DMA((2, count)), pltpu.SemaphoreType.DMA((count,)),
        ],
        compiler_params=params(),
        cost_estimate=cost(0, 6 * count * math.prod(piece)),
        name="add_pieces",
    )(place, *left, *right)


def turn_z(place_ref, k):
    return jnp.bitwise_and(place_ref[1] + k, 3)


def swap_chain(values):
    moved = yield [(value, "c", SWAP) for value in values]
    return list(zip(values, moved))


NEAR = [(0, 1), (1, 0), (2, 3), (3, 2)]
FAR = [(0, 2), (2, 0), (1, 3), (3, 1)]


def pick_z(both, k):
    return lax.dynamic_index_in_dim(both, jnp.bitwise_xor(lax.axis_index("z"), k), 0, keepdims=False)


def z_halves(both):
    away, mine = (jnp.stack([pick_z(both, k), pick_z(both, k ^ 2)]) for k in (1, 0))
    return (yield from z_two(away, mine))


def z_two(away, mine):
    (moved,) = yield [(away, "z", NEAR)]
    near = mine[0].astype(F32) + moved[0].astype(F32)
    (moved,) = yield [(add_rounded(mine[1], moved[1]), "z", FAR)]
    return near + moved.astype(F32)


def reduce_chain(place, halving, one, two, *mine):
    half, columns = one.shape[2:]
    rows = 2 * half
    parts = [pl.ds(0, half), pl.ds(half, half)]
    moved = yield [(one, "x", SWAP), (two, "y", SWAP)]

    def plan_two(_):
        return [(n, side, n if side else 2 + n, slice(None)) for side in (1, 0) for n in range(2)]

    outs = [(4, half, columns)] * 4
    one, two, *mine = add_pieces(place, list(mine), list(moved), outs, (4, half, columns), plan_two, 4)
    moved = yield [(one, "y", SWAP), (two, "x", SWAP)]

    if halving:

        def plan_halves(place_ref):
            turns = [(1, 0, 0), (3, 0, 1), (2, 1, 1), (0, 1, 0)]
            return [
                (n, jnp.bitwise_xor(place_ref[1], turn), out, (at, parts[n])) for turn, out, at in turns for n in range(2)
            ]

        outs = [(2, rows, columns)] * 2
        return (yield from z_two(*add_pieces(place, mine, list(moved), outs, (half, columns), plan_halves, 8)))

    def plan_three(place_ref):
        return [(n, turn_z(place_ref, k), k, parts[n]) for k in (2, 1, 3, 0) for n in range(2)]

    pieces = add_pieces(place, mine, list(moved), [(rows, columns)] * 4, (half, columns), plan_three, 8)
    moved = yield [(pieces[k], "z", turns()[k]) for k in (1, 3, 2)]
    return functools.reduce(jnp.add, [value.astype(F32) for value in moved], pieces[0].astype(F32))


def reduce_feed_plain(grad1, grad2):
    grad2 = grad2.reshape(-1, grad2.shape[3])
    return [lax.psum_scatter(g, ALL, scatter_dimension=0, tiled=True) for g in (grad1, grad2)]


def table_chain(table):
    row = lax.broadcasted_iota(jnp.int32, table.shape, 0)

    def combine(left, right):
        return jnp.where(row < VEC_ROWS, left + right, jnp.maximum(left, right))

    for axis in ("c", "x", "y"):
        moved = yield [(table, axis, SWAP)]
        table = combine(table, moved[0])
    moved = yield [(table, "z", turns()[k]) for k in (1, 3, 2)]
    return functools.reduce(combine, moved, table)


def vector_table(pack, row, rows, shard_cols):
    table = pack[:, row, : rows * shard_cols].reshape(32, rows, shard_cols).swapaxes(0, 1)
    return table.reshape(rows, 32 * shard_cols).astype(F32)


def feed_shard(expand, contract):
    width = contract.shape[1]
    pieces = [expand[:, n * width : (n + 1) * width] for n in range(expand.shape[1] // width)]
    return jnp.concatenate(pieces + [contract], axis=0)


def gather_fast(attention, expand, contract, vectors):
    width = attention.shape[2]
    line = jnp.pad(vectors.reshape(1, -1), ((0, 7), (0, width - vectors.size)))
    shard = jnp.concatenate([attention[m] for group in MATRICES for m in group] + [line], axis=0)
    pack = lax.all_gather(shard, ALL, axis=0, tiled=False)
    pack_f = lax.all_gather(feed_shard(expand, contract), ALL, axis=0, tiled=False)
    return parts_of(pack), pack_f, vector_table(pack, 256, *vectors.shape)


def parts_of(pack):
    return [Pack(pack, 64 * n) for n in range(4)]


def gather_plain(attention, expand, contract, vectors):
    attention = lax.all_gather(attention, ALL, axis=1, tiled=True)
    expand = lax.all_gather(expand, ALL, axis=0, tiled=True)
    contract = lax.all_gather(contract, ALL, axis=0, tiled=True)
    vectors = lax.all_gather(vectors, ALL, axis=1, tiled=True)
    width = attention.shape[2]
    pack = jnp.concatenate([attention[m].reshape(32, 32, width) for group in MATRICES for m in group], axis=1)
    first = expand.reshape(32, 32, 4, width).swapaxes(1, 2).reshape(32, 128, width)
    pack_f = jnp.concatenate([first, contract.reshape(32, 128, width)], axis=1)
    return parts_of(pack), pack_f, vectors.astype(F32)


def adam_update(master, gradient, first, second, step_value, clip_scale):
    first_new = beta_first * first.astype(F32) + (1.0 - beta_first) * gradient
    second_new = beta_second * second + (1.0 - beta_second) * gradient * gradient
    direction = (
        first_new
        / (1.0 - beta_first**step_value)
        / (jnp.sqrt(second_new / (1.0 - beta_second**step_value)) + eps_adam)
    )
    master_new = (master - learn_rate * (direction + weight_decay * master)) * clip_scale
    return (first_new, second_new, master_new)


def table_kernel(sums1, bias1, sums2, bias2, sums3, gb1, gb2, top1, top2, out):
    out[...] = jnp.zeros_like(out)
    rows = [
        sums1[0:1, :], sums1[1:2, :], sums2[0:1, :], sums2[1:2, :], sums3[0:1, :], sums3[1:2, :],
        bias1[0:1, :], bias1[1:2, :], sums2[2:3, :], bias2[0:1, :], bias2[1:2, :], sums3[2:3, :], gb2[...],
    ]
    for n, row in enumerate(rows):
        out[n : n + 1, :] = row
    half = gb1.shape[2]
    for n in range(gb1.shape[0]):
        out[len(rows) + n // 2 : len(rows) + n // 2 + 1, n % 2 * half : (n % 2 + 1) * half] = gb1[n]
    for n, top in enumerate((top1, top2)):
        for pair in range(top.shape[0]):
            lanes = slice(pair * 2 * HD, (pair + 1) * 2 * HD)
            out[VEC_ROWS + n : VEC_ROWS + n + 1, lanes] = top[pair]


def vector_table_of(*pieces):
    width = pieces[0].shape[1]
    return pl.pallas_call(
        table_kernel,
        out_shape=shape((24, width), F32),
        in_specs=[vmem()] * len(pieces),
        out_specs=vmem(),
        compiler_params=params(),
        cost_estimate=cost(0, 200000),
        name="vector_table",
    )(*pieces)


def maxima_of(table):
    return table[VEC_ROWS : VEC_ROWS + 2].reshape(2, -1, 2 * HD)[:, :, :2].reshape(2, -1)


def sequence_plain(place, x, enc, frames, cot, vec, packs, pack_f):
    rows, width = x.shape
    one_a, one_b, two_a, two_b = packs
    a1, q1, k1, v1 = self_in(place, x, vec, [one_a, one_b])
    o1, lse1, top1 = attend(q1, k1, v1, True, rows)
    x1, a2, q2 = self_out(place, o1, x, vec, [two_a, one_b])
    k2, v2 = cross_in(place, enc, vec, [two_a, two_b])
    o2, lse2, top2 = attend(q2, k2, v2, False, frames)
    x2, a3 = cross_out(place, o2, x1, vec, [two_b])
    result, df, gb1, gb2, grad2 = feed(a3, x2, cot, vec, pack_f)
    da3 = feed_grad(df, pack_f)
    dx2, do2, e2, sums3 = cross_out_grad(place, da3, x2, cot, vec, [two_b])
    dq2, dk2, dv2, bias2 = attend_grad(q2, k2, v2, o2, do2, lse2, False, frames)
    dx1, do1, e1, sums2 = cross_query_grad(place, dq2, x1, dx2, vec, [two_a, one_b])
    dq1, dk1, dv1, bias1 = attend_grad(q1, k1, v1, o1, do1, lse1, True, rows)
    grad_input, sums1 = self_in_grad(place, dq1, dk1, dv1, x, dx1, vec, [one_a, one_b])
    grad_encoder = encoder_grad(place, dk2, dv2, [two_a, two_b], frames).reshape(frames, width)
    table = vector_table_of(sums1, bias1, sums2, bias2, sums3, gb1, gb2, top1, top2)
    pairs = ((a1, dq1), (a1, dk1), (a1, dv1), (o1, e1), (a2, dq2), (enc, dk2), (enc, dv2), (o2, e2))
    g_attention = jnp.stack([dot_tn(left, right) for left, right in pairs])
    sums = [dot_tn(a3, df), grad2.astype(F32), g_attention]
    return result, grad_input, grad_encoder, table[:VEC_ROWS], maxima_of(table), sums


def gradients_plain(inputs, encoder, cotangent, owned):
    packs, pack_f, vec = gather_plain(*owned)
    place = jnp.zeros((2,), jnp.int32)
    frames = encoder.shape[1]
    done = []
    for n in range(inputs.shape[0]):
        enc = pad_frames(encoder[n])
        done.append(sequence_plain(place, inputs[n], enc, frames, cotangent[n], vec, packs, pack_f))
    result, grad_input, grad_encoder = (jnp.stack([d[k] for d in done]) for k in range(3))
    g_vectors = functools.reduce(jnp.add, [d[3] for d in done])
    maxima = functools.reduce(jnp.maximum, [d[4] for d in done])
    grad1, grad2, g_attention = (functools.reduce(jnp.add, values) for values in zip(*[d[5] for d in done]))
    sums = reduce_feed_plain(grad1, grad2) + [lax.psum_scatter(g_attention, ALL, scatter_dimension=1, tiled=True)]
    g_vectors = lax.psum_scatter(g_vectors, ALL, scatter_dimension=1, tiled=True)
    return result, grad_input, grad_encoder, sums, g_vectors, lax.pmax(maxima, ALL)


def pad_frames(enc):
    return jnp.pad(enc, ((0, -enc.shape[0] % 16), (0, 0)))


def gradients_fast(inputs, encoder, cotangent, owned):
    attention, expand, contract, vectors = owned
    x, cot = inputs[0], cotangent[0]
    rows, width = x.shape
    frames = encoder.shape[1]
    place = jnp.stack([lax.axis_index(("y", "x", "c")), lax.axis_index("z")]).astype(jnp.int32)
    (one_a, one_b, two_a, two_b), pack_f, vec = gather_fast(*owned)
    enc = pad_frames(encoder[0])
    a1, q1, k1, v1 = self_in(place, x, vec, [one_a, one_b])
    o1, lse1, top1 = attend(q1, k1, v1, True, rows)
    x1, a2, q2 = self_out(place, o1, x, vec, [two_a, one_b])
    k2, v2 = cross_in(place, enc, vec, [two_a, two_b])
    o2, lse2, top2 = attend(q2, k2, v2, False, frames)
    x2, a3 = cross_out(place, o2, x1, vec, [two_b])

    acts = Unit(swap_chain([a3, a1, o1, a2, o2, enc]))
    (x2,) = step(lambda x2: (x2,), [x2], start=[acts], finish=[acts])
    a3, a1, o1, a2, o2, enc = acts.result

    result, df, gb1, gb2, grad2 = feed(a3[0], x2, cot, vec, pack_f)
    plane_2 = lax.psum_scatter(grad2, ("y", "x", "c"), scatter_dimension=0, tiled=True)[0]
    swap_df = Unit(swap_chain([df]))
    da3 = step(lambda df: feed_grad(df, pack_f), [df], start=[swap_df], finish=[swap_df])
    f1 = Unit(reduce_chain(place, True, *weight_grads(place, [a3], swap_df.result, [(0, 0, k) for k in range(4)])))

    def cross_back(da3):
        dx2, do2, e2, sums3 = cross_out_grad(place, da3, x2, cot, vec, [two_b])
        swap = Unit(swap_chain([e2]))
        out = step(
            lambda do2: attend_grad(q2, k2, v2, o2[0], do2, lse2, False, frames), [do2], start=[swap], finish=[swap]
        )
        return dx2, swap.result, sums3, *out

    dx2, swap_e2, sums3, dq2, dk2, dv2, bias2 = step(cross_back, [da3], start=[f1], finish=[f1])
    swap_2 = Unit(swap_chain([dq2, dk2, dv2]))
    dx1, do1, e1, sums2 = step(
        lambda dx2: cross_query_grad(place, dq2, x1, dx2, vec, [two_a, one_b]),
        [dx2],
        start=[swap_2],
        finish=[swap_2],
    )
    swap_e1 = Unit(swap_chain([e1]))
    rights = swap_2.result + swap_e2
    blocks = step(
        lambda *rights: weight_grads(
            place, [enc, a2, o2], [rights[k : k + 2] for k in range(0, 8, 2)], ((0, 1, 0), (1, 0, 0), (0, 2, 0), (2, 3, 0))
        ),
        [value for pair in rights for value in pair],
        start=[swap_e1, f1],
        finish=[swap_e1, f1],
    )
    r1 = Unit(reduce_chain(place, True, *blocks))
    f2 = Unit(z_halves(plane_2))
    dq1, dk1, dv1, bias1 = step(
        lambda do1: attend_grad(q1, k1, v1, o1[0], do1, lse1, True, rows),
        [do1],
        start=[r1, f1, f2],
        finish=[r1, f1, f2],
    )
    swap_1 = Unit(swap_chain([dq1, dk1, dv1]))
    step(start=[swap_1], finish=[swap_1])
    rights = swap_e1.result + swap_1.result
    blocks = step(
        lambda *rights: weight_grads(
            place, [o1, a1], [rights[k : k + 2] for k in range(0, 8, 2)], ((0, 0, 0), (1, 1, 0), (1, 2, 0), (1, 3, 0))
        ),
        [value for pair in rights for value in pair],
        start=[r1, f1],
        finish=[r1, f1],
    )
    r2 = Unit(reduce_chain(place, False, *blocks))

    def last(dx1, dk2):
        grad_input, sums1 = self_in_grad(place, dq1, dk1, dv1, x, dx1, vec, [one_a, one_b])
        return grad_input, sums1, encoder_grad(place, dk2, dv2, [two_a, two_b], frames)

    grad_input, sums1, grad_encoder = step(last, [dx1, dk2], start=[r2, r1, f2], finish=[r2, r1, f2])
    table = Unit(table_chain(vector_table_of(sums1, bias1, sums2, bias2, sums3, gb1, gb2, top1, top2)))
    step(start=[table], finish=[table])
    step(start=[r2, r1, table], finish=[r2, r1, table])
    step(start=[r2, table], finish=[r2, table])
    step(start=[table], finish=[table])
    total = table.result
    shard_cols = vectors.shape[1]
    g_vectors = lax.dynamic_slice_in_dim(total[:VEC_ROWS], lax.axis_index(ALL) * shard_cols, shard_cols, 1)
    maxima = maxima_of(total)
    grad_encoder = grad_encoder.reshape(1, frames, width)
    g_expand = f1.result.reshape(4, 32, width).swapaxes(0, 1).reshape(32, 4 * width)
    cross, own = (value.reshape(4, 32, width) for value in (r1.result, r2.result))
    g_attention = jnp.concatenate([own[1:], own[:1], cross[1:2], cross[:1], cross[2:]], axis=0)
    sums = [g_expand, f2.result, g_attention]
    return result[None], grad_input[None], grad_encoder, sums, g_vectors, maxima


def local(
    fast,
    inputs,
    encoder,
    cotangent,
    attention_master,
    expand_master,
    contract_master,
    vectors_master,
    attention_first,
    expand_first,
    contract_first,
    vectors_first,
    attention_second,
    expand_second,
    contract_second,
    vectors_second,
):
    owned = [m.astype(BF) for m in (attention_master, expand_master, contract_master, vectors_master)]
    compute = gradients_fast if fast and inputs.shape[0] == 1 else gradients_plain
    result, grad_input, grad_encoder, sums, g_vectors, maxima = compute(inputs, encoder, cotangent, owned)
    g_expand, g_contract, g_attention = sums
    shard_cols = vectors_master.shape[1]
    first_col = lax.axis_index(ALL) * shard_cols

    clip_cols = jnp.repeat(jnp.sqrt(clip_limit / jnp.maximum(maxima, clip_limit)), HD, axis=1)
    unit_row = jnp.ones_like(clip_cols[0])
    clip_attention = jnp.stack(
        [clip_cols[0], clip_cols[0], unit_row, unit_row, clip_cols[1], clip_cols[1], unit_row, unit_row]
    )[:, None, :]
    local_cols = lax.dynamic_slice_in_dim(clip_cols, first_col, shard_cols, 1)
    row = lax.broadcasted_iota(jnp.int32, vectors_master.shape, 0)
    clip_vectors = jnp.where(row == 6, local_cols[0:1], jnp.where(row == 9, local_cols[1:2], 1.0))
    step_value = float(ADAM_STEP)
    new_attention = adam_update(
        attention_master, g_attention, attention_first, attention_second, step_value, clip_attention
    )
    new_expand = adam_update(expand_master, g_expand, expand_first, expand_second, step_value, 1.0)
    new_contract = adam_update(contract_master, g_contract, contract_first, contract_second, step_value, 1.0)
    new_vectors = adam_update(vectors_master, g_vectors, vectors_first, vectors_second, step_value, clip_vectors)
    return (
        result,
        grad_input,
        grad_encoder,
        g_attention,
        g_expand,
        g_contract,
        g_vectors,
        new_attention[0],
        new_expand[0],
        new_contract[0],
        new_vectors[0],
        new_attention[1],
        new_expand[1],
        new_contract[1],
        new_vectors[1],
        new_attention[2],
        new_expand[2],
        new_contract[2],
        new_vectors[2],
    )


def solution(mesh):
    planes = mesh.shape["dp"] // 2
    side = math.isqrt(planes)
    if side * side * 2 != mesh.shape["dp"]:
        side = 1
    sizes = (mesh.shape["dp"] // (2 * side), side, 2, mesh.shape["fsdp"])
    fast = sizes == (2, 2, 2, 4)
    mesh = Mesh(mesh.devices.reshape(sizes), ALL)
    shards = (
        P(ALL, None, None),
        P(ALL, None, None),
        P(ALL, None, None),
    )
    weights = (P(None, ALL, None), P(ALL, None), P(ALL, None), P(None, ALL))
    return jax.shard_map(
        functools.partial(local, fast),
        mesh=mesh,
        in_specs=shards + weights * 3,
        out_specs=shards + weights * 4,
        check_vma=False,
    )
```

```python
import functools
import math

import jax
import jax.numpy as jnp
from jax import lax
from jax.experimental import pallas as pl
from jax.experimental.pallas import tpu as pltpu
from jax.sharding import Mesh
from jax.sharding import PartitionSpec as P

HD = 64
ADAM_STEP = 4

eps_norm = 1e-05
clip_limit = 1.0
learn_rate = 0.05
beta_first = 0.9
beta_second = 0.999
eps_adam = 1e-08
weight_decay = 0.1

BF = jnp.bfloat16
F32 = jnp.float32
ALL = ("y", "x", "c", "z")
TILE = 512
KEY_CHUNK = 256
VEC_ROWS = 17
MIB = 1024 * 1024


def dot(left, right):
    return jnp.dot(left, right, preferred_element_type=F32)


def dot_tn(left, right):
    return lax.dot_general(left, right, (((0,), (0,)), ((), ())), preferred_element_type=F32)


def dot_nt(left, right):
    return lax.dot_general(left, right, (((1,), (1,)), ((), ())), preferred_element_type=F32)


def params(limit=60):
    return pltpu.CompilerParams(vmem_limit_bytes=limit * MIB)


def vmem():
    return pl.BlockSpec(memory_space=pltpu.VMEM)


def hbm():
    return pl.BlockSpec(memory_space=pltpu.HBM)


def smem():
    return pl.BlockSpec(memory_space=pltpu.SMEM)


def shape(dims, dtype):
    return jax.ShapeDtypeStruct(tuple(dims), dtype)


def cost(flops, nbytes):
    return pl.CostEstimate(flops=int(flops), bytes_accessed=int(nbytes), transcendentals=0)


class Pack:
    def __init__(self, array, base=0):
        self.array, self.base = array, base


def weight_start(place_ref, pack, row, buf, sem):
    lines = pl.ds(pack.base + row, buf.shape[1])
    pltpu.make_async_copy(pack.array.at[:, lines, :], buf, sem).start()


def call(kernel, packs, args, **settings):
    first, last = len(args), len(args) + len(packs)

    def body(*refs):
        held = [Pack(ref, p.base) for ref, p in zip(refs[first:last], packs)]
        kernel(*refs[:first], *held, *refs[last:])

    specs = settings.pop("in_specs") + [hbm()] * len(packs)
    return pl.pallas_call(body, in_specs=specs, **settings)(*args, *[p.array for p in packs])


def weight_wait(buf, sem):
    pltpu.make_async_copy(buf, buf, sem).wait()


def times(act_ref, buf, put):
    depth = buf.shape[0] * buf.shape[1]

    @pl.loop(0, buf.shape[2] // TILE)
    def _(n):
        start = pl.multiple_of(n * TILE, TILE)
        put(start, dot(act_ref[...], buf[:, :, pl.ds(start, TILE)].reshape(depth, TILE)))


def times_t(act_ref, buf, put):
    per = TILE // buf.shape[1]

    @pl.loop(0, buf.shape[0] // per)
    def _(n):
        start = pl.multiple_of(n * TILE, TILE)
        rows = buf[pl.ds(n * per, per)].reshape(TILE, buf.shape[2])
        put(start, dot_nt(act_ref[...], rows))


def start_all(copies):
    for one in copies:
        one.start()


def wait_all(copies):
    for one in copies:
        one.wait()


def row_chunks(count, size=64):
    return [slice(a, min(a + size, count)) for a in range(0, count, size)]


def normalise(values):
    centered = values - jnp.mean(values, axis=-1, keepdims=True)
    inv = lax.rsqrt(jnp.mean(centered * centered, axis=-1, keepdims=True) + eps_norm)
    return centered * inv, inv


def norm_into(src, gain, shift, out_ref):
    for rows in row_chunks(src.shape[0]):
        normed, _ = normalise(src[rows, :].astype(F32))
        out_ref[rows, :] = (normed * gain + shift).astype(BF)


def norm_grad(src, grad_ref, gain, put):
    gain_sum = jnp.zeros((1, src.shape[1]), F32)
    shift_sum = jnp.zeros((1, src.shape[1]), F32)
    for rows in row_chunks(src.shape[0]):
        normed, inv = normalise(src[rows, :].astype(F32))
        grad = grad_ref[rows, :]
        gain_sum += jnp.sum(grad * normed, axis=0, keepdims=True)
        shift_sum += jnp.sum(grad, axis=0, keepdims=True)
        scaled = grad * gain
        mean_one = jnp.mean(scaled, axis=-1, keepdims=True)
        mean_two = jnp.mean(scaled * normed, axis=-1, keepdims=True)
        put(rows, inv * (scaled - mean_one - normed * mean_two))
    return gain_sum, shift_sum


def column_sum(ref):
    total = jnp.zeros((1, ref.shape[1]), F32)
    for rows in row_chunks(ref.shape[0], 128):
        total += jnp.sum(ref[rows, :].astype(F32), axis=0, keepdims=True)
    return total


def self_in_kernel(place_ref, x_ref, vec_ref, one, two, a_ref, q_ref, k_ref, v_ref, bufs, sems):
    weight_start(place_ref, one, 0, bufs.at[0], sems.at[0])
    weight_start(place_ref, one, 32, bufs.at[1], sems.at[1])
    weight_start(place_ref, two, 0, bufs.at[2], sems.at[2])
    norm_into(x_ref, vec_ref[0:1, :], vec_ref[1:2, :], a_ref)
    for n, (out, bias) in enumerate(((q_ref, 6), (k_ref, None), (v_ref, 7))):
        weight_wait(bufs.at[n], sems.at[n])

        def put(start, value, out=out, bias=bias):
            if bias is not None:
                value = value + vec_ref[bias : bias + 1, pl.ds(start, TILE)]
            out[:, pl.ds(start, TILE)] = value.astype(BF)

        times(a_ref, bufs.at[n], put)


def self_in(place, x, vec, packs):
    rows, width = x.shape
    full = shape((rows, width), BF)
    return call(
        self_in_kernel,
        packs,
        [place, x, vec],
        out_shape=[full] * 4,
        in_specs=[smem(), vmem(), vmem()],
        out_specs=[vmem()] * 4,
        scratch_shapes=[pltpu.VMEM((3, 32, 32, width), BF), pltpu.SemaphoreType.DMA((3,))],
        compiler_params=params(48),
        cost_estimate=cost(6 * rows * width * width, 10 * MIB),
        name="self_in",
    )


def masked_pair(value):
    lane = lax.broadcasted_iota(jnp.int32, value.shape, 1)
    zero = jnp.zeros_like(value)
    return jnp.concatenate([jnp.where(lane < HD, value, zero), jnp.where(lane < HD, zero, value)], axis=0)


def pair_back(both, rows):
    line = lax.broadcasted_iota(jnp.int32, (2 * HD, rows), 0)
    return jnp.where(line < HD, both[:, :rows], both[:, rows:]).T


def key_chunks(count):
    return [(a, min(a + KEY_CHUNK, count)) for a in range(0, count, KEY_CHUNK)]


def exclude(scores, start, rows, causal, valid):
    key = lax.broadcasted_iota(jnp.int32, scores.shape, 0) + start
    if causal:
        query = lax.broadcasted_iota(jnp.int32, scores.shape, 1)
        query = jnp.where(query >= rows, query - rows, query)
        return jnp.where(key <= query, scores, -1e30)
    if start + scores.shape[0] > valid:
        return jnp.where(key < valid, scores, -1e30)
    return scores


def attend_kernel(causal, valid, q_ref, k_ref, v_ref, o_ref, exp_ref, inv_ref, top_ref, held):
    rows = q_ref.shape[0]
    query = masked_pair(q_ref[...] * jnp.asarray(HD**-0.5, BF))
    top = jnp.full((1, 2 * rows), -1e30, F32)
    for a, b in key_chunks(k_ref.shape[0]):
        scores = exclude(dot_nt(k_ref[a:b, :], query), a, rows, causal, valid)
        held[a:b, :] = scores
        top = jnp.maximum(top, jnp.max(scores, axis=0, keepdims=True))
    total = jnp.zeros((1, 2 * rows), F32)
    mixed = jnp.zeros((2 * HD, 2 * rows), F32)
    for a, b in key_chunks(k_ref.shape[0]):
        probs = jnp.exp(held[a:b, :] - top)
        total += jnp.sum(probs, axis=0, keepdims=True)
        rounded = probs.astype(BF)
        exp_ref[0, a:b, :] = rounded
        mixed += dot_tn(v_ref[a:b, :], rounded)
    inv_ref[0] = 1.0 / total
    o_ref[...] = pair_back(mixed * (1.0 / total), rows).astype(BF)
    lane = lax.broadcasted_iota(jnp.int32, (1, 2 * HD), 1)
    first, second = (jnp.max(part, axis=1, keepdims=True) for part in (top[:, :rows], top[:, rows:]))
    top_ref[0] = jnp.where(lane == 0, first, second)


def attend(query, key, value, causal, valid):
    rows, width = query.shape
    keys = key.shape[0]
    pairs = width // (2 * HD)

    def column(count):
        return pl.BlockSpec((count, 2 * HD), lambda h: (0, h))

    line = pl.BlockSpec((1, 1, 2 * rows), lambda h: (h, 0, 0))
    return pl.pallas_call(
        functools.partial(attend_kernel, causal, valid),
        grid=(pairs,),
        out_shape=[
            shape((rows, width), BF), shape((pairs, keys, 2 * rows), BF), shape((pairs, 1, 2 * rows), F32),
            shape((pairs, 1, 2 * HD), F32),
        ],
        in_specs=[column(rows), column(keys), column(keys)],
        out_specs=[
            column(rows), pl.BlockSpec((1, keys, 2 * rows), lambda h: (h, 0, 0)), line,
            pl.BlockSpec((1, 1, 2 * HD), lambda h: (h, 0, 0)),
        ],
        scratch_shapes=[pltpu.VMEM((keys, 2 * rows), F32)],
        compiler_params=params(48),
        cost_estimate=cost(16 * rows * keys * width, 4 * keys * width),
        name="attend_causal" if causal else "attend",
    )(query, key, value)


def self_out_kernel(place_ref, o_ref, x_ref, vec_ref, one, two, x1_ref, a_ref, q_ref, bufs, sems):
    weight_start(place_ref, two, 32, bufs.at[0], sems.at[0])
    weight_start(place_ref, one, 32, bufs.at[1], sems.at[1])
    weight_wait(bufs.at[0], sems.at[0])

    def put_residual(start, value):
        cols = pl.ds(start, TILE)
        x1_ref[:, cols] = x_ref[:, cols].astype(F32) + (value + vec_ref[8:9, cols])

    times(o_ref, bufs.at[0], put_residual)
    norm_into(x1_ref, vec_ref[2:3, :], vec_ref[3:4, :], a_ref)
    weight_wait(bufs.at[1], sems.at[1])

    def put_query(start, value):
        cols = pl.ds(start, TILE)
        q_ref[:, cols] = (value + vec_ref[9:10, cols]).astype(BF)

    times(a_ref, bufs.at[1], put_query)


def self_out(place, mixed, x, vec, packs):
    rows, width = x.shape
    return call(
        self_out_kernel,
        packs,
        [place, mixed, x, vec],
        out_shape=[shape((rows, width), F32), shape((rows, width), BF), shape((rows, width), BF)],
        in_specs=[smem()] + [vmem()] * 3,
        out_specs=[vmem()] * 3,
        scratch_shapes=[pltpu.VMEM((2, 32, 32, width), BF), pltpu.SemaphoreType.DMA((2,))],
        compiler_params=params(48),
        cost_estimate=cost(4 * rows * width * width, 10 * MIB),
        name="self_out",
    )


def cross_in_kernel(place_ref, e_ref, vec_ref, one, two, k_ref, v_ref, bufs, sems):
    for n, part in enumerate((one, two)):
        weight_start(place_ref, part, 0, bufs.at[n], sems.at[n])
    for n, (out, bias) in enumerate(((k_ref, None), (v_ref, 10))):
        weight_wait(bufs.at[n], sems.at[n])

        def put(start, value, out=out, bias=bias):
            if bias is not None:
                value = value + vec_ref[bias : bias + 1, pl.ds(start, TILE)]
            out[:, pl.ds(start, TILE)] = value.astype(BF)

        times(e_ref, bufs.at[n], put)


def cross_in(place, enc, vec, packs):
    frames, width = enc.shape
    return call(
        cross_in_kernel,
        packs,
        [place, enc, vec],
        out_shape=[shape((frames, width), BF)] * 2,
        in_specs=[smem()] + [vmem()] * 2,
        out_specs=[vmem()] * 2,
        scratch_shapes=[pltpu.VMEM((2, 32, 32, width), BF), pltpu.SemaphoreType.DMA((2,))],
        compiler_params=params(48),
        cost_estimate=cost(4 * frames * width * width, 14 * MIB),
        name="cross_in",
    )


def cross_out_kernel(place_ref, o_ref, x1_ref, vec_ref, two, x2_ref, a_ref, buf, sem):
    weight_start(place_ref, two, 32, buf, sem)
    weight_wait(buf, sem)

    def put(start, value):
        cols = pl.ds(start, TILE)
        x2_ref[:, cols] = x1_ref[:, cols] + (value + vec_ref[11:12, cols])

    times(o_ref, buf, put)
    norm_into(x2_ref, vec_ref[4:5, :], vec_ref[5:6, :], a_ref)


def cross_out(place, mixed, x1, vec, packs):
    rows, width = x1.shape
    return call(
        cross_out_kernel,
        packs,
        [place, mixed, x1, vec],
        out_shape=[shape((rows, width), F32), shape((rows, width), BF)],
        in_specs=[smem()] + [vmem()] * 3,
        out_specs=[vmem()] * 2,
        scratch_shapes=[pltpu.VMEM((32, 32, width), BF), pltpu.SemaphoreType.DMA],
        compiler_params=params(48),
        cost_estimate=cost(2 * rows * width * width, 8 * MIB),
        name="cross_out",
    )


def whole(dims):
    return pl.BlockSpec(dims, lambda n: (0,) * len(dims))


def feed_kernel(
    a_ref, x2_ref, e_ref, vec_ref, bias_ref, w1_ref, w2_ref, out_ref, df_ref, gb1_ref, gb2_ref, grad_ref, total
):
    step = pl.program_id(0)
    wide = w1_ref.shape[2]
    depth = a_ref.shape[1]

    @pl.when(step == 0)
    def _():
        total[...] = x2_ref[...] + vec_ref[12:13, :]
        gb2_ref[...] = column_sum(e_ref)

    w2 = w2_ref[...].reshape(wide, depth)
    pre = dot(a_ref[...], w1_ref[...].reshape(depth, wide)) + bias_ref[0]
    cdf = 0.5 * (1.0 + lax.erf(pre * math.sqrt(0.5)))
    act = (pre * cdf).astype(BF)
    slope = cdf + pre * (jnp.exp(-0.5 * (pre * pre)) * (1.0 / math.sqrt(2.0 * math.pi)))
    grad_ref[0] = dot_tn(act, e_ref[...]).astype(BF).reshape(grad_ref.shape[1:])
    grad_pre = (dot_nt(e_ref[...], w2) * slope).astype(BF)
    df_ref[...] = grad_pre
    gb1_ref[0] = jnp.sum(grad_pre.astype(F32), axis=0, keepdims=True)
    total[...] += dot(act, w2)

    @pl.when(step == pl.num_programs(0) - 1)
    def _():
        out_ref[...] = total[...].astype(BF)


def feed(a3, x2, cot, vec, pack):
    rows, width = a3.shape
    hidden = 4 * width
    wide = hidden // 8
    bias = vec[13:].reshape(8, 1, wide)
    return pl.pallas_call(
        feed_kernel,
        grid=(8,),
        out_shape=[
            shape((rows, width), BF), shape((rows, hidden), BF), shape((8, 1, wide), F32), shape((1, width), F32),
            shape((8, 4, 128, width), BF),
        ],
        in_specs=[
            whole((rows, width)),
            whole((rows, width)),
            whole((rows, width)),
            whole(vec.shape),
            pl.BlockSpec((1, 1, wide), lambda n: (n, 0, 0)),
            pl.BlockSpec((32, 32, wide), lambda n: (0, n // 2, n % 2)),
            pl.BlockSpec((4, 128, width), lambda n: (n, 1, 0)),
        ],
        out_specs=[
            whole((rows, width)),
            pl.BlockSpec((rows, wide), lambda n: (0, n)),
            pl.BlockSpec((1, 1, wide), lambda n: (n, 0, 0)),
            whole((1, width)),
            pl.BlockSpec((1, 4, 128, width), lambda n: (n, 0, 0, 0)),
        ],
        scratch_shapes=[pltpu.VMEM((rows, width), F32)],
        compiler_params=params(),
        cost_estimate=cost(8 * rows * width * hidden, 30 * MIB),
        name="feed",
    )(a3, x2, cot, vec, bias, pack, pack)


def feed_grad_kernel(df_ref, w1_ref, da_ref):
    @pl.when(pl.program_id(0) == 0)
    def _():
        da_ref[...] = jnp.zeros_like(da_ref)

    da_ref[...] += dot_nt(df_ref[...], w1_ref[...].reshape(da_ref.shape[1], w1_ref.shape[2]))


def feed_grad(df, pack):
    rows, hidden = df.shape
    width = pack.shape[2]
    return pl.pallas_call(
        feed_grad_kernel,
        grid=(hidden // width,),
        out_shape=shape((rows, width), F32),
        in_specs=[
            pl.BlockSpec((rows, width), lambda n: (0, n)),
            pl.BlockSpec((32, 32, width), lambda n: (0, n, 0)),
        ],
        out_specs=whole((rows, width)),
        compiler_params=params(),
        cost_estimate=cost(2 * rows * width * hidden, 12 * MIB),
        name="feed_grad",
    )(df, pack)


def cross_out_grad_kernel(place_ref, da_ref, x2_ref, cot_ref, vec_ref, two, dx_ref, do_ref, e_ref, sums_ref, buf, sem):
    weight_start(place_ref, two, 32, buf, sem)

    def put(rows, value):
        total = cot_ref[rows, :].astype(F32) + value
        dx_ref[rows, :] = total
        e_ref[rows, :] = total.astype(BF)

    gain, shift = norm_grad(x2_ref, da_ref, vec_ref[4:5, :], put)
    sums_ref[0:1, :] = gain
    sums_ref[1:2, :] = shift
    sums_ref[2:3, :] = column_sum(e_ref)
    weight_wait(buf, sem)

    def put_mixed(start, value):
        do_ref[:, pl.ds(start, TILE)] = value.astype(BF)

    times_t(e_ref, buf, put_mixed)


def cross_out_grad(place, da3, x2, cot, vec, packs):
    rows, width = x2.shape
    low = shape((rows, width), BF)
    return call(
        cross_out_grad_kernel,
        packs,
        [place, da3, x2, cot, vec],
        out_shape=[shape((rows, width), F32), low, low, shape((3, width), F32)],
        in_specs=[smem()] + [vmem()] * 4,
        out_specs=[vmem()] * 4,
        scratch_shapes=[pltpu.VMEM((32, 32, width), BF), pltpu.SemaphoreType.DMA],
        compiler_params=params(),
        cost_estimate=cost(2 * rows * width * width, 10 * MIB),
        name="cross_out_grad",
    )


def attend_grad_kernel(q_ref, k_ref, v_ref, o_ref, do_ref, exp_ref, inv_ref, dq_ref, dk_ref, dv_ref, sums_ref):
    rows = q_ref.shape[0]
    scale = jnp.asarray(HD**-0.5, BF)
    query = masked_pair(q_ref[...] * scale)
    grad_out = masked_pair(do_ref[...])
    product = (do_ref[...].astype(F32) * o_ref[...].astype(F32)).T
    delta = jnp.concatenate(
        [jnp.sum(product[:HD], axis=0, keepdims=True), jnp.sum(product[HD:], axis=0, keepdims=True)], axis=1
    )
    inv = inv_ref[0]
    grad_query = jnp.zeros((2 * HD, 2 * rows), F32)
    value_sum = jnp.zeros((1, 2 * HD), F32)
    for a, b in key_chunks(k_ref.shape[0]):
        key = k_ref[a:b, :]
        probs = exp_ref[0, a:b, :].astype(F32) * inv
        grad_probs = dot_nt(v_ref[a:b, :], grad_out)
        grad_scores = (probs * (grad_probs - delta)).astype(BF)
        grad_value = dot(probs.astype(BF), grad_out).astype(BF)
        dv_ref[a:b, :] = grad_value
        value_sum += jnp.sum(grad_value.astype(F32), axis=0, keepdims=True)
        dk_ref[a:b, :] = dot(grad_scores, query).astype(BF)
        grad_query += dot_tn(key, grad_scores)
    grad_query = (pair_back(grad_query, rows) * HD**-0.5).astype(BF)
    dq_ref[...] = grad_query
    sums_ref[0:1, :] = jnp.sum(grad_query.astype(F32), axis=0, keepdims=True)
    sums_ref[1:2, :] = value_sum


def attend_grad(query, key, value, mixed, grad_mixed, saved):
    rows, width = query.shape
    keys = key.shape[0]
    pairs = width // (2 * HD)

    def column(count):
        return pl.BlockSpec((count, 2 * HD), lambda h: (0, h))

    line = pl.BlockSpec((1, 1, 2 * rows), lambda h: (h, 0, 0))
    return pl.pallas_call(
        attend_grad_kernel,
        grid=(pairs,),
        out_shape=[shape((rows, width), BF)] + [shape((keys, width), BF)] * 2 + [shape((2, width), F32)],
        in_specs=[
            column(rows), column(keys), column(keys), column(rows), column(rows),
            pl.BlockSpec((1, keys, 2 * rows), lambda h: (h, 0, 0)), line,
        ],
        out_specs=[column(rows), column(keys), column(keys), column(2)],
        compiler_params=params(),
        cost_estimate=cost(32 * rows * keys * width, 8 * keys * width),
        name="attend_grad",
    )(query, key, value, mixed, grad_mixed, *saved)


def cross_query_grad_kernel(
    place_ref, dq_ref, x1_ref, dx2_ref, vec_ref, one, two, dx_ref, do_ref, e_ref, sums_ref, bufs, da_ref, sem
):
    for n, part in enumerate((one, two)):
        weight_start(place_ref, part, 32, bufs.at[n], sem.at[n])
    weight_wait(bufs.at[0], sem.at[0])

    def put_act(start, value):
        da_ref[:, pl.ds(start, TILE)] = value

    times_t(dq_ref, bufs.at[0], put_act)

    def put(rows, value):
        total = dx2_ref[rows, :] + value
        dx_ref[rows, :] = total
        e_ref[rows, :] = total.astype(BF)

    gain, shift = norm_grad(x1_ref, da_ref, vec_ref[2:3, :], put)
    sums_ref[0:1, :] = gain
    sums_ref[1:2, :] = shift
    sums_ref[2:3, :] = column_sum(e_ref)
    weight_wait(bufs.at[1], sem.at[1])

    def put_mixed(start, value):
        do_ref[:, pl.ds(start, TILE)] = value.astype(BF)

    times_t(e_ref, bufs.at[1], put_mixed)


def cross_query_grad(place, dq2, x1, dx2, vec, packs):
    rows, width = x1.shape
    low = shape((rows, width), BF)
    return call(
        cross_query_grad_kernel,
        packs,
        [place, dq2, x1, dx2, vec],
        out_shape=[shape((rows, width), F32), low, low, shape((3, width), F32)],
        in_specs=[smem()] + [vmem()] * 4,
        out_specs=[vmem()] * 4,
        scratch_shapes=[
            pltpu.VMEM((2, 32, 32, width), BF), pltpu.VMEM((rows, width), F32), pltpu.SemaphoreType.DMA((2,)),
        ],
        compiler_params=params(),
        cost_estimate=cost(4 * rows * width * width, 14 * MIB),
        name="cross_query_grad",
    )


def weight_grads_kernel(jobs, lefts, rights, place_ref, *refs):
    count = 2 * (lefts + rights)
    one_away, two_away, one_mine, two_mine = refs[count : count + 4]
    held, (grads, in_sems, sems) = refs[count + 4 : 2 * count + 4], refs[2 * count + 4 :]
    order = []
    for left, right, _ in jobs:
        order += [n for n in (2 * left, 2 * (lefts + right), 2 * left + 1, 2 * (lefts + right) + 1) if n not in order]
    pending = {n: pltpu.make_async_copy(refs[n], held[n], in_sems.at[n]) for n in order}
    start_all(pending.values())

    def ready(n):
        if n in pending:
            pending.pop(n).wait()
        return held[n]

    core = jnp.bitwise_and(place_ref[0], 1)
    plane = lax.shift_right_logical(place_ref[0], 1)
    split = len(jobs) // 2
    width = one_mine.shape[3]
    copies = []
    for pair in ((3, 1), (2, 0)):
        starts = [pl.multiple_of((jnp.bitwise_xor(plane, j) * 2 + core) * 128, 128) for j in pair]
        turned = {}
        for k, (left, right, block) in enumerate(jobs):
            wide = slice(block * width, (block + 1) * width)
            total = None
            for side in range(2):
                act, grad = ready(2 * left + side), ready(2 * (lefts + right) + side)
                if (left, side) not in turned:
                    columns = jnp.concatenate([act[:, pl.ds(start, 128)] for start in starts], axis=1)
                    turned[left, side] = columns.T
                value = dot(turned[left, side], grad[:, wide])
                total = value if total is None else total + value
            rounded = total.astype(BF).reshape((2,) + grads.shape[2:])
            lines = pl.ds(32 * (k % split), 32)
            for n, j in enumerate(pair):
                grads[k, j] = rounded[n]
                y, x = j // 2, j % 2
                if k < split:
                    target = (one_away if x else one_mine).at[y, :, lines, :]
                else:
                    target = (two_away if y else two_mine).at[x, :, lines, :]
                copies.append(pltpu.make_async_copy(grads.at[k, j], target, sems.at[k, j]))
                copies[-1].start()
    wait_all(copies)


def weight_grads(place, lefts, rights, jobs):
    width = lefts[0][0].shape[1]
    count = len(jobs)
    blocks = shape((2, 4, 16 * count, width), BF)
    operands = [value for pair in lefts + rights for value in pair]
    flops = sum(4 * lefts[left][0].shape[0] * width * width // 2 for left, _, _ in jobs)
    return pl.pallas_call(
        functools.partial(weight_grads_kernel, jobs, len(lefts), len(rights)),
        out_shape=[blocks] * 4,
        in_specs=[smem()] + [hbm()] * len(operands),
        out_specs=[hbm()] * 4,
        scratch_shapes=[pltpu.VMEM(value.shape, BF) for value in operands] + [
            pltpu.VMEM((count, 4, 4, 32, width), BF), pltpu.SemaphoreType.DMA((len(operands),)),
            pltpu.SemaphoreType.DMA((count, 4)),
        ],
        compiler_params=params(),
        cost_estimate=cost(flops, 12 * MIB),
        name="weight_grads",
    )(place, *operands)


def encoder_grad_kernel(place_ref, dk_ref, dv_ref, one, two, out_ref, bufs, held, sems):
    for n, part in enumerate((one, two)):
        weight_start(place_ref, part, 0, bufs.at[n], sems.at[n])
    for n in range(2):
        weight_wait(bufs.at[n], sems.at[n])
    width = dk_ref.shape[1]
    per = TILE // 32
    lines = width // 128

    @pl.loop(0, width // TILE)
    def _(n):
        total = dot_nt(dk_ref[...], bufs[0, pl.ds(n * per, per)].reshape(TILE, width))
        total += dot_nt(dv_ref[...], bufs[1, pl.ds(n * per, per)].reshape(TILE, width))
        for side in range(TILE // 128):
            start = n * (TILE // 128) + side
            held[pl.ds(start, total.shape[0], stride=lines), :] = total[:, side * 128 : (side + 1) * 128]

    copy = pltpu.make_async_copy(held.at[pl.ds(0, out_ref.shape[0]), :], out_ref, sems.at[2])
    copy.start()
    copy.wait()


def encoder_grad(place, dk2, dv2, packs, frames):
    padded, width = dk2.shape
    lines = width // 128
    return call(
        encoder_grad_kernel,
        packs,
        [place, dk2, dv2],
        out_shape=shape((frames * lines, 128), F32),
        in_specs=[smem()] + [vmem()] * 2,
        out_specs=hbm(),
        scratch_shapes=[
            pltpu.VMEM((2, 32, 32, width), BF), pltpu.VMEM((padded * lines, 128), F32), pltpu.SemaphoreType.DMA((3,)),
        ],
        compiler_params=params(),
        cost_estimate=cost(4 * padded * width * width, 16 * MIB),
        name="encoder_grad",
    )


def self_in_grad_kernel(
    place_ref, dq_ref, dk_ref, dv_ref, x_ref, dx1_ref, vec_ref, one, two, dx_ref, sums_ref, bufs, da_ref, sems
):
    weight_start(place_ref, one, 0, bufs.at[0], sems.at[0])
    weight_start(place_ref, one, 32, bufs.at[1], sems.at[1])
    weight_start(place_ref, two, 0, bufs.at[2], sems.at[2])
    for n, ref in enumerate((dq_ref, dk_ref, dv_ref)):
        weight_wait(bufs.at[n], sems.at[n])

        def put_act(start, value, n=n):
            if n:
                da_ref[:, pl.ds(start, TILE)] += value
            else:
                da_ref[:, pl.ds(start, TILE)] = value

        times_t(ref, bufs.at[n], put_act)

    def put(rows, value):
        dx_ref[rows, :] = dx1_ref[rows, :] + value

    gain, shift = norm_grad(x_ref, da_ref, vec_ref[0:1, :], put)
    sums_ref[0:1, :] = gain
    sums_ref[1:2, :] = shift


def self_in_grad(place, dq1, dk1, dv1, x, dx1, vec, packs):
    rows, width = x.shape
    return call(
        self_in_grad_kernel,
        packs,
        [place, dq1, dk1, dv1, x, dx1, vec],
        out_shape=[shape((rows, width), F32), shape((2, width), F32)],
        in_specs=[smem()] + [vmem()] * 6,
        out_specs=[vmem()] * 2,
        scratch_shapes=[
            pltpu.VMEM((3, 32, 32, width), BF), pltpu.VMEM((rows, width), F32), pltpu.SemaphoreType.DMA((3,)),
        ],
        compiler_params=params(),
        cost_estimate=cost(6 * rows * width * width, 14 * MIB),
        name="self_in_grad",
    )


SWAP = [(0, 1), (1, 0)]
MATRICES = ((0, 1), (2, 3), (5, 4), (6, 7))


class Unit:
    def __init__(self, chain):
        self.chain, self.result, self.moved = chain, None, None
        self.wanted = next(chain)

    def advance(self, arrived):
        try:
            self.wanted = self.chain.send(arrived)
        except StopIteration as stop:
            self.wanted, self.result = None, stop.value


def step(run=None, inputs=(), start=(), finish=()):
    start, finish = ([u for u in units if u is not None] for units in (start, finish))
    operands = [[value for value, _, _ in u.wanted] for u in start]
    inputs, operands = lax.optimization_barrier((tuple(inputs), operands))
    for u, values in zip(start, operands):
        u.moved = [lax.ppermute(v, axis, pairs) for v, (_, axis, pairs) in zip(values, u.wanted)]
    out = run(*inputs) if run else ()
    if finish:
        out, moved = lax.optimization_barrier((out, [u.moved for u in finish]))
        for u, values in zip(finish, moved):
            u.advance(values)
    return out


def turns():
    return [[(n, (n + k) % 4) for n in range(4)] for k in range(4)]


def add_rounded(left, right):
    return (left.astype(F32) + right.astype(F32)).astype(BF)


def add_kernel(plan, sources, place_ref, *refs):
    left, right = refs[:sources], refs[sources : 2 * sources]
    *outs, one, two, total, sems, out_sems = refs[2 * sources :]
    pieces = plan(place_ref)
    copies = [
        [
            pltpu.make_async_copy(side[source].at[index], held.at[n], sems.at[k, n])
            for k, (side, held) in enumerate(((left, one), (right, two)))
        ]
        for n, (source, index, _, _) in enumerate(pieces)
    ]
    for pair in copies:
        start_all(pair)
    away = []
    for n, (_, _, out, index) in enumerate(pieces):
        wait_all(copies[n])
        total[n] = add_rounded(one[n], two[n])
        away.append(pltpu.make_async_copy(total.at[n], outs[out].at[index], out_sems.at[n]))
        away[-1].start()
    wait_all(away)


def add_pieces(place, left, right, outs, piece, plan, count):
    held = pltpu.VMEM((count,) + piece, BF)
    return pl.pallas_call(
        functools.partial(add_kernel, plan, len(left)),
        out_shape=[shape(o, BF) for o in outs],
        in_specs=[smem()] + [hbm()] * (2 * len(left)),
        out_specs=[hbm()] * len(outs),
        scratch_shapes=[
            held, held, held, pltpu.SemaphoreType.DMA((2, count)), pltpu.SemaphoreType.DMA((count,)),
        ],
        compiler_params=params(),
        cost_estimate=cost(0, 6 * count * math.prod(piece)),
        name="add_pieces",
    )(place, *left, *right)


def turn_z(place_ref, k):
    return jnp.bitwise_and(place_ref[1] + k, 3)


def swap_chain(values):
    moved = yield [(value, "c", SWAP) for value in values]
    return list(zip(values, moved))


NEAR = [(0, 1), (1, 0), (2, 3), (3, 2)]
FAR = [(0, 2), (2, 0), (1, 3), (3, 1)]


def pick_z(both, k):
    return lax.dynamic_index_in_dim(both, jnp.bitwise_xor(lax.axis_index("z"), k), 0, keepdims=False)


def z_halves(both):
    away, mine = (jnp.stack([pick_z(both, k), pick_z(both, k ^ 2)]) for k in (1, 0))
    return (yield from z_two(away, mine))


def z_two(away, mine):
    (moved,) = yield [(away, "z", NEAR)]
    near = mine[0].astype(F32) + moved[0].astype(F32)
    (moved,) = yield [(add_rounded(mine[1], moved[1]), "z", FAR)]
    return near + moved.astype(F32)


def reduce_chain(place, halving, one, two, *mine):
    half, columns = one.shape[2:]
    rows = 2 * half
    parts = [pl.ds(0, half), pl.ds(half, half)]
    moved = yield [(one, "x", SWAP), (two, "y", SWAP)]

    def plan_two(_):
        return [(n, side, n if side else 2 + n, slice(None)) for side in (1, 0) for n in range(2)]

    outs = [(4, half, columns)] * 4
    one, two, *mine = add_pieces(place, list(mine), list(moved), outs, (4, half, columns), plan_two, 4)
    moved = yield [(one, "y", SWAP), (two, "x", SWAP)]

    if halving:

        def plan_halves(place_ref):
            turns = [(1, 0, 0), (3, 0, 1), (2, 1, 1), (0, 1, 0)]
            return [
                (n, jnp.bitwise_xor(place_ref[1], turn), out, (at, parts[n])) for turn, out, at in turns for n in range(2)
            ]

        outs = [(2, rows, columns)] * 2
        return (yield from z_two(*add_pieces(place, mine, list(moved), outs, (half, columns), plan_halves, 8)))

    def plan_three(place_ref):
        return [(n, turn_z(place_ref, k), k, parts[n]) for k in (2, 1, 3, 0) for n in range(2)]

    pieces = add_pieces(place, mine, list(moved), [(rows, columns)] * 4, (half, columns), plan_three, 8)
    moved = yield [(pieces[k], "z", turns()[k]) for k in (1, 3, 2)]
    return functools.reduce(jnp.add, [value.astype(F32) for value in moved], pieces[0].astype(F32))


def reduce_feed_plain(grad1, grad2):
    grad2 = grad2.reshape(-1, grad2.shape[3])
    return [lax.psum_scatter(g, ALL, scatter_dimension=0, tiled=True) for g in (grad1, grad2)]


def table_chain(table):
    row = lax.broadcasted_iota(jnp.int32, table.shape, 0)

    def combine(left, right):
        return jnp.where(row < VEC_ROWS, left + right, jnp.maximum(left, right))

    for axis in ("c", "x", "y"):
        moved = yield [(table, axis, SWAP)]
        table = combine(table, moved[0])
    for pairs in (NEAR, FAR):
        moved = yield [(table, "z", pairs)]
        table = combine(table, moved[0])
    return table


def vector_table(pack, row, rows, shard_cols):
    table = pack[:, row, : rows * shard_cols].reshape(32, rows, shard_cols).swapaxes(0, 1)
    return table.reshape(rows, 32 * shard_cols).astype(F32)


def expand_shard(expand, width):
    return jnp.concatenate([expand[:, n * width : (n + 1) * width] for n in range(expand.shape[1] // width)], axis=0)


def gather_fast(attention, expand, contract, vectors):
    width = attention.shape[2]
    line = jnp.pad(vectors.reshape(1, -1), ((0, 7), (0, width - vectors.size)))
    shard = jnp.concatenate([attention[m] for group in MATRICES for m in group] + [line], axis=0)
    pack = lax.all_gather(shard, ALL, axis=0, tiled=False)
    parts = []
    before = []
    for part in (expand_shard(expand, width), contract):
        moved = []
        part, _ = lax.optimization_barrier((part, before))
        for k in (3, 1, 2):
            part, moved = lax.optimization_barrier((part, moved))
            moved.append(lax.ppermute(part, "z", turns()[k]))
        part, moved = lax.optimization_barrier((part, moved))
        before = moved
        line = jnp.stack([part, moved[0], moved[2], moved[1]] * 2)
        parts.append(lax.dynamic_slice_in_dim(line, (4 - lax.axis_index("z")) % 4, 4, 0))
    pack_f = lax.all_gather(jnp.concatenate(parts, axis=1), ("y", "x", "c"), axis=0, tiled=True)
    return parts_of(pack), pack_f, vector_table(pack, 256, *vectors.shape)


def parts_of(pack):
    return [Pack(pack, 64 * n) for n in range(4)]


def gather_plain(attention, expand, contract, vectors):
    attention = lax.all_gather(attention, ALL, axis=1, tiled=True)
    expand = lax.all_gather(expand, ALL, axis=0, tiled=True)
    contract = lax.all_gather(contract, ALL, axis=0, tiled=True)
    vectors = lax.all_gather(vectors, ALL, axis=1, tiled=True)
    width = attention.shape[2]
    pack = jnp.concatenate([attention[m].reshape(32, 32, width) for group in MATRICES for m in group], axis=1)
    first = expand.reshape(32, 32, 4, width).swapaxes(1, 2).reshape(32, 128, width)
    pack_f = jnp.concatenate([first, contract.reshape(32, 128, width)], axis=1)
    return parts_of(pack), pack_f, vectors.astype(F32)


def adam_update(master, gradient, first, second, step_value, clip_scale):
    first_new = beta_first * first.astype(F32) + (1.0 - beta_first) * gradient
    second_new = beta_second * second + (1.0 - beta_second) * gradient * gradient
    direction = (
        first_new
        / (1.0 - beta_first**step_value)
        / (jnp.sqrt(second_new / (1.0 - beta_second**step_value)) + eps_adam)
    )
    master_new = (master - learn_rate * (direction + weight_decay * master)) * clip_scale
    return (first_new, second_new, master_new)


def table_kernel(sums1, bias1, sums2, bias2, sums3, gb1, gb2, top1, top2, out):
    out[...] = jnp.zeros_like(out)
    rows = [
        sums1[0:1, :], sums1[1:2, :], sums2[0:1, :], sums2[1:2, :], sums3[0:1, :], sums3[1:2, :],
        bias1[0:1, :], bias1[1:2, :], sums2[2:3, :], bias2[0:1, :], bias2[1:2, :], sums3[2:3, :], gb2[...],
    ]
    for n, row in enumerate(rows):
        out[n : n + 1, :] = row
    half = gb1.shape[2]
    for n in range(gb1.shape[0]):
        out[len(rows) + n // 2 : len(rows) + n // 2 + 1, n % 2 * half : (n % 2 + 1) * half] = gb1[n]
    for n, top in enumerate((top1, top2)):
        for pair in range(top.shape[0]):
            lanes = slice(pair * 2 * HD, (pair + 1) * 2 * HD)
            out[VEC_ROWS + n : VEC_ROWS + n + 1, lanes] = top[pair]


def vector_table_of(*pieces):
    width = pieces[0].shape[1]
    return pl.pallas_call(
        table_kernel,
        out_shape=shape((24, width), F32),
        in_specs=[vmem()] * len(pieces),
        out_specs=vmem(),
        compiler_params=params(),
        cost_estimate=cost(0, 200000),
        name="vector_table",
    )(*pieces)


def maxima_of(table):
    return table[VEC_ROWS : VEC_ROWS + 2].reshape(2, -1, 2 * HD)[:, :, :2].reshape(2, -1)


def sequence_plain(place, x, enc, frames, cot, vec, packs, pack_f):
    rows, width = x.shape
    one_a, one_b, two_a, two_b = packs
    a1, q1, k1, v1 = self_in(place, x, vec, [one_a, one_b])
    o1, *saved1, top1 = attend(q1, k1, v1, True, rows)
    x1, a2, q2 = self_out(place, o1, x, vec, [two_a, one_b])
    k2, v2 = cross_in(place, enc, vec, [two_a, two_b])
    o2, *saved2, top2 = attend(q2, k2, v2, False, frames)
    x2, a3 = cross_out(place, o2, x1, vec, [two_b])
    result, df, gb1, gb2, grad2 = feed(a3, x2, cot, vec, pack_f)
    da3 = feed_grad(df, pack_f)
    dx2, do2, e2, sums3 = cross_out_grad(place, da3, x2, cot, vec, [two_b])
    dq2, dk2, dv2, bias2 = attend_grad(q2, k2, v2, o2, do2, saved2)
    dx1, do1, e1, sums2 = cross_query_grad(place, dq2, x1, dx2, vec, [two_a, one_b])
    dq1, dk1, dv1, bias1 = attend_grad(q1, k1, v1, o1, do1, saved1)
    grad_input, sums1 = self_in_grad(place, dq1, dk1, dv1, x, dx1, vec, [one_a, one_b])
    grad_encoder = encoder_grad(place, dk2, dv2, [two_a, two_b], frames).reshape(frames, width)
    table = vector_table_of(sums1, bias1, sums2, bias2, sums3, gb1, gb2, top1, top2)
    pairs = ((a1, dq1), (a1, dk1), (a1, dv1), (o1, e1), (a2, dq2), (enc, dk2), (enc, dv2), (o2, e2))
    g_attention = jnp.stack([dot_tn(left, right) for left, right in pairs])
    sums = [dot_tn(a3, df), grad2.astype(F32), g_attention]
    return result, grad_input, grad_encoder, table[:VEC_ROWS], maxima_of(table), sums


def gradients_plain(inputs, encoder, cotangent, owned):
    packs, pack_f, vec = gather_plain(*owned)
    place = jnp.zeros((2,), jnp.int32)
    frames = encoder.shape[1]
    done = []
    for n in range(inputs.shape[0]):
        enc = pad_frames(encoder[n])
        done.append(sequence_plain(place, inputs[n], enc, frames, cotangent[n], vec, packs, pack_f))
    result, grad_input, grad_encoder = (jnp.stack([d[k] for d in done]) for k in range(3))
    g_vectors = functools.reduce(jnp.add, [d[3] for d in done])
    maxima = functools.reduce(jnp.maximum, [d[4] for d in done])
    grad1, grad2, g_attention = (functools.reduce(jnp.add, values) for values in zip(*[d[5] for d in done]))
    sums = reduce_feed_plain(grad1, grad2) + [lax.psum_scatter(g_attention, ALL, scatter_dimension=1, tiled=True)]
    g_vectors = lax.psum_scatter(g_vectors, ALL, scatter_dimension=1, tiled=True)
    return result, grad_input, grad_encoder, sums, g_vectors, lax.pmax(maxima, ALL)


def pad_frames(enc):
    return jnp.pad(enc, ((0, -enc.shape[0] % 16), (0, 0)))


def gradients_fast(inputs, encoder, cotangent, owned):
    attention, expand, contract, vectors = owned
    x, cot = inputs[0], cotangent[0]
    rows, width = x.shape
    frames = encoder.shape[1]
    place = jnp.stack([lax.axis_index(("y", "x", "c")), lax.axis_index("z")]).astype(jnp.int32)
    (one_a, one_b, two_a, two_b), pack_f, vec = gather_fast(*owned)
    enc = pad_frames(encoder[0])
    a1, q1, k1, v1 = self_in(place, x, vec, [one_a, one_b])
    o1, *saved1, top1 = attend(q1, k1, v1, True, rows)
    x1, a2, q2 = self_out(place, o1, x, vec, [two_a, one_b])
    k2, v2 = cross_in(place, enc, vec, [two_a, two_b])
    o2, *saved2, top2 = attend(q2, k2, v2, False, frames)
    x2, a3 = cross_out(place, o2, x1, vec, [two_b])

    acts = Unit(swap_chain([a3, a1, o1, a2, o2, enc]))
    (x2,) = step(lambda x2: (x2,), [x2], start=[acts], finish=[acts])
    a3, a1, o1, a2, o2, enc = acts.result

    result, df, gb1, gb2, grad2 = feed(a3[0], x2, cot, vec, pack_f)
    plane_2 = lax.psum_scatter(grad2, ("y", "x", "c"), scatter_dimension=0, tiled=True)[0]
    swap_df = Unit(swap_chain([df]))
    da3 = step(lambda df: feed_grad(df, pack_f), [df], start=[swap_df], finish=[swap_df])
    f1 = Unit(reduce_chain(place, True, *weight_grads(place, [a3], swap_df.result, [(0, 0, k) for k in range(4)])))

    def cross_back(da3):
        dx2, do2, e2, sums3 = cross_out_grad(place, da3, x2, cot, vec, [two_b])
        swap = Unit(swap_chain([e2]))
        out = step(
            lambda do2: attend_grad(q2, k2, v2, o2[0], do2, saved2), [do2], start=[swap], finish=[swap]
        )
        return dx2, swap.result, sums3, *out

    dx2, swap_e2, sums3, dq2, dk2, dv2, bias2 = step(cross_back, [da3], start=[f1], finish=[f1])
    swap_2 = Unit(swap_chain([dq2, dk2, dv2]))
    dx1, do1, e1, sums2 = step(
        lambda dx2: cross_query_grad(place, dq2, x1, dx2, vec, [two_a, one_b]),
        [dx2],
        start=[swap_2],
        finish=[swap_2],
    )
    swap_e1 = Unit(swap_chain([e1]))
    rights = swap_2.result + swap_e2
    blocks = step(
        lambda *rights: weight_grads(
            place, [enc, a2, o2], [rights[k : k + 2] for k in range(0, 8, 2)], ((0, 1, 0), (1, 0, 0), (0, 2, 0), (2, 3, 0))
        ),
        [value for pair in rights for value in pair],
        start=[swap_e1, f1],
        finish=[swap_e1, f1],
    )
    r1 = Unit(reduce_chain(place, True, *blocks))
    f2 = Unit(z_halves(plane_2))

    def self_back(do1):
        dq1, dk1, dv1, bias1 = attend_grad(q1, k1, v1, o1[0], do1, saved1)
        grad_input, sums1 = self_in_grad(place, dq1, dk1, dv1, x, dx1, vec, [one_a, one_b])
        return dq1, dk1, dv1, bias1, grad_input, sums1

    dq1, dk1, dv1, bias1, grad_input, sums1 = step(self_back, [do1], start=[r1, f1, f2], finish=[r1, f1, f2])
    table = Unit(table_chain(vector_table_of(sums1, bias1, sums2, bias2, sums3, gb1, gb2, top1, top2)))
    swap_1 = Unit(swap_chain([dq1, dk1, dv1]))
    step(start=[swap_1, table], finish=[swap_1, table])
    rights = swap_e1.result + swap_1.result
    blocks = step(
        lambda *rights: weight_grads(
            place, [o1, a1], [rights[k : k + 2] for k in range(0, 8, 2)], ((0, 0, 0), (1, 1, 0), (1, 2, 0), (1, 3, 0))
        ),
        [value for pair in rights for value in pair],
        start=[r1, f1, table],
        finish=[r1, f1, table],
    )
    r2 = Unit(reduce_chain(place, False, *blocks))
    grad_encoder = step(
        lambda dk2: encoder_grad(place, dk2, dv2, [two_a, two_b], frames),
        [dk2],
        start=[r2, r1, f2, table],
        finish=[r2, r1, f2, table],
    )
    step(start=[r2, r1, table], finish=[r2, r1, table])
    step(start=[r2, table], finish=[r2, table])
    total = table.result
    shard_cols = vectors.shape[1]
    g_vectors = lax.dynamic_slice_in_dim(total[:VEC_ROWS], lax.axis_index(ALL) * shard_cols, shard_cols, 1)
    maxima = maxima_of(total)
    grad_encoder = grad_encoder.reshape(1, frames, width)
    g_expand = f1.result.reshape(4, 32, width).swapaxes(0, 1).reshape(32, 4 * width)
    cross, own = (value.reshape(4, 32, width) for value in (r1.result, r2.result))
    g_attention = jnp.concatenate([own[1:], own[:1], cross[1:2], cross[:1], cross[2:]], axis=0)
    sums = [g_expand, f2.result, g_attention]
    return result[None], grad_input[None], grad_encoder, sums, g_vectors, maxima


def local(
    fast,
    inputs,
    encoder,
    cotangent,
    attention_master,
    expand_master,
    contract_master,
    vectors_master,
    attention_first,
    expand_first,
    contract_first,
    vectors_first,
    attention_second,
    expand_second,
    contract_second,
    vectors_second,
):
    owned = [m.astype(BF) for m in (attention_master, expand_master, contract_master, vectors_master)]
    compute = gradients_fast if fast and inputs.shape[0] == 1 else gradients_plain
    result, grad_input, grad_encoder, sums, g_vectors, maxima = compute(inputs, encoder, cotangent, owned)
    g_expand, g_contract, g_attention = sums
    shard_cols = vectors_master.shape[1]
    first_col = lax.axis_index(ALL) * shard_cols

    clip_cols = jnp.repeat(jnp.sqrt(clip_limit / jnp.maximum(maxima, clip_limit)), HD, axis=1)
    unit_row = jnp.ones_like(clip_cols[0])
    clip_attention = jnp.stack(
        [clip_cols[0], clip_cols[0], unit_row, unit_row, clip_cols[1], clip_cols[1], unit_row, unit_row]
    )[:, None, :]
    local_cols = lax.dynamic_slice_in_dim(clip_cols, first_col, shard_cols, 1)
    row = lax.broadcasted_iota(jnp.int32, vectors_master.shape, 0)
    clip_vectors = jnp.where(row == 6, local_cols[0:1], jnp.where(row == 9, local_cols[1:2], 1.0))
    step_value = float(ADAM_STEP)
    new_attention = adam_update(
        attention_master, g_attention, attention_first, attention_second, step_value, clip_attention
    )
    new_expand = adam_update(expand_master, g_expand, expand_first, expand_second, step_value, 1.0)
    new_contract = adam_update(contract_master, g_contract, contract_first, contract_second, step_value, 1.0)
    new_vectors = adam_update(vectors_master, g_vectors, vectors_first, vectors_second, step_value, clip_vectors)
    return (
        result,
        grad_input,
        grad_encoder,
        g_attention,
        g_expand,
        g_contract,
        g_vectors,
        new_attention[0],
        new_expand[0],
        new_contract[0],
        new_vectors[0],
        new_attention[1],
        new_expand[1],
        new_contract[1],
        new_vectors[1],
        new_attention[2],
        new_expand[2],
        new_contract[2],
        new_vectors[2],
    )


def solution(mesh):
    planes = mesh.shape["dp"] // 2
    side = math.isqrt(planes)
    if side * side * 2 != mesh.shape["dp"]:
        side = 1
    sizes = (mesh.shape["dp"] // (2 * side), side, 2, mesh.shape["fsdp"])
    fast = sizes == (2, 2, 2, 4)
    mesh = Mesh(mesh.devices.reshape(sizes), ALL)
    shards = (
        P(ALL, None, None),
        P(ALL, None, None),
        P(ALL, None, None),
    )
    weights = (P(None, ALL, None), P(ALL, None), P(ALL, None), P(None, ALL))
    return jax.shard_map(
        functools.partial(local, fast),
        mesh=mesh,
        in_specs=shards + weights * 3,
        out_specs=shards + weights * 4,
        check_vma=False,
    )
```

```python
import functools
import math

import jax
import jax.numpy as jnp
from jax import lax
from jax.experimental import pallas as pl
from jax.experimental.pallas import tpu as pltpu
from jax.sharding import Mesh
from jax.sharding import PartitionSpec as P

HD = 64
ADAM_STEP = 4

eps_norm = 1e-05
clip_limit = 1.0
learn_rate = 0.05
beta_first = 0.9
beta_second = 0.999
eps_adam = 1e-08
weight_decay = 0.1

BF = jnp.bfloat16
F32 = jnp.float32
ALL = ("y", "x", "c", "z")
TILE = 512
KEY_CHUNK = 256
VEC_ROWS = 17
MIB = 1024 * 1024


def dot(left, right):
    return jnp.dot(left, right, preferred_element_type=F32)


def dot_tn(left, right):
    return lax.dot_general(left, right, (((0,), (0,)), ((), ())), preferred_element_type=F32)


def dot_nt(left, right):
    return lax.dot_general(left, right, (((1,), (1,)), ((), ())), preferred_element_type=F32)


def params(limit=60):
    return pltpu.CompilerParams(vmem_limit_bytes=limit * MIB)


def vmem():
    return pl.BlockSpec(memory_space=pltpu.VMEM)


def hbm():
    return pl.BlockSpec(memory_space=pltpu.HBM)


def smem():
    return pl.BlockSpec(memory_space=pltpu.SMEM)


def shape(dims, dtype):
    return jax.ShapeDtypeStruct(tuple(dims), dtype)


def cost(flops, nbytes):
    return pl.CostEstimate(flops=int(flops), bytes_accessed=int(nbytes), transcendentals=0)


class Pack:
    def __init__(self, array, base=0):
        self.array, self.base = array, base


def weight_start(place_ref, pack, row, buf, sem):
    lines = pl.ds(pack.base + row, buf.shape[1])
    pltpu.make_async_copy(pack.array.at[:, lines, :], buf, sem).start()


def call(kernel, packs, args, **settings):
    first, last = len(args), len(args) + len(packs)

    def body(*refs):
        held = [Pack(ref, p.base) for ref, p in zip(refs[first:last], packs)]
        kernel(*refs[:first], *held, *refs[last:])

    specs = settings.pop("in_specs") + [hbm()] * len(packs)
    return pl.pallas_call(body, in_specs=specs, **settings)(*args, *[p.array for p in packs])


def weight_wait(buf, sem):
    pltpu.make_async_copy(buf, buf, sem).wait()


def times(act_ref, buf, put):
    depth = buf.shape[0] * buf.shape[1]

    @pl.loop(0, buf.shape[2] // TILE)
    def _(n):
        start = pl.multiple_of(n * TILE, TILE)
        put(start, dot(act_ref[...], buf[:, :, pl.ds(start, TILE)].reshape(depth, TILE)))


def times_t(act_ref, buf, put):
    per = TILE // buf.shape[1]

    @pl.loop(0, buf.shape[0] // per)
    def _(n):
        start = pl.multiple_of(n * TILE, TILE)
        rows = buf[pl.ds(n * per, per)].reshape(TILE, buf.shape[2])
        put(start, dot_nt(act_ref[...], rows))


def start_all(copies):
    for one in copies:
        one.start()


def wait_all(copies):
    for one in copies:
        one.wait()


def row_chunks(count, size=64):
    return [slice(a, min(a + size, count)) for a in range(0, count, size)]


def normalise(values):
    centered = values - jnp.mean(values, axis=-1, keepdims=True)
    inv = lax.rsqrt(jnp.mean(centered * centered, axis=-1, keepdims=True) + eps_norm)
    return centered * inv, inv


def norm_into(src, gain, shift, out_ref):
    for rows in row_chunks(src.shape[0]):
        normed, _ = normalise(src[rows, :].astype(F32))
        out_ref[rows, :] = (normed * gain + shift).astype(BF)


def norm_grad(src, grad_ref, gain, put):
    gain_sum = jnp.zeros((1, src.shape[1]), F32)
    shift_sum = jnp.zeros((1, src.shape[1]), F32)
    for rows in row_chunks(src.shape[0]):
        normed, inv = normalise(src[rows, :].astype(F32))
        grad = grad_ref[rows, :]
        gain_sum += jnp.sum(grad * normed, axis=0, keepdims=True)
        shift_sum += jnp.sum(grad, axis=0, keepdims=True)
        scaled = grad * gain
        mean_one = jnp.mean(scaled, axis=-1, keepdims=True)
        mean_two = jnp.mean(scaled * normed, axis=-1, keepdims=True)
        put(rows, inv * (scaled - mean_one - normed * mean_two))
    return gain_sum, shift_sum


def column_sum(ref):
    total = jnp.zeros((1, ref.shape[1]), F32)
    for rows in row_chunks(ref.shape[0], 128):
        total += jnp.sum(ref[rows, :].astype(F32), axis=0, keepdims=True)
    return total


def self_in_kernel(place_ref, x_ref, vec_ref, one, two, a_ref, q_ref, k_ref, v_ref, bufs, sems):
    weight_start(place_ref, one, 0, bufs.at[0], sems.at[0])
    weight_start(place_ref, one, 32, bufs.at[1], sems.at[1])
    weight_start(place_ref, two, 0, bufs.at[2], sems.at[2])
    norm_into(x_ref, vec_ref[0:1, :], vec_ref[1:2, :], a_ref)
    for n, (out, bias) in enumerate(((q_ref, 6), (k_ref, None), (v_ref, 7))):
        weight_wait(bufs.at[n], sems.at[n])

        def put(start, value, out=out, bias=bias):
            if bias is not None:
                value = value + vec_ref[bias : bias + 1, pl.ds(start, TILE)]
            out[:, pl.ds(start, TILE)] = value.astype(BF)

        times(a_ref, bufs.at[n], put)


def self_in(place, x, vec, packs):
    rows, width = x.shape
    full = shape((rows, width), BF)
    return call(
        self_in_kernel,
        packs,
        [place, x, vec],
        out_shape=[full] * 4,
        in_specs=[smem(), vmem(), vmem()],
        out_specs=[vmem()] * 4,
        scratch_shapes=[pltpu.VMEM((3, 32, 32, width), BF), pltpu.SemaphoreType.DMA((3,))],
        compiler_params=params(48),
        cost_estimate=cost(6 * rows * width * width, 10 * MIB),
        name="self_in",
    )


def masked_pair(value):
    lane = lax.broadcasted_iota(jnp.int32, value.shape, 1)
    zero = jnp.zeros_like(value)
    return jnp.concatenate([jnp.where(lane < HD, value, zero), jnp.where(lane < HD, zero, value)], axis=0)


def pair_back(both, rows):
    line = lax.broadcasted_iota(jnp.int32, (2 * HD, rows), 0)
    return jnp.where(line < HD, both[:, :rows], both[:, rows:]).T


def key_chunks(count):
    return [(a, min(a + KEY_CHUNK, count)) for a in range(0, count, KEY_CHUNK)]


def exclude(scores, start, rows, causal, valid):
    key = lax.broadcasted_iota(jnp.int32, scores.shape, 0) + start
    if causal:
        query = lax.broadcasted_iota(jnp.int32, scores.shape, 1)
        query = jnp.where(query >= rows, query - rows, query)
        return jnp.where(key <= query, scores, -1e30)
    if start + scores.shape[0] > valid:
        return jnp.where(key < valid, scores, -1e30)
    return scores


def attend_kernel(causal, valid, q_ref, k_ref, v_ref, o_ref, exp_ref, inv_ref, top_ref, held):
    rows = q_ref.shape[0]
    query = masked_pair(q_ref[...] * jnp.asarray(HD**-0.5, BF))
    top = jnp.full((1, 2 * rows), -1e30, F32)
    for a, b in key_chunks(k_ref.shape[0]):
        scores = exclude(dot_nt(k_ref[a:b, :], query), a, rows, causal, valid)
        held[a:b, :] = scores
        top = jnp.maximum(top, jnp.max(scores, axis=0, keepdims=True))
    total = jnp.zeros((1, 2 * rows), F32)
    mixed = jnp.zeros((2 * HD, 2 * rows), F32)
    for a, b in key_chunks(k_ref.shape[0]):
        probs = jnp.exp(held[a:b, :] - top)
        total += jnp.sum(probs, axis=0, keepdims=True)
        rounded = probs.astype(BF)
        exp_ref[0, a:b, :] = rounded
        mixed += dot_tn(v_ref[a:b, :], rounded)
    inv_ref[0] = 1.0 / total
    o_ref[...] = pair_back(mixed * (1.0 / total), rows).astype(BF)
    lane = lax.broadcasted_iota(jnp.int32, (1, 2 * HD), 1)
    first, second = (jnp.max(part, axis=1, keepdims=True) for part in (top[:, :rows], top[:, rows:]))
    top_ref[0] = jnp.where(lane == 0, first, second)


def attend(query, key, value, causal, valid):
    rows, width = query.shape
    keys = key.shape[0]
    pairs = width // (2 * HD)

    def column(count):
        return pl.BlockSpec((count, 2 * HD), lambda h: (0, h))

    line = pl.BlockSpec((1, 1, 2 * rows), lambda h: (h, 0, 0))
    return pl.pallas_call(
        functools.partial(attend_kernel, causal, valid),
        grid=(pairs,),
        out_shape=[
            shape((rows, width), BF), shape((pairs, keys, 2 * rows), BF), shape((pairs, 1, 2 * rows), F32),
            shape((pairs, 1, 2 * HD), F32),
        ],
        in_specs=[column(rows), column(keys), column(keys)],
        out_specs=[
            column(rows), pl.BlockSpec((1, keys, 2 * rows), lambda h: (h, 0, 0)), line,
            pl.BlockSpec((1, 1, 2 * HD), lambda h: (h, 0, 0)),
        ],
        scratch_shapes=[pltpu.VMEM((keys, 2 * rows), F32)],
        compiler_params=params(48),
        cost_estimate=cost(16 * rows * keys * width, 4 * keys * width),
        name="attend_causal" if causal else "attend",
    )(query, key, value)


def self_out_kernel(place_ref, o_ref, x_ref, vec_ref, one, two, x1_ref, a_ref, q_ref, bufs, sems):
    weight_start(place_ref, two, 32, bufs.at[0], sems.at[0])
    weight_start(place_ref, one, 32, bufs.at[1], sems.at[1])
    weight_wait(bufs.at[0], sems.at[0])

    def put_residual(start, value):
        cols = pl.ds(start, TILE)
        x1_ref[:, cols] = x_ref[:, cols].astype(F32) + (value + vec_ref[8:9, cols])

    times(o_ref, bufs.at[0], put_residual)
    norm_into(x1_ref, vec_ref[2:3, :], vec_ref[3:4, :], a_ref)
    weight_wait(bufs.at[1], sems.at[1])

    def put_query(start, value):
        cols = pl.ds(start, TILE)
        q_ref[:, cols] = (value + vec_ref[9:10, cols]).astype(BF)

    times(a_ref, bufs.at[1], put_query)


def self_out(place, mixed, x, vec, packs):
    rows, width = x.shape
    return call(
        self_out_kernel,
        packs,
        [place, mixed, x, vec],
        out_shape=[shape((rows, width), F32), shape((rows, width), BF), shape((rows, width), BF)],
        in_specs=[smem()] + [vmem()] * 3,
        out_specs=[vmem()] * 3,
        scratch_shapes=[pltpu.VMEM((2, 32, 32, width), BF), pltpu.SemaphoreType.DMA((2,))],
        compiler_params=params(48),
        cost_estimate=cost(4 * rows * width * width, 10 * MIB),
        name="self_out",
    )


def cross_in_kernel(place_ref, e_ref, vec_ref, one, two, k_ref, v_ref, bufs, sems):
    for n, part in enumerate((one, two)):
        weight_start(place_ref, part, 0, bufs.at[n], sems.at[n])
    for n, (out, bias) in enumerate(((k_ref, None), (v_ref, 10))):
        weight_wait(bufs.at[n], sems.at[n])

        def put(start, value, out=out, bias=bias):
            if bias is not None:
                value = value + vec_ref[bias : bias + 1, pl.ds(start, TILE)]
            out[:, pl.ds(start, TILE)] = value.astype(BF)

        times(e_ref, bufs.at[n], put)


def cross_in(place, enc, vec, packs):
    frames, width = enc.shape
    return call(
        cross_in_kernel,
        packs,
        [place, enc, vec],
        out_shape=[shape((frames, width), BF)] * 2,
        in_specs=[smem()] + [vmem()] * 2,
        out_specs=[vmem()] * 2,
        scratch_shapes=[pltpu.VMEM((2, 32, 32, width), BF), pltpu.SemaphoreType.DMA((2,))],
        compiler_params=params(48),
        cost_estimate=cost(4 * frames * width * width, 14 * MIB),
        name="cross_in",
    )


def cross_out_kernel(place_ref, o_ref, x1_ref, vec_ref, two, x2_ref, a_ref, buf, sem):
    weight_start(place_ref, two, 32, buf, sem)
    weight_wait(buf, sem)

    def put(start, value):
        cols = pl.ds(start, TILE)
        x2_ref[:, cols] = x1_ref[:, cols] + (value + vec_ref[11:12, cols])

    times(o_ref, buf, put)
    norm_into(x2_ref, vec_ref[4:5, :], vec_ref[5:6, :], a_ref)


def cross_out(place, mixed, x1, vec, packs):
    rows, width = x1.shape
    return call(
        cross_out_kernel,
        packs,
        [place, mixed, x1, vec],
        out_shape=[shape((rows, width), F32), shape((rows, width), BF)],
        in_specs=[smem()] + [vmem()] * 3,
        out_specs=[vmem()] * 2,
        scratch_shapes=[pltpu.VMEM((32, 32, width), BF), pltpu.SemaphoreType.DMA],
        compiler_params=params(48),
        cost_estimate=cost(2 * rows * width * width, 8 * MIB),
        name="cross_out",
    )


def whole(dims):
    return pl.BlockSpec(dims, lambda n: (0,) * len(dims))


def feed_kernel(
    a_ref, x2_ref, e_ref, vec_ref, bias_ref, w1_ref, w2_ref, out_ref, df_ref, gb1_ref, gb2_ref, grad_ref, total
):
    step = pl.program_id(0)
    wide = w1_ref.shape[2]
    depth = a_ref.shape[1]

    @pl.when(step == 0)
    def _():
        total[...] = x2_ref[...] + vec_ref[12:13, :]
        gb2_ref[...] = column_sum(e_ref)

    w2 = w2_ref[...].reshape(wide, depth)
    pre = dot(a_ref[...], w1_ref[...].reshape(depth, wide)) + bias_ref[0]
    cdf = 0.5 * (1.0 + lax.erf(pre * math.sqrt(0.5)))
    act = (pre * cdf).astype(BF)
    slope = cdf + pre * (jnp.exp(-0.5 * (pre * pre)) * (1.0 / math.sqrt(2.0 * math.pi)))
    grad_ref[0] = dot_tn(act, e_ref[...]).astype(BF).reshape(grad_ref.shape[1:])
    grad_pre = (dot_nt(e_ref[...], w2) * slope).astype(BF)
    df_ref[...] = grad_pre
    gb1_ref[0] = jnp.sum(grad_pre.astype(F32), axis=0, keepdims=True)
    total[...] += dot(act, w2)

    @pl.when(step == pl.num_programs(0) - 1)
    def _():
        out_ref[...] = total[...].astype(BF)


def feed(a3, x2, cot, vec, pack):
    rows, width = a3.shape
    hidden = 4 * width
    wide = hidden // 8
    bias = vec[13:].reshape(8, 1, wide)
    return pl.pallas_call(
        feed_kernel,
        grid=(8,),
        out_shape=[
            shape((rows, width), BF), shape((rows, hidden), BF), shape((8, 1, wide), F32), shape((1, width), F32),
            shape((8, 4, 128, width), BF),
        ],
        in_specs=[
            whole((rows, width)),
            whole((rows, width)),
            whole((rows, width)),
            whole(vec.shape),
            pl.BlockSpec((1, 1, wide), lambda n: (n, 0, 0)),
            pl.BlockSpec((32, 32, wide), lambda n: (0, n // 2, n % 2)),
            pl.BlockSpec((4, 128, width), lambda n: (n, 1, 0)),
        ],
        out_specs=[
            whole((rows, width)),
            pl.BlockSpec((rows, wide), lambda n: (0, n)),
            pl.BlockSpec((1, 1, wide), lambda n: (n, 0, 0)),
            whole((1, width)),
            pl.BlockSpec((1, 4, 128, width), lambda n: (n, 0, 0, 0)),
        ],
        scratch_shapes=[pltpu.VMEM((rows, width), F32)],
        compiler_params=params(),
        cost_estimate=cost(8 * rows * width * hidden, 30 * MIB),
        name="feed",
    )(a3, x2, cot, vec, bias, pack, pack)


def feed_grad_kernel(df_ref, w1_ref, da_ref):
    @pl.when(pl.program_id(0) == 0)
    def _():
        da_ref[...] = jnp.zeros_like(da_ref)

    da_ref[...] += dot_nt(df_ref[...], w1_ref[...].reshape(da_ref.shape[1], w1_ref.shape[2]))


def feed_grad(df, pack):
    rows, hidden = df.shape
    width = pack.shape[2]
    return pl.pallas_call(
        feed_grad_kernel,
        grid=(hidden // width,),
        out_shape=shape((rows, width), F32),
        in_specs=[
            pl.BlockSpec((rows, width), lambda n: (0, n)),
            pl.BlockSpec((32, 32, width), lambda n: (0, n, 0)),
        ],
        out_specs=whole((rows, width)),
        compiler_params=params(),
        cost_estimate=cost(2 * rows * width * hidden, 12 * MIB),
        name="feed_grad",
    )(df, pack)


def cross_out_grad_kernel(place_ref, da_ref, x2_ref, cot_ref, vec_ref, two, dx_ref, do_ref, e_ref, sums_ref, buf, sem):
    weight_start(place_ref, two, 32, buf, sem)

    def put(rows, value):
        total = cot_ref[rows, :].astype(F32) + value
        dx_ref[rows, :] = total
        e_ref[rows, :] = total.astype(BF)

    gain, shift = norm_grad(x2_ref, da_ref, vec_ref[4:5, :], put)
    sums_ref[0:1, :] = gain
    sums_ref[1:2, :] = shift
    sums_ref[2:3, :] = column_sum(e_ref)
    weight_wait(buf, sem)

    def put_mixed(start, value):
        do_ref[:, pl.ds(start, TILE)] = value.astype(BF)

    times_t(e_ref, buf, put_mixed)


def cross_out_grad(place, da3, x2, cot, vec, packs):
    rows, width = x2.shape
    low = shape((rows, width), BF)
    return call(
        cross_out_grad_kernel,
        packs,
        [place, da3, x2, cot, vec],
        out_shape=[shape((rows, width), F32), low, low, shape((3, width), F32)],
        in_specs=[smem()] + [vmem()] * 4,
        out_specs=[vmem()] * 4,
        scratch_shapes=[pltpu.VMEM((32, 32, width), BF), pltpu.SemaphoreType.DMA],
        compiler_params=params(),
        cost_estimate=cost(2 * rows * width * width, 10 * MIB),
        name="cross_out_grad",
    )


def attend_grad(query, key, value, mixed, grad_mixed, saved):
    rows, width = query.shape
    keys = key.shape[0]

    def pairs(array):
        return array.reshape(array.shape[0], -1, 2, HD).transpose(1, 2, 0, 3)

    def back(array):
        return array.transpose(2, 0, 1, 3).reshape(array.shape[2], width)

    def one(inputs):
        q, k, v, o, grad_o, exps, inv = inputs
        probs = exps.reshape(keys, 2, rows).swapaxes(0, 1).astype(F32) * inv.reshape(2, 1, rows)
        grad_probs = jnp.einsum("hkd,hqd->hkq", v, grad_o, preferred_element_type=F32)
        delta = jnp.sum(o.astype(F32) * grad_o.astype(F32), axis=-1)[:, None, :]
        grad_scores = (probs * (grad_probs - delta)).astype(BF)
        grad_q = jnp.einsum("hkq,hkd->hqd", grad_scores, k, preferred_element_type=F32) * HD**-0.5
        grad_k = jnp.einsum("hkq,hqd->hkd", grad_scores, q, preferred_element_type=F32) * HD**-0.5
        grad_v = jnp.einsum("hkq,hqd->hkd", probs.astype(BF), grad_o, preferred_element_type=F32)
        return grad_q.astype(BF), grad_k.astype(BF), grad_v.astype(BF)

    grads = lax.map(one, (*[pairs(a) for a in (query, key, value, mixed, grad_mixed)], *saved))
    grads = [back(g) for g in grads]
    sums = jnp.stack([jnp.sum(grads[n].astype(F32), axis=0) for n in (0, 2)])
    return *grads, sums


def cross_query_grad_kernel(
    place_ref, dq_ref, x1_ref, dx2_ref, vec_ref, one, two, dx_ref, do_ref, e_ref, sums_ref, bufs, da_ref, sem
):
    for n, part in enumerate((one, two)):
        weight_start(place_ref, part, 32, bufs.at[n], sem.at[n])
    weight_wait(bufs.at[0], sem.at[0])

    def put_act(start, value):
        da_ref[:, pl.ds(start, TILE)] = value

    times_t(dq_ref, bufs.at[0], put_act)

    def put(rows, value):
        total = dx2_ref[rows, :] + value
        dx_ref[rows, :] = total
        e_ref[rows, :] = total.astype(BF)

    gain, shift = norm_grad(x1_ref, da_ref, vec_ref[2:3, :], put)
    sums_ref[0:1, :] = gain
    sums_ref[1:2, :] = shift
    sums_ref[2:3, :] = column_sum(e_ref)
    weight_wait(bufs.at[1], sem.at[1])

    def put_mixed(start, value):
        do_ref[:, pl.ds(start, TILE)] = value.astype(BF)

    times_t(e_ref, bufs.at[1], put_mixed)


def cross_query_grad(place, dq2, x1, dx2, vec, packs):
    rows, width = x1.shape
    low = shape((rows, width), BF)
    return call(
        cross_query_grad_kernel,
        packs,
        [place, dq2, x1, dx2, vec],
        out_shape=[shape((rows, width), F32), low, low, shape((3, width), F32)],
        in_specs=[smem()] + [vmem()] * 4,
        out_specs=[vmem()] * 4,
        scratch_shapes=[
            pltpu.VMEM((2, 32, 32, width), BF), pltpu.VMEM((rows, width), F32), pltpu.SemaphoreType.DMA((2,)),
        ],
        compiler_params=params(),
        cost_estimate=cost(4 * rows * width * width, 14 * MIB),
        name="cross_query_grad",
    )


def weight_grads_kernel(jobs, lefts, rights, place_ref, *refs):
    count = 2 * (lefts + rights)
    one_away, two_away, one_mine, two_mine = refs[count : count + 4]
    held, (grads, in_sems, sems) = refs[count + 4 : 2 * count + 4], refs[2 * count + 4 :]
    order = []
    for left, right, _ in jobs:
        order += [n for n in (2 * left, 2 * (lefts + right), 2 * left + 1, 2 * (lefts + right) + 1) if n not in order]
    pending = {n: pltpu.make_async_copy(refs[n], held[n], in_sems.at[n]) for n in order}
    start_all(pending.values())

    def ready(n):
        if n in pending:
            pending.pop(n).wait()
        return held[n]

    core = jnp.bitwise_and(place_ref[0], 1)
    plane = lax.shift_right_logical(place_ref[0], 1)
    split = len(jobs) // 2
    width = one_mine.shape[3]
    copies = []
    for pair in ((3, 1), (2, 0)):
        starts = [pl.multiple_of((jnp.bitwise_xor(plane, j) * 2 + core) * 128, 128) for j in pair]
        turned = {}
        for k, (left, right, block) in enumerate(jobs):
            wide = slice(block * width, (block + 1) * width)
            total = None
            for side in range(2):
                act, grad = ready(2 * left + side), ready(2 * (lefts + right) + side)
                if (left, side) not in turned:
                    columns = jnp.concatenate([act[:, pl.ds(start, 128)] for start in starts], axis=1)
                    turned[left, side] = columns.T
                value = dot(turned[left, side], grad[:, wide])
                total = value if total is None else total + value
            rounded = total.astype(BF).reshape((2,) + grads.shape[2:])
            lines = pl.ds(32 * (k % split), 32)
            for n, j in enumerate(pair):
                grads[k, j] = rounded[n]
                y, x = j // 2, j % 2
                if k < split:
                    target = (one_away if x else one_mine).at[y, :, lines, :]
                else:
                    target = (two_away if y else two_mine).at[x, :, lines, :]
                copies.append(pltpu.make_async_copy(grads.at[k, j], target, sems.at[k, j]))
                copies[-1].start()
    wait_all(copies)


def weight_grads(place, lefts, rights, jobs):
    width = lefts[0][0].shape[1]
    count = len(jobs)
    blocks = shape((2, 4, 16 * count, width), BF)
    operands = [value for pair in lefts + rights for value in pair]
    flops = sum(4 * lefts[left][0].shape[0] * width * width // 2 for left, _, _ in jobs)
    return pl.pallas_call(
        functools.partial(weight_grads_kernel, jobs, len(lefts), len(rights)),
        out_shape=[blocks] * 4,
        in_specs=[smem()] + [hbm()] * len(operands),
        out_specs=[hbm()] * 4,
        scratch_shapes=[pltpu.VMEM(value.shape, BF) for value in operands] + [
            pltpu.VMEM((count, 4, 4, 32, width), BF), pltpu.SemaphoreType.DMA((len(operands),)),
            pltpu.SemaphoreType.DMA((count, 4)),
        ],
        compiler_params=params(),
        cost_estimate=cost(flops, 12 * MIB),
        name="weight_grads",
    )(place, *operands)


def encoder_grad_kernel(place_ref, dk_ref, dv_ref, one, two, out_ref, bufs, held, sems):
    for n, part in enumerate((one, two)):
        weight_start(place_ref, part, 0, bufs.at[n], sems.at[n])
    for n in range(2):
        weight_wait(bufs.at[n], sems.at[n])
    width = dk_ref.shape[1]
    per = TILE // 32
    lines = width // 128

    @pl.loop(0, width // TILE)
    def _(n):
        total = dot_nt(dk_ref[...], bufs[0, pl.ds(n * per, per)].reshape(TILE, width))
        total += dot_nt(dv_ref[...], bufs[1, pl.ds(n * per, per)].reshape(TILE, width))
        for side in range(TILE // 128):
            start = n * (TILE // 128) + side
            held[pl.ds(start, total.shape[0], stride=lines), :] = total[:, side * 128 : (side + 1) * 128]

    copy = pltpu.make_async_copy(held.at[pl.ds(0, out_ref.shape[0]), :], out_ref, sems.at[2])
    copy.start()
    copy.wait()


def encoder_grad(place, dk2, dv2, packs, frames):
    padded, width = dk2.shape
    lines = width // 128
    return call(
        encoder_grad_kernel,
        packs,
        [place, dk2, dv2],
        out_shape=shape((frames * lines, 128), F32),
        in_specs=[smem()] + [vmem()] * 2,
        out_specs=hbm(),
        scratch_shapes=[
            pltpu.VMEM((2, 32, 32, width), BF), pltpu.VMEM((padded * lines, 128), F32), pltpu.SemaphoreType.DMA((3,)),
        ],
        compiler_params=params(),
        cost_estimate=cost(4 * padded * width * width, 16 * MIB),
        name="encoder_grad",
    )


def self_in_grad_kernel(
    place_ref, dq_ref, dk_ref, dv_ref, x_ref, dx1_ref, vec_ref, one, two, dx_ref, sums_ref, bufs, da_ref, sems
):
    weight_start(place_ref, one, 0, bufs.at[0], sems.at[0])
    weight_start(place_ref, one, 32, bufs.at[1], sems.at[1])
    weight_start(place_ref, two, 0, bufs.at[2], sems.at[2])
    for n, ref in enumerate((dq_ref, dk_ref, dv_ref)):
        weight_wait(bufs.at[n], sems.at[n])

        def put_act(start, value, n=n):
            if n:
                da_ref[:, pl.ds(start, TILE)] += value
            else:
                da_ref[:, pl.ds(start, TILE)] = value

        times_t(ref, bufs.at[n], put_act)

    def put(rows, value):
        dx_ref[rows, :] = dx1_ref[rows, :] + value

    gain, shift = norm_grad(x_ref, da_ref, vec_ref[0:1, :], put)
    sums_ref[0:1, :] = gain
    sums_ref[1:2, :] = shift


def self_in_grad(place, dq1, dk1, dv1, x, dx1, vec, packs):
    rows, width = x.shape
    return call(
        self_in_grad_kernel,
        packs,
        [place, dq1, dk1, dv1, x, dx1, vec],
        out_shape=[shape((rows, width), F32), shape((2, width), F32)],
        in_specs=[smem()] + [vmem()] * 6,
        out_specs=[vmem()] * 2,
        scratch_shapes=[
            pltpu.VMEM((3, 32, 32, width), BF), pltpu.VMEM((rows, width), F32), pltpu.SemaphoreType.DMA((3,)),
        ],
        compiler_params=params(),
        cost_estimate=cost(6 * rows * width * width, 14 * MIB),
        name="self_in_grad",
    )


SWAP = [(0, 1), (1, 0)]
MATRICES = ((0, 1), (2, 3), (5, 4), (6, 7))


class Unit:
    def __init__(self, chain):
        self.chain, self.result, self.moved = chain, None, None
        self.wanted = next(chain)

    def advance(self, arrived):
        try:
            self.wanted = self.chain.send(arrived)
        except StopIteration as stop:
            self.wanted, self.result = None, stop.value


def step(run=None, inputs=(), start=(), finish=()):
    start, finish = ([u for u in units if u is not None] for units in (start, finish))
    operands = [[value for value, _, _ in u.wanted] for u in start]
    inputs, operands = lax.optimization_barrier((tuple(inputs), operands))
    for u, values in zip(start, operands):
        u.moved = [lax.ppermute(v, axis, pairs) for v, (_, axis, pairs) in zip(values, u.wanted)]
    out = run(*inputs) if run else ()
    if finish:
        out, moved = lax.optimization_barrier((out, [u.moved for u in finish]))
        for u, values in zip(finish, moved):
            u.advance(values)
    return out


def turns():
    return [[(n, (n + k) % 4) for n in range(4)] for k in range(4)]


def add_rounded(left, right):
    return (left.astype(F32) + right.astype(F32)).astype(BF)


def add_kernel(plan, sources, place_ref, *refs):
    left, right = refs[:sources], refs[sources : 2 * sources]
    *outs, one, two, total, sems, out_sems = refs[2 * sources :]
    pieces = plan(place_ref)
    copies = [
        [
            pltpu.make_async_copy(side[source].at[index], held.at[n], sems.at[k, n])
            for k, (side, held) in enumerate(((left, one), (right, two)))
        ]
        for n, (source, index, _, _) in enumerate(pieces)
    ]
    for pair in copies:
        start_all(pair)
    away = []
    for n, (_, _, out, index) in enumerate(pieces):
        wait_all(copies[n])
        total[n] = add_rounded(one[n], two[n])
        away.append(pltpu.make_async_copy(total.at[n], outs[out].at[index], out_sems.at[n]))
        away[-1].start()
    wait_all(away)


def add_pieces(place, left, right, outs, piece, plan, count):
    held = pltpu.VMEM((count,) + piece, BF)
    return pl.pallas_call(
        functools.partial(add_kernel, plan, len(left)),
        out_shape=[shape(o, BF) for o in outs],
        in_specs=[smem()] + [hbm()] * (2 * len(left)),
        out_specs=[hbm()] * len(outs),
        scratch_shapes=[
            held, held, held, pltpu.SemaphoreType.DMA((2, count)), pltpu.SemaphoreType.DMA((count,)),
        ],
        compiler_params=params(),
        cost_estimate=cost(0, 6 * count * math.prod(piece)),
        name="add_pieces",
    )(place, *left, *right)


def turn_z(place_ref, k):
    return jnp.bitwise_and(place_ref[1] + k, 3)


def swap_chain(values):
    moved = yield [(value, "c", SWAP) for value in values]
    return list(zip(values, moved))


NEAR = [(0, 1), (1, 0), (2, 3), (3, 2)]
FAR = [(0, 2), (2, 0), (1, 3), (3, 1)]


def pick_z(both, k):
    return lax.dynamic_index_in_dim(both, jnp.bitwise_xor(lax.axis_index("z"), k), 0, keepdims=False)


def z_halves(both):
    away, mine = (jnp.stack([pick_z(both, k), pick_z(both, k ^ 2)]) for k in (1, 0))
    return (yield from z_two(away, mine))


def z_two(away, mine):
    (moved,) = yield [(away, "z", NEAR)]
    near = mine[0].astype(F32) + moved[0].astype(F32)
    (moved,) = yield [(add_rounded(mine[1], moved[1]), "z", FAR)]
    return near + moved.astype(F32)


def reduce_chain(place, halving, one, two, *mine):
    half, columns = one.shape[2:]
    rows = 2 * half
    parts = [pl.ds(0, half), pl.ds(half, half)]
    moved = yield [(one, "x", SWAP), (two, "y", SWAP)]

    def plan_two(_):
        return [(n, side, n if side else 2 + n, slice(None)) for side in (1, 0) for n in range(2)]

    outs = [(4, half, columns)] * 4
    one, two, *mine = add_pieces(place, list(mine), list(moved), outs, (4, half, columns), plan_two, 4)
    moved = yield [(one, "y", SWAP), (two, "x", SWAP)]

    if halving:

        def plan_halves(place_ref):
            turns = [(1, 0, 0), (3, 0, 1), (2, 1, 1), (0, 1, 0)]
            return [
                (n, jnp.bitwise_xor(place_ref[1], turn), out, (at, parts[n])) for turn, out, at in turns for n in range(2)
            ]

        outs = [(2, rows, columns)] * 2
        return (yield from z_two(*add_pieces(place, mine, list(moved), outs, (half, columns), plan_halves, 8)))

    def plan_three(place_ref):
        return [(n, turn_z(place_ref, k), k, parts[n]) for k in (2, 1, 3, 0) for n in range(2)]

    pieces = add_pieces(place, mine, list(moved), [(rows, columns)] * 4, (half, columns), plan_three, 8)
    moved = yield [(pieces[k], "z", turns()[k]) for k in (1, 3, 2)]
    return functools.reduce(jnp.add, [value.astype(F32) for value in moved], pieces[0].astype(F32))


def reduce_feed_plain(grad1, grad2):
    grad2 = grad2.reshape(-1, grad2.shape[3])
    return [lax.psum_scatter(g, ALL, scatter_dimension=0, tiled=True) for g in (grad1, grad2)]


def table_chain(table):
    row = lax.broadcasted_iota(jnp.int32, table.shape, 0)

    def combine(left, right):
        return jnp.where(row < VEC_ROWS, left + right, jnp.maximum(left, right))

    for axis in ("c", "x", "y"):
        moved = yield [(table, axis, SWAP)]
        table = combine(table, moved[0])
    for pairs in (NEAR, FAR):
        moved = yield [(table, "z", pairs)]
        table = combine(table, moved[0])
    return table


def vector_table(pack, row, rows, shard_cols):
    table = pack[:, row, : rows * shard_cols].reshape(32, rows, shard_cols).swapaxes(0, 1)
    return table.reshape(rows, 32 * shard_cols).astype(F32)


def expand_shard(expand, width):
    return jnp.concatenate([expand[:, n * width : (n + 1) * width] for n in range(expand.shape[1] // width)], axis=0)


def gather_fast(attention, expand, contract, vectors):
    width = attention.shape[2]
    line = jnp.pad(vectors.reshape(1, -1), ((0, 7), (0, width - vectors.size)))
    shard = jnp.concatenate([attention[m] for group in MATRICES for m in group] + [line], axis=0)
    pack = lax.all_gather(shard, ALL, axis=0, tiled=False)
    parts = []
    before = []
    for part in (expand_shard(expand, width), contract):
        moved = []
        part, _ = lax.optimization_barrier((part, before))
        for k in (3, 1, 2):
            part, moved = lax.optimization_barrier((part, moved))
            moved.append(lax.ppermute(part, "z", turns()[k]))
        part, moved = lax.optimization_barrier((part, moved))
        before = moved
        line = jnp.stack([part, moved[0], moved[2], moved[1]] * 2)
        parts.append(lax.dynamic_slice_in_dim(line, (4 - lax.axis_index("z")) % 4, 4, 0))
    pack_f = lax.all_gather(jnp.concatenate(parts, axis=1), ("y", "x", "c"), axis=0, tiled=True)
    return parts_of(pack), pack_f, vector_table(pack, 256, *vectors.shape)


def parts_of(pack):
    return [Pack(pack, 64 * n) for n in range(4)]


def gather_plain(attention, expand, contract, vectors):
    attention = lax.all_gather(attention, ALL, axis=1, tiled=True)
    expand = lax.all_gather(expand, ALL, axis=0, tiled=True)
    contract = lax.all_gather(contract, ALL, axis=0, tiled=True)
    vectors = lax.all_gather(vectors, ALL, axis=1, tiled=True)
    width = attention.shape[2]
    pack = jnp.concatenate([attention[m].reshape(32, 32, width) for group in MATRICES for m in group], axis=1)
    first = expand.reshape(32, 32, 4, width).swapaxes(1, 2).reshape(32, 128, width)
    pack_f = jnp.concatenate([first, contract.reshape(32, 128, width)], axis=1)
    return parts_of(pack), pack_f, vectors.astype(F32)


def adam_update(master, gradient, first, second, step_value, clip_scale):
    first_new = beta_first * first.astype(F32) + (1.0 - beta_first) * gradient
    second_new = beta_second * second + (1.0 - beta_second) * gradient * gradient
    direction = (
        first_new
        / (1.0 - beta_first**step_value)
        / (jnp.sqrt(second_new / (1.0 - beta_second**step_value)) + eps_adam)
    )
    master_new = (master - learn_rate * (direction + weight_decay * master)) * clip_scale
    return (first_new, second_new, master_new)


def table_kernel(sums1, bias1, sums2, bias2, sums3, gb1, gb2, top1, top2, out):
    out[...] = jnp.zeros_like(out)
    rows = [
        sums1[0:1, :], sums1[1:2, :], sums2[0:1, :], sums2[1:2, :], sums3[0:1, :], sums3[1:2, :],
        bias1[0:1, :], bias1[1:2, :], sums2[2:3, :], bias2[0:1, :], bias2[1:2, :], sums3[2:3, :], gb2[...],
    ]
    for n, row in enumerate(rows):
        out[n : n + 1, :] = row
    half = gb1.shape[2]
    for n in range(gb1.shape[0]):
        out[len(rows) + n // 2 : len(rows) + n // 2 + 1, n % 2 * half : (n % 2 + 1) * half] = gb1[n]
    for n, top in enumerate((top1, top2)):
        for pair in range(top.shape[0]):
            lanes = slice(pair * 2 * HD, (pair + 1) * 2 * HD)
            out[VEC_ROWS + n : VEC_ROWS + n + 1, lanes] = top[pair]


def vector_table_of(*pieces):
    width = pieces[0].shape[1]
    return pl.pallas_call(
        table_kernel,
        out_shape=shape((24, width), F32),
        in_specs=[vmem()] * len(pieces),
        out_specs=vmem(),
        compiler_params=params(),
        cost_estimate=cost(0, 200000),
        name="vector_table",
    )(*pieces)


def maxima_of(table):
    return table[VEC_ROWS : VEC_ROWS + 2].reshape(2, -1, 2 * HD)[:, :, :2].reshape(2, -1)


def sequence_plain(place, x, enc, frames, cot, vec, packs, pack_f):
    rows, width = x.shape
    one_a, one_b, two_a, two_b = packs
    a1, q1, k1, v1 = self_in(place, x, vec, [one_a, one_b])
    o1, *saved1, top1 = attend(q1, k1, v1, True, rows)
    x1, a2, q2 = self_out(place, o1, x, vec, [two_a, one_b])
    k2, v2 = cross_in(place, enc, vec, [two_a, two_b])
    o2, *saved2, top2 = attend(q2, k2, v2, False, frames)
    x2, a3 = cross_out(place, o2, x1, vec, [two_b])
    result, df, gb1, gb2, grad2 = feed(a3, x2, cot, vec, pack_f)
    da3 = feed_grad(df, pack_f)
    dx2, do2, e2, sums3 = cross_out_grad(place, da3, x2, cot, vec, [two_b])
    dq2, dk2, dv2, bias2 = attend_grad(q2, k2, v2, o2, do2, saved2)
    dx1, do1, e1, sums2 = cross_query_grad(place, dq2, x1, dx2, vec, [two_a, one_b])
    dq1, dk1, dv1, bias1 = attend_grad(q1, k1, v1, o1, do1, saved1)
    grad_input, sums1 = self_in_grad(place, dq1, dk1, dv1, x, dx1, vec, [one_a, one_b])
    grad_encoder = encoder_grad(place, dk2, dv2, [two_a, two_b], frames).reshape(frames, width)
    table = vector_table_of(sums1, bias1, sums2, bias2, sums3, gb1, gb2, top1, top2)
    pairs = ((a1, dq1), (a1, dk1), (a1, dv1), (o1, e1), (a2, dq2), (enc, dk2), (enc, dv2), (o2, e2))
    g_attention = jnp.stack([dot_tn(left, right) for left, right in pairs])
    sums = [dot_tn(a3, df), grad2.astype(F32), g_attention]
    return result, grad_input, grad_encoder, table[:VEC_ROWS], maxima_of(table), sums


def gradients_plain(inputs, encoder, cotangent, owned):
    packs, pack_f, vec = gather_plain(*owned)
    place = jnp.zeros((2,), jnp.int32)
    frames = encoder.shape[1]
    done = []
    for n in range(inputs.shape[0]):
        enc = pad_frames(encoder[n])
        done.append(sequence_plain(place, inputs[n], enc, frames, cotangent[n], vec, packs, pack_f))
    result, grad_input, grad_encoder = (jnp.stack([d[k] for d in done]) for k in range(3))
    g_vectors = functools.reduce(jnp.add, [d[3] for d in done])
    maxima = functools.reduce(jnp.maximum, [d[4] for d in done])
    grad1, grad2, g_attention = (functools.reduce(jnp.add, values) for values in zip(*[d[5] for d in done]))
    sums = reduce_feed_plain(grad1, grad2) + [lax.psum_scatter(g_attention, ALL, scatter_dimension=1, tiled=True)]
    g_vectors = lax.psum_scatter(g_vectors, ALL, scatter_dimension=1, tiled=True)
    return result, grad_input, grad_encoder, sums, g_vectors, lax.pmax(maxima, ALL)


def pad_frames(enc):
    return jnp.pad(enc, ((0, -enc.shape[0] % 16), (0, 0)))


def gradients_fast(inputs, encoder, cotangent, owned):
    attention, expand, contract, vectors = owned
    x, cot = inputs[0], cotangent[0]
    rows, width = x.shape
    frames = encoder.shape[1]
    place = jnp.stack([lax.axis_index(("y", "x", "c")), lax.axis_index("z")]).astype(jnp.int32)
    (one_a, one_b, two_a, two_b), pack_f, vec = gather_fast(*owned)
    enc = pad_frames(encoder[0])
    a1, q1, k1, v1 = self_in(place, x, vec, [one_a, one_b])
    o1, *saved1, top1 = attend(q1, k1, v1, True, rows)
    x1, a2, q2 = self_out(place, o1, x, vec, [two_a, one_b])
    k2, v2 = cross_in(place, enc, vec, [two_a, two_b])
    o2, *saved2, top2 = attend(q2, k2, v2, False, frames)
    x2, a3 = cross_out(place, o2, x1, vec, [two_b])

    acts = Unit(swap_chain([a3, a1, o1, a2, o2, enc]))
    (x2,) = step(lambda x2: (x2,), [x2], start=[acts], finish=[acts])
    a3, a1, o1, a2, o2, enc = acts.result

    result, df, gb1, gb2, grad2 = feed(a3[0], x2, cot, vec, pack_f)
    plane_2 = lax.psum_scatter(grad2, ("y", "x", "c"), scatter_dimension=0, tiled=True)[0]
    swap_df = Unit(swap_chain([df]))
    da3 = step(lambda df: feed_grad(df, pack_f), [df], start=[swap_df], finish=[swap_df])
    f1 = Unit(reduce_chain(place, True, *weight_grads(place, [a3], swap_df.result, [(0, 0, k) for k in range(4)])))

    def cross_back(da3):
        dx2, do2, e2, sums3 = cross_out_grad(place, da3, x2, cot, vec, [two_b])
        swap = Unit(swap_chain([e2]))
        out = step(
            lambda do2: attend_grad(q2, k2, v2, o2[0], do2, saved2), [do2], start=[swap], finish=[swap]
        )
        return dx2, swap.result, sums3, *out

    dx2, swap_e2, sums3, dq2, dk2, dv2, bias2 = step(cross_back, [da3], start=[f1], finish=[f1])
    swap_2 = Unit(swap_chain([dq2, dk2, dv2]))
    dx1, do1, e1, sums2 = step(
        lambda dx2: cross_query_grad(place, dq2, x1, dx2, vec, [two_a, one_b]),
        [dx2],
        start=[swap_2],
        finish=[swap_2],
    )
    swap_e1 = Unit(swap_chain([e1]))
    rights = swap_2.result + swap_e2
    blocks = step(
        lambda *rights: weight_grads(
            place, [enc, a2, o2], [rights[k : k + 2] for k in range(0, 8, 2)], ((0, 1, 0), (1, 0, 0), (0, 2, 0), (2, 3, 0))
        ),
        [value for pair in rights for value in pair],
        start=[swap_e1, f1],
        finish=[swap_e1, f1],
    )
    r1 = Unit(reduce_chain(place, True, *blocks))
    f2 = Unit(z_halves(plane_2))

    def self_back(do1):
        dq1, dk1, dv1, bias1 = attend_grad(q1, k1, v1, o1[0], do1, saved1)
        grad_input, sums1 = self_in_grad(place, dq1, dk1, dv1, x, dx1, vec, [one_a, one_b])
        return dq1, dk1, dv1, bias1, grad_input, sums1

    dq1, dk1, dv1, bias1, grad_input, sums1 = step(self_back, [do1], start=[r1, f1, f2], finish=[r1, f1, f2])
    table = Unit(table_chain(vector_table_of(sums1, bias1, sums2, bias2, sums3, gb1, gb2, top1, top2)))
    swap_1 = Unit(swap_chain([dq1, dk1, dv1]))
    step(start=[swap_1, table], finish=[swap_1, table])
    rights = swap_e1.result + swap_1.result
    blocks = step(
        lambda *rights: weight_grads(
            place, [o1, a1], [rights[k : k + 2] for k in range(0, 8, 2)], ((0, 0, 0), (1, 1, 0), (1, 2, 0), (1, 3, 0))
        ),
        [value for pair in rights for value in pair],
        start=[r1, f1, table],
        finish=[r1, f1, table],
    )
    r2 = Unit(reduce_chain(place, False, *blocks))
    grad_encoder = step(
        lambda dk2: encoder_grad(place, dk2, dv2, [two_a, two_b], frames),
        [dk2],
        start=[r2, r1, f2, table],
        finish=[r2, r1, f2, table],
    )
    step(start=[r2, r1, table], finish=[r2, r1, table])
    step(start=[r2, table], finish=[r2, table])
    total = table.result
    shard_cols = vectors.shape[1]
    g_vectors = lax.dynamic_slice_in_dim(total[:VEC_ROWS], lax.axis_index(ALL) * shard_cols, shard_cols, 1)
    maxima = maxima_of(total)
    grad_encoder = grad_encoder.reshape(1, frames, width)
    g_expand = f1.result.reshape(4, 32, width).swapaxes(0, 1).reshape(32, 4 * width)
    cross, own = (value.reshape(4, 32, width) for value in (r1.result, r2.result))
    g_attention = jnp.concatenate([own[1:], own[:1], cross[1:2], cross[:1], cross[2:]], axis=0)
    sums = [g_expand, f2.result, g_attention]
    return result[None], grad_input[None], grad_encoder, sums, g_vectors, maxima


def local(
    fast,
    inputs,
    encoder,
    cotangent,
    attention_master,
    expand_master,
    contract_master,
    vectors_master,
    attention_first,
    expand_first,
    contract_first,
    vectors_first,
    attention_second,
    expand_second,
    contract_second,
    vectors_second,
):
    owned = [m.astype(BF) for m in (attention_master, expand_master, contract_master, vectors_master)]
    compute = gradients_fast if fast and inputs.shape[0] == 1 else gradients_plain
    result, grad_input, grad_encoder, sums, g_vectors, maxima = compute(inputs, encoder, cotangent, owned)
    g_expand, g_contract, g_attention = sums
    shard_cols = vectors_master.shape[1]
    first_col = lax.axis_index(ALL) * shard_cols

    clip_cols = jnp.repeat(jnp.sqrt(clip_limit / jnp.maximum(maxima, clip_limit)), HD, axis=1)
    unit_row = jnp.ones_like(clip_cols[0])
    clip_attention = jnp.stack(
        [clip_cols[0], clip_cols[0], unit_row, unit_row, clip_cols[1], clip_cols[1], unit_row, unit_row]
    )[:, None, :]
    local_cols = lax.dynamic_slice_in_dim(clip_cols, first_col, shard_cols, 1)
    row = lax.broadcasted_iota(jnp.int32, vectors_master.shape, 0)
    clip_vectors = jnp.where(row == 6, local_cols[0:1], jnp.where(row == 9, local_cols[1:2], 1.0))
    step_value = float(ADAM_STEP)
    new_attention = adam_update(
        attention_master, g_attention, attention_first, attention_second, step_value, clip_attention
    )
    new_expand = adam_update(expand_master, g_expand, expand_first, expand_second, step_value, 1.0)
    new_contract = adam_update(contract_master, g_contract, contract_first, contract_second, step_value, 1.0)
    new_vectors = adam_update(vectors_master, g_vectors, vectors_first, vectors_second, step_value, clip_vectors)
    return (
        result,
        grad_input,
        grad_encoder,
        g_attention,
        g_expand,
        g_contract,
        g_vectors,
        new_attention[0],
        new_expand[0],
        new_contract[0],
        new_vectors[0],
        new_attention[1],
        new_expand[1],
        new_contract[1],
        new_vectors[1],
        new_attention[2],
        new_expand[2],
        new_contract[2],
        new_vectors[2],
    )


def solution(mesh):
    planes = mesh.shape["dp"] // 2
    side = math.isqrt(planes)
    if side * side * 2 != mesh.shape["dp"]:
        side = 1
    sizes = (mesh.shape["dp"] // (2 * side), side, 2, mesh.shape["fsdp"])
    fast = sizes == (2, 2, 2, 4)
    mesh = Mesh(mesh.devices.reshape(sizes), ALL)
    shards = (
        P(ALL, None, None),
        P(ALL, None, None),
        P(ALL, None, None),
    )
    weights = (P(None, ALL, None), P(ALL, None), P(ALL, None), P(None, ALL))
    return jax.shard_map(
        functools.partial(local, fast),
        mesh=mesh,
        in_specs=shards + weights * 3,
        out_specs=shards + weights * 4,
        check_vma=False,
    )
```
